32 devices in a mesh: dp: 16 (over z, y, core), tensor: 2 (over x).
Axes of the slice: x: 2, y: 2, z: 4, core: 2. Of those that a mesh axis runs over, the one named last changes fastest.
Arguments:
- latent: bfloat16 [64, 1024, 1152], P('dp', 'tensor'), may hold values from -6 to 6
- condition: bfloat16 [64, 1152], P('dp'), may hold values from -6 to 6
- cotangent: bfloat16 [64, 1024, 1152], P('dp', 'tensor'), may hold values from -6 to 6
- mod_weight: bfloat16 [1152, 6, 1152], P('dp', None, 'tensor'), may hold values from -0.1875 to 0.1875
- mod_bias: bfloat16 [6, 1152], P(None, 'tensor'), may hold values from -3 to 3
- head_weight: bfloat16 [1152, 3, 1152], P('dp', None, 'tensor'), may hold values from -0.1875 to 0.1875
- head_bias: bfloat16 [2, 1152], P(None, 'tensor'), may hold values from -3 to 3
- mix_weight: bfloat16 [1152, 1152], P('tensor', 'dp'), may hold values from -1 to 1
- branch_bias: bfloat16 [2, 1152], P(None, 'tensor'), may hold values from -3 to 3
- up_weight: bfloat16 [1152, 4608], P('dp', 'tensor'), may hold values from -0.1875 to 0.1875
- up_bias: bfloat16 [4608], P('tensor'), may hold values from -3 to 3
- down_weight: bfloat16 [4608, 1152], P('tensor', 'dp'), may hold values from -0.09375 to 0.09375
Outputs:
- block_out: bfloat16 [64, 1024, 1152], P('dp', 'tensor')
- latent_grad: bfloat16 [64, 1024, 1152], P('dp', 'tensor')
- condition_grad: float32 [64, 1152], P('dp')
- mod_weight_grad: float32 [1152, 6, 1152], P('dp', None, 'tensor')
- mod_bias_grad: float32 [6, 1152], P(None, 'tensor')
- head_weight_grad: float32 [1152, 3, 1152], P('dp', None, 'tensor')
- head_bias_grad: float32 [2, 1152], P(None, 'tensor')
- mix_weight_grad: float32 [1152, 1152], P('tensor', 'dp')
- branch_bias_grad: float32 [2, 1152], P(None, 'tensor')
- up_weight_grad: float32 [1152, 4608], P('dp', 'tensor')
- up_bias_grad: float32 [4608], P('tensor')
- down_weight_grad: float32 [4608, 1152], P('tensor', 'dp')
The draws below stay inside these ranges and needn't reach their ends.
All inputs are finite; a program needn't handle non-finite values.
Results may differ from the reference program's by a relative error of at most 0.022.
The reference program's roundings to bfloat16 on the way count: a program that leaves them out, or rounds other values in their place, can miss the bound.
Values may be sent and summed in bfloat16 or wider, within the bound.
A program may use at most 448 MiB of HBM per device.

```python
from functools import partial
import jax
import jax.numpy as jnp
from jax import lax

D = 1152
HEADS = 16
FF = 4608
SEQ = 1024
HEAD_DIM = 72
LATENTS = 64


def strengthened(array, key, source, target, blocks, factor):
    owner, partner = [(jnp.arange(array.shape[axis_at]) // (array.shape[axis_at] // blocks)).reshape([-1 if axis == axis_at else 1 for axis in range(array.ndim)]) for axis_at in (source, target)]
    chosen = jax.random.permutation(key, blocks)[partner]
    strong = (owner == chosen) | (owner == (partner + blocks // 2) % blocks)
    return jnp.where(strong, factor * array, array)


def levels(own_key, shape, cuts, smallest, high):
    loudness = 1.0
    for axis_at, shards_of in cuts:
        heights = jax.random.uniform(jax.random.fold_in(jax.random.fold_in(own_key, 6), axis_at), (shards_of,), jnp.float32, smallest / len(cuts), high / len(cuts))
        loudness = loudness * jnp.repeat(jnp.exp(heights), shape[axis_at] // shards_of).reshape((-1,) + (1,) * (len(shape) - 1 - axis_at))
    return loudness


def bell_draw(own_key, extent, scale, limit, pieces=(), held_as=jnp.bfloat16):
    array = scale * jax.random.normal(own_key, extent, jnp.float32)
    if pieces:
        array = array * levels(own_key, extent, pieces, -0.22, 0.18)
    return jnp.clip(array, -limit, limit).astype(held_as)


def bell_draw_with(own_key, shape, scale, limit, split, heavy, kind=jnp.bfloat16):
    values = scale * jax.random.normal(own_key, shape, jnp.float32)
    if split:
        values = values * levels(own_key, shape, split, -0.22, 0.18)
    return jnp.clip(strengthened(values, jax.random.fold_in(own_key, 3), *heavy), -limit, limit).astype(kind)


def setup_inputs(seed: int = 0) -> dict:
    streams_of = jax.random.split(jax.random.key(seed), 13)
    latent = bell_draw(streams_of[0], (LATENTS, SEQ, D), 1.0, 6.0, ((0, 16), (1, 2)))
    condition = bell_draw(streams_of[1], (LATENTS, D), 1.0, 6.0, ((0, 16),))
    cotangent = bell_draw_with(streams_of[2], (LATENTS, SEQ, D), 1.0, 6.0, ((0, 16), (1, 2)), (0, 2, 16, 2.0))
    mod_weight = bell_draw(streams_of[3], (D, 6, D), D ** -0.5, 0.1875, ((0, 16), (2, 2)))
    mod_bias = bell_draw(streams_of[4], (6, D), 0.5, 3.0, ((1, 2),))
    head_weight = bell_draw(streams_of[5], (D, 3, D), D ** -0.5, 0.1875, ((0, 16), (2, 2)))
    head_bias = bell_draw(streams_of[6], (2, D), 0.5, 3.0, ((1, 2),))
    mix_weight = bell_draw(streams_of[7], (D, D), (D // 32) ** -0.5, 1.0, ((0, 2), (1, 16)))
    branch_bias = bell_draw(streams_of[8], (2, D), 0.5, 3.0, ((1, 2),))
    up_weight = bell_draw(streams_of[9], (D, FF), D ** -0.5, 0.1875, ((0, 16), (1, 2)))
    up_bias = bell_draw(streams_of[10], (FF,), 0.5, 3.0, ((0, 2),))
    down_weight = bell_draw(streams_of[11], (FF, D), FF ** -0.5, 0.09375, ((0, 2), (1, 16)))
    return {"latent": latent, "condition": condition, "cotangent": cotangent, "mod_weight": mod_weight, "mod_bias": mod_bias, "head_weight": head_weight, "head_bias": head_bias, "mix_weight": mix_weight, "branch_bias": branch_bias, "up_weight": up_weight, "up_bias": up_bias, "down_weight": down_weight}


HIGHEST = lax.Precision.HIGHEST
EPSILON = 1e-06

@jax.custom_vjp
def low(v):
    return lax.optimization_barrier(v.astype(jnp.bfloat16)).astype(jnp.float32)

@jax.custom_vjp
def low_back(v):
    return v

def low_keep(v):
    return (low(v), None)

def low_pass(kept, grad):
    return (grad,)

def back_keep(v):
    return (v, None)

def back_low(kept, grad):
    return (low(grad),)
low.defvjp(low_keep, low_pass)
low_back.defvjp(back_keep, back_low)

def layer_norm(values):
    centred = values - lax.optimization_barrier(jnp.mean(values, axis=-1, keepdims=True))
    variance = lax.optimization_barrier(jnp.mean(centred * centred, axis=-1, keepdims=True))
    return centred * lax.rsqrt(variance + EPSILON)

def softmax_rows(scores):
    raised = jnp.exp(scores - lax.optimization_barrier(jnp.max(scores, axis=-1, keepdims=True)))
    return raised / lax.optimization_barrier(jnp.sum(raised, axis=-1, keepdims=True))

def one_latent(params, latent_rows, cond_row):
    mod_weight, mod_bias, head_weight, head_bias, mix_weight, branch_bias, up_weight, up_bias, down_weight = params
    cond_low = low(jax.nn.silu(cond_row))
    modulation = low_back(jnp.einsum('d,dkc->kc', cond_low, mod_weight, precision=HIGHEST) + mod_bias)
    attn_in = low(layer_norm(latent_rows) * (1.0 + modulation[1]) + modulation[0])
    projected = jnp.einsum('sd,dkc->skc', attn_in, head_weight, precision=HIGHEST)
    queries = low_back(low(projected[:, 0] + head_bias[0]))
    keys = low_back(low(projected[:, 1]))
    values = low_back(low(projected[:, 2] + head_bias[1]))
    seq_len = latent_rows.shape[0]
    query_heads = queries.reshape(seq_len, HEADS, HEAD_DIM)
    key_heads = keys.reshape(seq_len, HEADS, HEAD_DIM)
    value_heads = values.reshape(seq_len, HEADS, HEAD_DIM)
    scores = low_back(jnp.einsum('qhd,khd->hqk', query_heads, key_heads, precision=HIGHEST) * HEAD_DIM ** (-0.5))
    probs = low(softmax_rows(scores))
    mixed_heads = jnp.einsum('hqk,khd->qhd', probs, value_heads, precision=HIGHEST)
    mixed = low_back(low(mixed_heads.reshape(seq_len, D)))
    attn_branch = low_back(jnp.dot(mixed, mix_weight, precision=HIGHEST))
    first = latent_rows + modulation[2] * (attn_branch + branch_bias[0])
    mlp_in = low(layer_norm(first) * (1.0 + modulation[4]) + modulation[3])
    pre_act = low_back(jnp.dot(mlp_in, up_weight, precision=HIGHEST) + up_bias)
    act = low(jax.nn.gelu(pre_act, approximate=True))
    mlp_branch = low_back(jnp.dot(act, down_weight, precision=HIGHEST))
    return first + modulation[5] * (mlp_branch + branch_bias[1])

def forward(latent, condition, *params):
    step_latent = jax.checkpoint(partial(one_latent, params))

    def run_latent(paired):
        return step_latent(paired[0], paired[1])
    return lax.map(run_latent, (latent, condition))

def reference(latent, condition, cotangent, mod_weight, mod_bias, head_weight, head_bias, mix_weight, branch_bias, up_weight, up_bias, down_weight):
    inputs = [latent, condition, mod_weight, mod_bias, head_weight, head_bias, mix_weight, branch_bias, up_weight, up_bias, down_weight]
    floats = [item.astype(jnp.float32) for item in inputs]
    block_out, pullback = jax.vjp(forward, *floats)
    grads = pullback(cotangent.astype(jnp.float32))
    return (block_out.astype(jnp.bfloat16), grads[0].astype(jnp.bfloat16), grads[1], grads[2], grads[3], grads[4], grads[5], grads[6], grads[7], grads[8], grads[9], grads[10])
```

```python
from functools import partial

import jax
import jax.numpy as jnp
from jax import lax
from jax.experimental import pallas as pl
from jax.experimental.pallas import tpu as pltpu
from jax.sharding import PartitionSpec as P

SEQ = 1024
HEAD_DIM = 72
MICRO = 4
LOG2E = 1.4426950408889634
WINDOW = 256
f32 = jnp.float32
bf16 = jnp.bfloat16
NT = (((1,), (1,)), ((), ()))


EPSILON = 1e-06


def layer_norm(values):
    centred = values - jnp.mean(values, axis=-1, keepdims=True)
    variance = jnp.mean(centred * centred, axis=-1, keepdims=True)
    return centred * lax.rsqrt(variance + EPSILON)


def modulate(values, shift, scale):
    return layer_norm(values) * (1.0 + scale[:, None, :]) + shift[:, None, :]


def gelu_tanh(values):
    return jax.nn.gelu(values, approximate=True)


def fetch_weights(mod_weight, head_weight, mix_weight, up_weight, down_weight):
    return (
        lax.all_gather(mod_weight, "dp", axis=0, tiled=True),
        lax.all_gather(head_weight, "dp", axis=0, tiled=True),
        lax.all_gather(mix_weight, "dp", axis=1, tiled=True),
        lax.all_gather(up_weight, "dp", axis=0, tiled=True),
        lax.all_gather(down_weight, "dp", axis=1, tiled=True),
    )


def reduce_weights(grads):
    return (
        lax.psum_scatter(
            grads[0].astype(jnp.bfloat16), "dp", scatter_dimension=0, tiled=True
        ).astype(jnp.float32),
        lax.psum_scatter(
            grads[1].astype(jnp.bfloat16), "dp", scatter_dimension=0, tiled=True
        ).astype(jnp.float32),
        lax.psum_scatter(
            grads[2].astype(jnp.bfloat16), "dp", scatter_dimension=1, tiled=True
        ).astype(jnp.float32),
        lax.psum_scatter(
            grads[3].astype(jnp.bfloat16), "dp", scatter_dimension=0, tiled=True
        ).astype(jnp.float32),
        lax.psum_scatter(
            grads[4].astype(jnp.bfloat16), "dp", scatter_dimension=1, tiled=True
        ).astype(jnp.float32),
    )


def attend_forward(queries, keys, values, block_rows, scale_factor):
    seq_len = queries.shape[0]
    blocked = queries.reshape(seq_len // block_rows, block_rows, queries.shape[1], queries.shape[2])

    def one_block(query_block):
        scores = (
            jnp.einsum("qhd,khd->hqk", query_block, keys, preferred_element_type=jnp.float32)
            * scale_factor
        )
        peak = jnp.max(scores, axis=-1, keepdims=True)
        raised = jnp.exp(scores - peak)
        total = jnp.sum(raised, axis=-1, keepdims=True)
        weights = (raised / total).astype(jnp.bfloat16)
        mixed = jnp.einsum("hqk,khd->qhd", weights, values, preferred_element_type=jnp.float32)
        return (mixed, (peak + jnp.log(total))[..., 0])

    mixed, logsum = lax.map(one_block, blocked)
    return (mixed.reshape(queries.shape), logsum)


def attend_backward(queries, keys, values, grad_mixed, logsum, block_rows, scale_factor):
    seq_len = queries.shape[0]
    block_shape = (seq_len // block_rows, block_rows, queries.shape[1], queries.shape[2])

    def one_block(carried, pieces):
        key_sum, value_sum = carried
        query_block, grad_block, logsum_block = pieces
        scores = (
            jnp.einsum("qhd,khd->hqk", query_block, keys, preferred_element_type=jnp.float32)
            * scale_factor
        )
        probs = jnp.exp(scores - logsum_block[..., None])
        prob_grad = jnp.einsum(
            "qhd,khd->hqk", grad_block, values, preferred_element_type=jnp.float32
        )
        inner = jnp.sum(probs * prob_grad, axis=-1, keepdims=True)
        score_grad = (probs * (prob_grad - inner)).astype(jnp.bfloat16)
        query_grad = (
            jnp.einsum("hqk,khd->qhd", score_grad, keys, preferred_element_type=jnp.float32)
            * scale_factor
        )
        key_sum = (
            key_sum
            + jnp.einsum(
                "hqk,qhd->khd", score_grad, query_block, preferred_element_type=jnp.float32
            )
            * scale_factor
        )
        value_sum = value_sum + jnp.einsum(
            "hqk,qhd->khd",
            probs.astype(jnp.bfloat16),
            grad_block,
            preferred_element_type=jnp.float32,
        )
        return ((key_sum, value_sum), query_grad)

    empty = jnp.zeros(keys.shape, jnp.float32)
    (key_grad, value_grad), query_grads = lax.scan(
        one_block,
        (empty, empty),
        (queries.reshape(block_shape), grad_mixed.reshape(block_shape), logsum),
    )
    return (query_grads.reshape(queries.shape), key_grad, value_grad)


def body_by_heads(
    latent,
    condition,
    cotangent,
    mod_weight,
    mod_bias,
    head_weight,
    head_bias,
    mix_weight,
    branch_bias,
    up_weight,
    up_bias,
    down_weight,
):
    per_group = latent.shape[0] // MICRO
    seq_len = SEQ
    head_cols = head_weight.shape[2]
    local_heads = head_cols // HEAD_DIM
    block_rows = min(512, seq_len)
    scale_factor = HEAD_DIM ** (-0.5)
    attend_fwd = jax.vmap(partial(attend_forward, block_rows=block_rows, scale_factor=scale_factor))
    attend_bwd = jax.vmap(
        partial(attend_backward, block_rows=block_rows, scale_factor=scale_factor)
    )
    head_bias_f = head_bias.astype(jnp.float32)
    up_bias_f = up_bias.astype(jnp.float32)
    mod_bias_f = mod_bias.astype(jnp.float32)
    branch_bias_f = branch_bias.astype(jnp.float32)
    bias_totals = (
        jnp.zeros(mod_bias.shape, jnp.float32),
        jnp.zeros(head_bias.shape, jnp.float32),
        jnp.zeros(up_bias.shape, jnp.float32),
        jnp.zeros(branch_bias.shape, jnp.float32),
    )
    grad_sums = None
    block_outs = []
    latent_grads = []
    condition_grads = []
    for micro_step in range(MICRO):
        row_start = micro_step * per_group
        row_stop = row_start + per_group
        mod_full, head_full, mix_full, up_full, down_full = fetch_weights(
            mod_weight, head_weight, mix_weight, up_weight, down_weight
        )
        lat_part = latent[row_start:row_stop].astype(jnp.float32)
        cond_part = condition[row_start:row_stop].astype(jnp.float32)
        cond_act, silu_back = jax.vjp(jax.nn.silu, cond_part)
        cond_low = cond_act.astype(jnp.bfloat16)
        mod_cols = (
            jnp.einsum("bd,dkc->bkc", cond_low, mod_full, preferred_element_type=jnp.float32)
            + mod_bias_f
        )
        mod_all, bias_all = (
            lax.all_gather(mod_cols, "tensor", axis=2, tiled=True),
            lax.all_gather(branch_bias_f, "tensor", axis=1, tiled=True),
        )
        norm_first, first_back = jax.vjp(modulate, lat_part, mod_all[:, 0], mod_all[:, 1])
        attn_rows = lax.all_gather(norm_first.astype(jnp.bfloat16), "tensor", axis=1, tiled=True)
        projected = jnp.einsum(
            "bsd,dkc->bskc", attn_rows, head_full, preferred_element_type=jnp.float32
        )
        head_shape = (per_group, seq_len, local_heads, HEAD_DIM)
        query_heads = (projected[:, :, 0] + head_bias_f[0]).astype(jnp.bfloat16).reshape(head_shape)
        key_heads = projected[:, :, 1].astype(jnp.bfloat16).reshape(head_shape)
        value_heads = (projected[:, :, 2] + head_bias_f[1]).astype(jnp.bfloat16).reshape(head_shape)
        mixed, logsum = attend_fwd(query_heads, key_heads, value_heads)
        mixed_low = mixed.reshape(per_group, seq_len, head_cols).astype(jnp.bfloat16)
        attn_part = jnp.einsum(
            "bsc,cd->bsd", mixed_low, mix_full, preferred_element_type=jnp.float32
        )
        attn_local = lax.psum_scatter(
            attn_part.astype(jnp.bfloat16), "tensor", scatter_dimension=1, tiled=True
        ).astype(jnp.float32)
        gate_attn = mod_all[:, 2][:, None, :]
        gate_mlp = mod_all[:, 5][:, None, :]
        first = lat_part + gate_attn * (attn_local + bias_all[0])
        norm_second, second_back = jax.vjp(modulate, first, mod_all[:, 3], mod_all[:, 4])
        mlp_rows = lax.all_gather(norm_second.astype(jnp.bfloat16), "tensor", axis=1, tiled=True)
        pre_act = (
            jnp.einsum("bsd,df->bsf", mlp_rows, up_full, preferred_element_type=jnp.float32)
            + up_bias_f
        )
        act_value, gelu_back = jax.vjp(gelu_tanh, pre_act)
        act_low = act_value.astype(jnp.bfloat16)
        mlp_part = jnp.einsum("bsf,fd->bsd", act_low, down_full, preferred_element_type=jnp.float32)
        mlp_local = lax.psum_scatter(
            mlp_part.astype(jnp.bfloat16), "tensor", scatter_dimension=1, tiled=True
        ).astype(jnp.float32)
        block_outs.append((first + gate_mlp * (mlp_local + bias_all[1])).astype(jnp.bfloat16))
        mod_full, head_full, mix_full, up_full, down_full = fetch_weights(
            mod_weight, head_weight, mix_weight, up_weight, down_weight
        )
        upstream = cotangent[row_start:row_stop].astype(jnp.float32)
        gate_m_grad = jnp.sum(upstream * (mlp_local + bias_all[1]), axis=1)
        tail_bias_grad = jnp.sum(gate_mlp * upstream, axis=(0, 1))
        mlp_grad = lax.all_gather(
            (gate_mlp * upstream).astype(jnp.bfloat16), "tensor", axis=1, tiled=True
        )
        down_grad = jnp.einsum("bsf,bsd->fd", act_low, mlp_grad, preferred_element_type=jnp.float32)
        act_grad = jnp.einsum(
            "bsd,fd->bsf", mlp_grad, down_full, preferred_element_type=jnp.float32
        )
        pre_grad = gelu_back(act_grad)[0].astype(jnp.bfloat16)
        up_bias_term = jnp.sum(pre_grad, axis=(0, 1), dtype=jnp.float32)
        up_grad = jnp.einsum("bsd,bsf->df", mlp_rows, pre_grad, preferred_element_type=jnp.float32)
        mlp_in_part = jnp.einsum(
            "bsf,df->bsd", pre_grad, up_full, preferred_element_type=jnp.float32
        )
        mlp_in_grad = lax.psum_scatter(
            mlp_in_part.astype(jnp.bfloat16), "tensor", scatter_dimension=1, tiled=True
        ).astype(jnp.float32)
        first_grad, shift_m_grad, scale_m_grad = second_back(mlp_in_grad)
        first_grad = first_grad + upstream
        gate_a_grad = jnp.sum(first_grad * (attn_local + bias_all[0]), axis=1)
        attn_bias_grad = jnp.sum(gate_attn * first_grad, axis=(0, 1))
        attn_branch_grad = (gate_attn * first_grad).astype(jnp.bfloat16)
        attn_grad = lax.all_gather(attn_branch_grad, "tensor", axis=1, tiled=True)
        mix_grad = jnp.einsum(
            "bsc,bsd->cd", mixed_low, attn_grad, preferred_element_type=jnp.float32
        )
        mixed_grad = jnp.einsum(
            "bsd,cd->bsc", attn_grad, mix_full, preferred_element_type=jnp.float32
        ).astype(jnp.bfloat16)
        query_grad, key_grad, value_grad = attend_bwd(
            query_heads, key_heads, value_heads, mixed_grad.reshape(head_shape), logsum
        )
        head_grads = (
            jnp.stack([query_grad, key_grad, value_grad], axis=2)
            .reshape(per_group, seq_len, 3, head_cols)
            .astype(jnp.bfloat16)
        )
        head_bias_term = jnp.sum(head_grads[:, :, 0::2], axis=(0, 1), dtype=jnp.float32)
        head_grad = jnp.einsum(
            "bsd,bskc->dkc", attn_rows, head_grads, preferred_element_type=jnp.float32
        )
        attn_in_part = jnp.einsum(
            "bskc,dkc->bsd", head_grads, head_full, preferred_element_type=jnp.float32
        )
        attn_in_grad = lax.psum_scatter(
            attn_in_part.astype(jnp.bfloat16), "tensor", scatter_dimension=1, tiled=True
        ).astype(jnp.float32)
        lat_grad, shift_a_grad, scale_a_grad = first_back(attn_in_grad)
        latent_grads.append((lat_grad + first_grad).astype(jnp.bfloat16))
        mod_terms = jnp.stack(
            [shift_a_grad, scale_a_grad, gate_a_grad, shift_m_grad, scale_m_grad, gate_m_grad],
            axis=1,
        )
        branch_terms = jnp.stack([attn_bias_grad, tail_bias_grad], axis=0)
        mod_grad_cols, branch_grad_cols = (
            lax.psum_scatter(
                mod_terms.astype(jnp.bfloat16), "tensor", scatter_dimension=2, tiled=True
            ).astype(jnp.float32),
            lax.psum_scatter(
                branch_terms.astype(jnp.bfloat16), "tensor", scatter_dimension=1, tiled=True
            ).astype(jnp.float32),
        )
        mod_grad_low = mod_grad_cols.astype(jnp.bfloat16)
        mod_grad = jnp.einsum(
            "bd,bkc->dkc", cond_low, mod_grad_low, preferred_element_type=jnp.float32
        )
        mod_bias_term = jnp.sum(mod_grad_low, axis=0, dtype=jnp.float32)
        cond_part_grad = jnp.einsum(
            "bkc,dkc->bd", mod_grad_low, mod_full, preferred_element_type=jnp.float32
        )
        cond_act_grad = lax.psum(cond_part_grad, "tensor")
        condition_grads.append(silu_back(cond_act_grad)[0])
        bias_totals = (
            bias_totals[0] + mod_bias_term,
            bias_totals[1] + head_bias_term,
            bias_totals[2] + up_bias_term,
            bias_totals[3] + branch_grad_cols,
        )
        weight_terms = (mod_grad, head_grad, mix_grad, up_grad, down_grad)
        grad_sums = (
            weight_terms if grad_sums is None else jax.tree.map(jnp.add, grad_sums, weight_terms)
        )
    grad_sums = reduce_weights(grad_sums)
    bias_sums = lax.psum((bias_totals[0], bias_totals[1], bias_totals[2], bias_totals[3]), "dp")
    return (
        jnp.concatenate(block_outs, axis=0),
        jnp.concatenate(latent_grads, axis=0),
        jnp.concatenate(condition_grads, axis=0),
        grad_sums[0],
        bias_sums[0],
        grad_sums[1],
        bias_sums[1],
        grad_sums[2],
        bias_sums[3],
        grad_sums[3],
        bias_sums[2],
        grad_sums[4],
    )


def head_window(col, width):
    start = jnp.minimum(col // 128 * 128, width - WINDOW)
    return pl.multiple_of(start, 128), col - start


def attn_fwd_kernel(q_ref, k_ref, v_ref, o_ref, lse_ref, vt_ref, ot_ref, *, blk):
    seq, width = q_ref.shape[1:]
    heads = width // HEAD_DIM
    c = HEAD_DIM ** -0.5 * LOG2E
    vt_ref[...] = v_ref[0].T
    lanes = lax.broadcasted_iota(jnp.int32, (blk, WINDOW), 1)

    def pair(i, carry):
        for odd in range(2):
            head = 2 * i + odd
            start, off = head_window(head * HEAD_DIM, width)
            keys = k_ref[0, :, pl.ds(start, WINDOW)]
            mask = (lanes >= off) & (lanes < off + HEAD_DIM)
            row = pl.multiple_of(i * (2 * HEAD_DIM) + odd * 64, 16)
            vt = vt_ref[pl.ds(row, 80), :]
            for b in range(seq // blk):
                rows = slice(b * blk, (b + 1) * blk)
                qb = q_ref[0, rows, pl.ds(start, WINDOW)]
                qb = jnp.where(mask, qb, jnp.zeros_like(qb))
                st = lax.dot_general(keys, qb, NT, preferred_element_type=f32)
                m = jnp.max(st, axis=0, keepdims=True)
                p = jnp.exp2((st - m) * c)
                l = jnp.sum(p, axis=0, keepdims=True)
                ot = jnp.dot(vt, p.astype(bf16), preferred_element_type=f32)
                ot_ref[pl.ds(pl.multiple_of(head * HEAD_DIM, 8), HEAD_DIM), rows] = (
                    ot[8 * odd : 8 * odd + HEAD_DIM] * (1.0 / l)
                )
                lse_ref[0, pl.ds(head, 1), rows] = m * c + jnp.log2(l)
        return carry

    lax.fori_loop(0, heads // 2, pair, 0)
    o_ref[0] = ot_ref[...].T.astype(bf16)


def attn_fwd(qkv, width, blk=256):
    n, seq, _ = qkv.shape
    spec = lambda j: pl.BlockSpec((1, seq, width), lambda b: (b, 0, j))
    heads = width // HEAD_DIM
    return pl.pallas_call(
        partial(attn_fwd_kernel, blk=blk),
        grid=(n,),
        in_specs=[spec(0), spec(1), spec(2)],
        out_specs=[
            pl.BlockSpec((1, seq, width), lambda b: (b, 0, 0)),
            pl.BlockSpec((1, heads, seq), lambda b: (b, 0, 0)),
        ],
        out_shape=[
            jax.ShapeDtypeStruct((n, seq, width), bf16),
            jax.ShapeDtypeStruct((n, heads, seq), f32),
        ],
        scratch_shapes=[pltpu.VMEM((width, seq), bf16), pltpu.VMEM((width, seq), f32)],
        compiler_params=pltpu.CompilerParams(vmem_limit_bytes=56 << 20),
        cost_estimate=pl.CostEstimate(
            flops=4 * n * seq * seq * width, bytes_accessed=8 * n * seq * width, transcendentals=n * heads * seq * seq
        ),
        name="attention_forward",
    )(qkv, qkv, qkv)


def attn_bwd_kernel(
    q_ref, k_ref, v_ref, do_ref, o_ref, lse_ref, dqkv_ref,
    kt_ref, dqt_ref, delta_ref, pt_ref, dst_ref, *, blk
):
    seq, width = q_ref.shape[1:]
    heads = width // HEAD_DIM
    scale = HEAD_DIM ** -0.5
    c = scale * LOG2E
    kt_ref[...] = k_ref[0].T
    prod = do_ref[0].astype(f32) * o_ref[0].astype(f32)
    high = prod.astype(bf16)
    low = (prod - high.astype(f32)).astype(bf16)
    col = lax.broadcasted_iota(jnp.int32, (heads, width), 1)
    first = lax.broadcasted_iota(jnp.int32, (heads, width), 0) * HEAD_DIM
    member = jnp.where((col >= first) & (col < first + HEAD_DIM), 1.0, 0.0).astype(bf16)
    delta_ref[...] = lax.dot_general(member, high, NT, preferred_element_type=f32) + lax.dot_general(
        member, low, NT, preferred_element_type=f32
    )
    lanes = lax.broadcasted_iota(jnp.int32, (seq, WINDOW), 1)

    def pair(i, carry):
        for odd in range(2):
            head = 2 * i + odd
            start, off = head_window(head * HEAD_DIM, width)
            window = pl.ds(start, WINDOW)
            mask = (lanes >= off) & (lanes < off + HEAD_DIM)
            keys = k_ref[0, :, window]
            values = v_ref[0, :, window]
            qm = q_ref[0, :, window]
            qm = jnp.where(mask, qm, jnp.zeros_like(qm))
            dom = do_ref[0, :, window]
            dom = jnp.where(mask, dom, jnp.zeros_like(dom))
            row = pl.multiple_of(i * (2 * HEAD_DIM) + odd * 64, 16)
            kt = kt_ref[pl.ds(row, 80), :]
            for b in range(seq // blk):
                rows = slice(b * blk, (b + 1) * blk)
                st = lax.dot_general(keys, qm[rows], NT, preferred_element_type=f32)
                dpt = lax.dot_general(values, dom[rows], NT, preferred_element_type=f32)
                p = jnp.exp2(st * c - lse_ref[0, pl.ds(head, 1), rows])
                dst = (p * (dpt - delta_ref[pl.ds(head, 1), rows])).astype(bf16)
                pt_ref[:, rows] = p.astype(bf16)
                dst_ref[:, rows] = dst
                dqt = jnp.dot(kt, dst, preferred_element_type=f32)
                dqt_ref[pl.ds(pl.multiple_of(head * HEAD_DIM, 8), HEAD_DIM), rows] = (
                    dqt[8 * odd : 8 * odd + HEAD_DIM] * scale
                )
            dk = jnp.dot(dst_ref[...], qm, preferred_element_type=f32) * scale
            dv = jnp.dot(pt_ref[...], dom, preferred_element_type=f32)
            kwin = pl.ds(pl.multiple_of(width + start, 128), WINDOW)
            vwin = pl.ds(pl.multiple_of(2 * width + start, 128), WINDOW)
            dqkv_ref[0, :, kwin] = jnp.where(mask, dk.astype(bf16), dqkv_ref[0, :, kwin])
            dqkv_ref[0, :, vwin] = jnp.where(mask, dv.astype(bf16), dqkv_ref[0, :, vwin])
        return carry

    lax.fori_loop(0, heads // 2, pair, 0)
    dqkv_ref[0, :, :width] = dqt_ref[...].T.astype(bf16)


def attn_bwd(qkv, grad, mixed, lse, width, blk=256):
    n, seq, _ = qkv.shape
    spec = lambda j: pl.BlockSpec((1, seq, width), lambda b: (b, 0, j))
    heads = width // HEAD_DIM
    return pl.pallas_call(
        partial(attn_bwd_kernel, blk=blk),
        grid=(n,),
        in_specs=[spec(0), spec(1), spec(2), spec(0), spec(0), pl.BlockSpec((1, heads, seq), lambda b: (b, 0, 0))],
        out_specs=pl.BlockSpec((1, seq, 3 * width), lambda b: (b, 0, 0)),
        out_shape=jax.ShapeDtypeStruct((n, seq, 3 * width), bf16),
        scratch_shapes=[
            pltpu.VMEM((width, seq), bf16),
            pltpu.VMEM((width, seq), f32),
            pltpu.VMEM((heads, seq), f32),
            pltpu.VMEM((seq, seq), bf16),
            pltpu.VMEM((seq, seq), bf16),
        ],
        compiler_params=pltpu.CompilerParams(vmem_limit_bytes=60 << 20),
        cost_estimate=pl.CostEstimate(
            flops=10 * n * seq * seq * width, bytes_accessed=16 * n * seq * width, transcendentals=n * heads * seq * seq
        ),
        name="attention_backward",
    )(qkv, qkv, qkv, grad, mixed, lse)


def normed(values):
    centred = values - jnp.mean(values, axis=-1, keepdims=True)
    variance = jnp.mean(centred * centred, axis=-1, keepdims=True)
    inverse = lax.rsqrt(variance + EPSILON)
    return centred * inverse, inverse


def normed_back(grad, norm, inverse):
    return inverse * (
        grad
        - jnp.mean(grad, axis=-1, keepdims=True)
        - norm * jnp.mean(grad * norm, axis=-1, keepdims=True)
    )


def mm(spec, a, b):
    return jnp.einsum(spec, a, b, preferred_element_type=f32)


def body_by_latents(
    latent,
    condition,
    cotangent,
    mod_weight,
    mod_bias,
    head_weight,
    head_bias,
    mix_weight,
    branch_bias,
    up_weight,
    up_bias,
    down_weight,
):
    side = lax.axis_index("tensor")
    rank = lax.axis_index("dp")
    groups = lax.axis_size("dp")
    count, half_seq, width = latent.shape
    own = count // 2
    cols = width // 2
    depth = head_weight.shape[0]
    hidden = 2 * up_weight.shape[1]

    def swap(a):
        return lax.ppermute(a, "tensor", [(0, 1), (1, 0)])

    def with_other(a, axis):
        return jnp.concatenate([a, swap(a)], axis=axis)

    def in_order(mine, other, axis):
        return jnp.where(
            side == 0,
            jnp.concatenate([mine, other], axis=axis),
            jnp.concatenate([other, mine], axis=axis),
        )

    def own_latents(a, axis=0):
        return lax.dynamic_slice_in_dim(a, side * own, own, axis)

    def other_latents(a, axis=0):
        return lax.dynamic_slice_in_dim(a, (1 - side) * own, own, axis)

    def take(a):
        return jnp.concatenate([own_latents(a), swap(other_latents(a))], axis=1)

    def give(a):
        return in_order(a[:, :half_seq], swap(a[:, half_seq:]), 0)

    cond_f = condition.astype(f32)
    cond_low = jax.nn.silu(cond_f).astype(bf16)
    cond_all = lax.all_gather(cond_low, "dp", axis=0, tiled=True)
    cond_cols = lax.dynamic_slice_in_dim(cond_all, rank * depth, depth, 1)
    partial_mod = mm("bd,dkc->bkc", cond_cols, mod_weight)
    arrived = lax.all_to_all(partial_mod, "dp", split_axis=0, concat_axis=0, tiled=True)
    mod_cols = jnp.sum(arrived.reshape(groups, count, 6, cols), axis=0) + mod_bias.astype(f32)
    modulation = in_order(own_latents(mod_cols), swap(other_latents(mod_cols)), 2)
    branch = branch_bias.astype(f32)
    branch_all = in_order(branch, swap(branch), 1)
    row = lambda k: modulation[:, k][:, None, :]
    shift_a, scale_a, gate_a, shift_m, scale_m, gate_m = [row(k) for k in range(6)]

    head_all = lax.all_gather(
        with_other(head_weight, 2).reshape(depth, 3 * width), "dp", axis=0, tiled=True
    )
    rest_all = lax.all_gather(
        jnp.concatenate(
            [with_other(mix_weight.T, 1), with_other(up_weight, 1), with_other(down_weight.T, 1)],
            axis=1,
        ),
        "dp",
        axis=0,
        tiled=True,
    )
    mix_t = rest_all[:, :width]
    up_all = rest_all[:, width : width + hidden]
    down_t = rest_all[:, width + hidden :]
    head_bias_f = with_other(head_bias.astype(f32), 1)
    up_bias_f = with_other(up_bias.astype(f32), 0)

    lat = take(latent)
    upstream_low = take(cotangent)
    lat_f = lat.astype(f32)
    norm1, inv1 = normed(lat_f)
    attn_in = (norm1 * (1.0 + scale_a) + shift_a).astype(bf16)
    qkv_bias = jnp.concatenate([head_bias_f[0], jnp.zeros((width,), f32), head_bias_f[1]])
    qkv = (mm("bsd,dc->bsc", attn_in, head_all) + qkv_bias).astype(bf16)
    mixed, logsum = attn_fwd(qkv, width)
    attn_out = mm("bsc,dc->bsd", mixed, mix_t) + branch_all[0]
    first = lat_f + gate_a * attn_out
    norm2, inv2 = normed(first)
    mlp_in = (norm2 * (1.0 + scale_m) + shift_m).astype(bf16)
    pre_act = mm("bsd,df->bsf", mlp_in, up_all) + up_bias_f
    act, gelu_back = jax.vjp(gelu_tanh, pre_act)
    act = act.astype(bf16)
    mlp_out = mm("bsf,df->bsd", act, down_t) + branch_all[1]
    block_out = give((first + gate_m * mlp_out).astype(bf16))

    upstream = upstream_low.astype(f32)
    gate_m_grad = jnp.sum(upstream * mlp_out, axis=1)
    tail_bias_grad = jnp.sum(gate_m[:, 0] * jnp.sum(upstream, axis=1), axis=0)
    mlp_grad = (gate_m * upstream).astype(bf16)
    down_grad = mm("bsd,bsf->df", mlp_grad, act).astype(bf16)
    down_sum = lax.psum_scatter(down_grad, "dp", scatter_dimension=0, tiled=True)
    pre_grad = gelu_back(mm("bsd,df->bsf", mlp_grad, down_t))[0].astype(bf16)
    up_bias_term = jnp.sum(pre_grad, axis=(0, 1), dtype=f32)
    up_grad = mm("bsd,bsf->df", mlp_in, pre_grad).astype(bf16)
    up_sum = lax.psum_scatter(up_grad, "dp", scatter_dimension=0, tiled=True)
    mlp_in_grad = mm("bsf,df->bsd", pre_grad, up_all)
    shift_m_grad = jnp.sum(mlp_in_grad, axis=1)
    scale_m_grad = jnp.sum(mlp_in_grad * norm2, axis=1)
    first_grad = upstream + normed_back(mlp_in_grad * (1.0 + scale_m), norm2, inv2)
    gate_a_grad = jnp.sum(first_grad * attn_out, axis=1)
    attn_bias_grad = jnp.sum(gate_a[:, 0] * jnp.sum(first_grad, axis=1), axis=0)
    attn_grad = (gate_a * first_grad).astype(bf16)
    mixed_grad = mm("bsd,dc->bsc", attn_grad, mix_t).astype(bf16)
    mix_grad = mm("bsd,bsc->dc", attn_grad, mixed).astype(bf16)
    mix_sum = lax.psum_scatter(mix_grad, "dp", scatter_dimension=0, tiled=True)
    qkv_grad = attn_bwd(qkv, mixed_grad, mixed, logsum, width)
    head_grad = mm("bsd,bsc->dc", attn_in, qkv_grad).astype(bf16)
    head_sum = lax.psum_scatter(head_grad, "dp", scatter_dimension=0, tiled=True)
    qkv_bias_term = jnp.sum(qkv_grad, axis=(0, 1), dtype=f32)
    attn_in_grad = mm("bsc,dc->bsd", qkv_grad, head_all)
    shift_a_grad = jnp.sum(attn_in_grad, axis=1)
    scale_a_grad = jnp.sum(attn_in_grad * norm1, axis=1)
    lat_grad = first_grad + normed_back(attn_in_grad * (1.0 + scale_a), norm1, inv1)
    latent_grad = give(lat_grad.astype(bf16))

    mod_low = jnp.stack(
        [shift_a_grad, scale_a_grad, gate_a_grad, shift_m_grad, scale_m_grad, gate_m_grad], axis=1
    ).astype(bf16)
    my_cols = lax.dynamic_slice_in_dim(mod_low, side * cols, cols, 2)
    other_cols = lax.dynamic_slice_in_dim(mod_low, (1 - side) * cols, cols, 2)
    mod_rows = lax.all_gather(
        in_order(my_cols, swap(other_cols), 0), "dp", axis=0, tiled=True
    )
    mod_weight_grad = mm("bd,bkc->dkc", cond_cols, mod_rows)
    mod_bias_grad = jnp.sum(mod_rows, axis=0, dtype=f32)
    cond_act = mm("bkc,dkc->bd", mod_rows, mod_weight)
    cond_act = cond_act + swap(cond_act)
    cond_act = lax.all_to_all(cond_act, "dp", split_axis=0, concat_axis=1, tiled=True)
    gate = jax.nn.sigmoid(cond_f)
    condition_grad = cond_act * (gate * (1.0 + cond_f * (1.0 - gate)))

    def joined(summed, axis):
        mine, other = jnp.split(summed, 2, axis=axis)
        return mine.astype(f32) + swap(other).astype(f32)

    head_weight_grad = joined(head_sum.reshape(depth, 3, width), 2)
    mix_weight_grad = joined(mix_sum, 1).T
    up_weight_grad = joined(up_sum, 1)
    down_weight_grad = joined(down_sum, 1).T
    branch_term = jnp.stack([attn_bias_grad, tail_bias_grad])
    head_term = qkv_bias_term.reshape(3, width)[0::2]

    def bias_half(mine):
        if mine:
            pieces = (head_term[:, :cols], lax.dynamic_slice_in_dim(branch_term, side * cols, cols, 1))
            ups = up_bias_term[: hidden // 2]
        else:
            pieces = (
                head_term[:, cols:],
                lax.dynamic_slice_in_dim(branch_term, (1 - side) * cols, cols, 1),
            )
            ups = up_bias_term[hidden // 2 :]
        return jnp.concatenate([p.reshape(-1) for p in pieces] + [ups])

    biases = lax.psum(bias_half(True) + swap(bias_half(False)), "dp")
    return (
        block_out,
        latent_grad,
        condition_grad,
        mod_weight_grad,
        mod_bias_grad,
        head_weight_grad,
        biases[: 2 * cols].reshape(2, cols),
        mix_weight_grad,
        biases[2 * cols : 4 * cols].reshape(2, cols),
        up_weight_grad,
        biases[4 * cols :],
        down_weight_grad,
    )


def solution(mesh):
    placed = (
        P("dp", "tensor", None),
        P("dp", None),
        P("dp", "tensor", None),
        P("dp", None, "tensor"),
        P(None, "tensor"),
        P("dp", None, "tensor"),
        P(None, "tensor"),
        P("tensor", "dp"),
        P(None, "tensor"),
        P("dp", "tensor"),
        P("tensor"),
        P("tensor", "dp"),
    )
    whole_latents = mesh.shape["tensor"] == 2
    return jax.shard_map(
        body_by_latents if whole_latents else body_by_heads,
        mesh=mesh,
        in_specs=placed,
        out_specs=(
            P("dp", "tensor", None),
            P("dp", "tensor", None),
            P("dp", None),
            P("dp", None, "tensor"),
            P(None, "tensor"),
            P("dp", None, "tensor"),
            P(None, "tensor"),
            P("tensor", "dp"),
            P(None, "tensor"),
            P("dp", "tensor"),
            P("tensor"),
            P("tensor", "dp"),
        ),
        check_vma=False,
    )
```

```python
from functools import partial

import jax
import jax.numpy as jnp
from jax import lax
from jax.experimental import pallas as pl
from jax.experimental.pallas import tpu as pltpu
from jax.sharding import PartitionSpec as P

SEQ = 1024
HEAD_DIM = 72
MICRO = 4
LOG2E = 1.4426950408889634
WINDOW = 256
f32 = jnp.float32
bf16 = jnp.bfloat16
NT = (((1,), (1,)), ((), ()))
MESH = pl.DeviceIdType.MESH


EPSILON = 1e-06


def layer_norm(values):
    centred = values - jnp.mean(values, axis=-1, keepdims=True)
    variance = jnp.mean(centred * centred, axis=-1, keepdims=True)
    return centred * lax.rsqrt(variance + EPSILON)


def modulate(values, shift, scale):
    return layer_norm(values) * (1.0 + scale[:, None, :]) + shift[:, None, :]


def gelu_tanh(values):
    return jax.nn.gelu(values, approximate=True)


def fetch_weights(mod_weight, head_weight, mix_weight, up_weight, down_weight):
    return (
        lax.all_gather(mod_weight, "dp", axis=0, tiled=True),
        lax.all_gather(head_weight, "dp", axis=0, tiled=True),
        lax.all_gather(mix_weight, "dp", axis=1, tiled=True),
        lax.all_gather(up_weight, "dp", axis=0, tiled=True),
        lax.all_gather(down_weight, "dp", axis=1, tiled=True),
    )


def reduce_weights(grads):
    return (
        lax.psum_scatter(
            grads[0].astype(jnp.bfloat16), "dp", scatter_dimension=0, tiled=True
        ).astype(jnp.float32),
        lax.psum_scatter(
            grads[1].astype(jnp.bfloat16), "dp", scatter_dimension=0, tiled=True
        ).astype(jnp.float32),
        lax.psum_scatter(
            grads[2].astype(jnp.bfloat16), "dp", scatter_dimension=1, tiled=True
        ).astype(jnp.float32),
        lax.psum_scatter(
            grads[3].astype(jnp.bfloat16), "dp", scatter_dimension=0, tiled=True
        ).astype(jnp.float32),
        lax.psum_scatter(
            grads[4].astype(jnp.bfloat16), "dp", scatter_dimension=1, tiled=True
        ).astype(jnp.float32),
    )


def attend_forward(queries, keys, values, block_rows, scale_factor):
    seq_len = queries.shape[0]
    blocked = queries.reshape(seq_len // block_rows, block_rows, queries.shape[1], queries.shape[2])

    def one_block(query_block):
        scores = (
            jnp.einsum("qhd,khd->hqk", query_block, keys, preferred_element_type=jnp.float32)
            * scale_factor
        )
        peak = jnp.max(scores, axis=-1, keepdims=True)
        raised = jnp.exp(scores - peak)
        total = jnp.sum(raised, axis=-1, keepdims=True)
        weights = (raised / total).astype(jnp.bfloat16)
        mixed = jnp.einsum("hqk,khd->qhd", weights, values, preferred_element_type=jnp.float32)
        return (mixed, (peak + jnp.log(total))[..., 0])

    mixed, logsum = lax.map(one_block, blocked)
    return (mixed.reshape(queries.shape), logsum)


def attend_backward(queries, keys, values, grad_mixed, logsum, block_rows, scale_factor):
    seq_len = queries.shape[0]
    block_shape = (seq_len // block_rows, block_rows, queries.shape[1], queries.shape[2])

    def one_block(carried, pieces):
        key_sum, value_sum = carried
        query_block, grad_block, logsum_block = pieces
        scores = (
            jnp.einsum("qhd,khd->hqk", query_block, keys, preferred_element_type=jnp.float32)
            * scale_factor
        )
        probs = jnp.exp(scores - logsum_block[..., None])
        prob_grad = jnp.einsum(
            "qhd,khd->hqk", grad_block, values, preferred_element_type=jnp.float32
        )
        inner = jnp.sum(probs * prob_grad, axis=-1, keepdims=True)
        score_grad = (probs * (prob_grad - inner)).astype(jnp.bfloat16)
        query_grad = (
            jnp.einsum("hqk,khd->qhd", score_grad, keys, preferred_element_type=jnp.float32)
            * scale_factor
        )
        key_sum = (
            key_sum
            + jnp.einsum(
                "hqk,qhd->khd", score_grad, query_block, preferred_element_type=jnp.float32
            )
            * scale_factor
        )
        value_sum = value_sum + jnp.einsum(
            "hqk,qhd->khd",
            probs.astype(jnp.bfloat16),
            grad_block,
            preferred_element_type=jnp.float32,
        )
        return ((key_sum, value_sum), query_grad)

    empty = jnp.zeros(keys.shape, jnp.float32)
    (key_grad, value_grad), query_grads = lax.scan(
        one_block,
        (empty, empty),
        (queries.reshape(block_shape), grad_mixed.reshape(block_shape), logsum),
    )
    return (query_grads.reshape(queries.shape), key_grad, value_grad)


def body_by_heads(
    latent,
    condition,
    cotangent,
    mod_weight,
    mod_bias,
    head_weight,
    head_bias,
    mix_weight,
    branch_bias,
    up_weight,
    up_bias,
    down_weight,
):
    per_group = latent.shape[0] // MICRO
    seq_len = SEQ
    head_cols = head_weight.shape[2]
    local_heads = head_cols // HEAD_DIM
    block_rows = min(512, seq_len)
    scale_factor = HEAD_DIM ** (-0.5)
    attend_fwd = jax.vmap(partial(attend_forward, block_rows=block_rows, scale_factor=scale_factor))
    attend_bwd = jax.vmap(
        partial(attend_backward, block_rows=block_rows, scale_factor=scale_factor)
    )
    head_bias_f = head_bias.astype(jnp.float32)
    up_bias_f = up_bias.astype(jnp.float32)
    mod_bias_f = mod_bias.astype(jnp.float32)
    branch_bias_f = branch_bias.astype(jnp.float32)
    bias_totals = (
        jnp.zeros(mod_bias.shape, jnp.float32),
        jnp.zeros(head_bias.shape, jnp.float32),
        jnp.zeros(up_bias.shape, jnp.float32),
        jnp.zeros(branch_bias.shape, jnp.float32),
    )
    grad_sums = None
    block_outs = []
    latent_grads = []
    condition_grads = []
    for micro_step in range(MICRO):
        row_start = micro_step * per_group
        row_stop = row_start + per_group
        mod_full, head_full, mix_full, up_full, down_full = fetch_weights(
            mod_weight, head_weight, mix_weight, up_weight, down_weight
        )
        lat_part = latent[row_start:row_stop].astype(jnp.float32)
        cond_part = condition[row_start:row_stop].astype(jnp.float32)
        cond_act, silu_back = jax.vjp(jax.nn.silu, cond_part)
        cond_low = cond_act.astype(jnp.bfloat16)
        mod_cols = (
            jnp.einsum("bd,dkc->bkc", cond_low, mod_full, preferred_element_type=jnp.float32)
            + mod_bias_f
        )
        mod_all, bias_all = (
            lax.all_gather(mod_cols, "tensor", axis=2, tiled=True),
            lax.all_gather(branch_bias_f, "tensor", axis=1, tiled=True),
        )
        norm_first, first_back = jax.vjp(modulate, lat_part, mod_all[:, 0], mod_all[:, 1])
        attn_rows = lax.all_gather(norm_first.astype(jnp.bfloat16), "tensor", axis=1, tiled=True)
        projected = jnp.einsum(
            "bsd,dkc->bskc", attn_rows, head_full, preferred_element_type=jnp.float32
        )
        head_shape = (per_group, seq_len, local_heads, HEAD_DIM)
        query_heads = (projected[:, :, 0] + head_bias_f[0]).astype(jnp.bfloat16).reshape(head_shape)
        key_heads = projected[:, :, 1].astype(jnp.bfloat16).reshape(head_shape)
        value_heads = (projected[:, :, 2] + head_bias_f[1]).astype(jnp.bfloat16).reshape(head_shape)
        mixed, logsum = attend_fwd(query_heads, key_heads, value_heads)
        mixed_low = mixed.reshape(per_group, seq_len, head_cols).astype(jnp.bfloat16)
        attn_part = jnp.einsum(
            "bsc,cd->bsd", mixed_low, mix_full, preferred_element_type=jnp.float32
        )
        attn_local = lax.psum_scatter(
            attn_part.astype(jnp.bfloat16), "tensor", scatter_dimension=1, tiled=True
        ).astype(jnp.float32)
        gate_attn = mod_all[:, 2][:, None, :]
        gate_mlp = mod_all[:, 5][:, None, :]
        first = lat_part + gate_attn * (attn_local + bias_all[0])
        norm_second, second_back = jax.vjp(modulate, first, mod_all[:, 3], mod_all[:, 4])
        mlp_rows = lax.all_gather(norm_second.astype(jnp.bfloat16), "tensor", axis=1, tiled=True)
        pre_act = (
            jnp.einsum("bsd,df->bsf", mlp_rows, up_full, preferred_element_type=jnp.float32)
            + up_bias_f
        )
        act_value, gelu_back = jax.vjp(gelu_tanh, pre_act)
        act_low = act_value.astype(jnp.bfloat16)
        mlp_part = jnp.einsum("bsf,fd->bsd", act_low, down_full, preferred_element_type=jnp.float32)
        mlp_local = lax.psum_scatter(
            mlp_part.astype(jnp.bfloat16), "tensor", scatter_dimension=1, tiled=True
        ).astype(jnp.float32)
        block_outs.append((first + gate_mlp * (mlp_local + bias_all[1])).astype(jnp.bfloat16))
        mod_full, head_full, mix_full, up_full, down_full = fetch_weights(
            mod_weight, head_weight, mix_weight, up_weight, down_weight
        )
        upstream = cotangent[row_start:row_stop].astype(jnp.float32)
        gate_m_grad = jnp.sum(upstream * (mlp_local + bias_all[1]), axis=1)
        tail_bias_grad = jnp.sum(gate_mlp * upstream, axis=(0, 1))
        mlp_grad = lax.all_gather(
            (gate_mlp * upstream).astype(jnp.bfloat16), "tensor", axis=1, tiled=True
        )
        down_grad = jnp.einsum("bsf,bsd->fd", act_low, mlp_grad, preferred_element_type=jnp.float32)
        act_grad = jnp.einsum(
            "bsd,fd->bsf", mlp_grad, down_full, preferred_element_type=jnp.float32
        )
        pre_grad = gelu_back(act_grad)[0].astype(jnp.bfloat16)
        up_bias_term = jnp.sum(pre_grad, axis=(0, 1), dtype=jnp.float32)
        up_grad = jnp.einsum("bsd,bsf->df", mlp_rows, pre_grad, preferred_element_type=jnp.float32)
        mlp_in_part = jnp.einsum(
            "bsf,df->bsd", pre_grad, up_full, preferred_element_type=jnp.float32
        )
        mlp_in_grad = lax.psum_scatter(
            mlp_in_part.astype(jnp.bfloat16), "tensor", scatter_dimension=1, tiled=True
        ).astype(jnp.float32)
        first_grad, shift_m_grad, scale_m_grad = second_back(mlp_in_grad)
        first_grad = first_grad + upstream
        gate_a_grad = jnp.sum(first_grad * (attn_local + bias_all[0]), axis=1)
        attn_bias_grad = jnp.sum(gate_attn * first_grad, axis=(0, 1))
        attn_branch_grad = (gate_attn * first_grad).astype(jnp.bfloat16)
        attn_grad = lax.all_gather(attn_branch_grad, "tensor", axis=1, tiled=True)
        mix_grad = jnp.einsum(
            "bsc,bsd->cd", mixed_low, attn_grad, preferred_element_type=jnp.float32
        )
        mixed_grad = jnp.einsum(
            "bsd,cd->bsc", attn_grad, mix_full, preferred_element_type=jnp.float32
        ).astype(jnp.bfloat16)
        query_grad, key_grad, value_grad = attend_bwd(
            query_heads, key_heads, value_heads, mixed_grad.reshape(head_shape), logsum
        )
        head_grads = (
            jnp.stack([query_grad, key_grad, value_grad], axis=2)
            .reshape(per_group, seq_len, 3, head_cols)
            .astype(jnp.bfloat16)
        )
        head_bias_term = jnp.sum(head_grads[:, :, 0::2], axis=(0, 1), dtype=jnp.float32)
        head_grad = jnp.einsum(
            "bsd,bskc->dkc", attn_rows, head_grads, preferred_element_type=jnp.float32
        )
        attn_in_part = jnp.einsum(
            "bskc,dkc->bsd", head_grads, head_full, preferred_element_type=jnp.float32
        )
        attn_in_grad = lax.psum_scatter(
            attn_in_part.astype(jnp.bfloat16), "tensor", scatter_dimension=1, tiled=True
        ).astype(jnp.float32)
        lat_grad, shift_a_grad, scale_a_grad = first_back(attn_in_grad)
        latent_grads.append((lat_grad + first_grad).astype(jnp.bfloat16))
        mod_terms = jnp.stack(
            [shift_a_grad, scale_a_grad, gate_a_grad, shift_m_grad, scale_m_grad, gate_m_grad],
            axis=1,
        )
        branch_terms = jnp.stack([attn_bias_grad, tail_bias_grad], axis=0)
        mod_grad_cols, branch_grad_cols = (
            lax.psum_scatter(
                mod_terms.astype(jnp.bfloat16), "tensor", scatter_dimension=2, tiled=True
            ).astype(jnp.float32),
            lax.psum_scatter(
                branch_terms.astype(jnp.bfloat16), "tensor", scatter_dimension=1, tiled=True
            ).astype(jnp.float32),
        )
        mod_grad_low = mod_grad_cols.astype(jnp.bfloat16)
        mod_grad = jnp.einsum(
            "bd,bkc->dkc", cond_low, mod_grad_low, preferred_element_type=jnp.float32
        )
        mod_bias_term = jnp.sum(mod_grad_low, axis=0, dtype=jnp.float32)
        cond_part_grad = jnp.einsum(
            "bkc,dkc->bd", mod_grad_low, mod_full, preferred_element_type=jnp.float32
        )
        cond_act_grad = lax.psum(cond_part_grad, "tensor")
        condition_grads.append(silu_back(cond_act_grad)[0])
        bias_totals = (
            bias_totals[0] + mod_bias_term,
            bias_totals[1] + head_bias_term,
            bias_totals[2] + up_bias_term,
            bias_totals[3] + branch_grad_cols,
        )
        weight_terms = (mod_grad, head_grad, mix_grad, up_grad, down_grad)
        grad_sums = (
            weight_terms if grad_sums is None else jax.tree.map(jnp.add, grad_sums, weight_terms)
        )
    grad_sums = reduce_weights(grad_sums)
    bias_sums = lax.psum((bias_totals[0], bias_totals[1], bias_totals[2], bias_totals[3]), "dp")
    return (
        jnp.concatenate(block_outs, axis=0),
        jnp.concatenate(latent_grads, axis=0),
        jnp.concatenate(condition_grads, axis=0),
        grad_sums[0],
        bias_sums[0],
        grad_sums[1],
        bias_sums[1],
        grad_sums[2],
        bias_sums[3],
        grad_sums[3],
        bias_sums[2],
        grad_sums[4],
    )


def head_window(col, width):
    start = jnp.minimum(col // 128 * 128, width - WINDOW)
    return pl.multiple_of(start, 128), col - start


def head_members(heads, width):
    col = lax.broadcasted_iota(jnp.int32, (heads, width), 1)
    first = lax.broadcasted_iota(jnp.int32, (heads, width), 0) * HEAD_DIM
    return jnp.where((col >= first) & (col < first + HEAD_DIM), 1.0, 0.0).astype(bf16)


def attn_fwd_kernel(q_ref, k_ref, v_ref, o_ref, lse_ref, ot_ref, *, blk, heads):
    seq, width = q_ref.shape[1:]
    c = HEAD_DIM ** -0.5 * LOG2E
    ot_ref[...] = v_ref[0].astype(f32).T
    lanes = lax.broadcasted_iota(jnp.int32, (blk, WINDOW), 1)
    ones = jnp.ones((8, seq), f32)
    member = head_members(heads, width)
    longest = [
        jnp.max(
            lax.dot_general(member, ref[0] * ref[0], NT, preferred_element_type=f32),
            axis=1,
            keepdims=True,
        )
        for ref in (q_ref, k_ref)
    ]
    small = jnp.max(longest[0] * longest[1]) * (1.1 * c * c) < 60.0 * 60.0

    def run(shifted):
        def pair(i, carry):
            steps = [(2 * i + odd, b) for odd in range(2) for b in range(seq // blk)]

            def scores(head, b):
                start, off = head_window(head * HEAD_DIM, width)
                mask = (lanes >= off) & (lanes < off + HEAD_DIM)
                qb = q_ref[0, b * blk : (b + 1) * blk, pl.ds(start, WINDOW)]
                qb = jnp.where(mask, qb, jnp.zeros_like(qb))
                return lax.dot_general(
                    k_ref[0, :, pl.ds(start, WINDOW)], qb, NT, preferred_element_type=f32
                )

            st = scores(*steps[0])
            vt = None
            for n, (head, b) in enumerate(steps):
                after = scores(*steps[n + 1]) if n + 1 < len(steps) else None
                mine = pl.ds(pl.multiple_of(head * HEAD_DIM, 8), HEAD_DIM)
                if b == 0:
                    vt = jnp.concatenate([ot_ref[mine, :], ones], axis=0).astype(bf16)
                rows = slice(b * blk, (b + 1) * blk)
                if shifted:
                    m = jnp.max(st, axis=0, keepdims=True)
                    p = jnp.exp2((st - m) * c).astype(bf16)
                else:
                    p = jnp.exp2(st * c).astype(bf16)
                ot = jnp.dot(vt, p, preferred_element_type=f32)
                l = ot[HEAD_DIM : HEAD_DIM + 1]
                ot_ref[mine, rows] = ot[:HEAD_DIM] * (1.0 / l)
                lse_ref[0, 0, pl.ds(head, 1), rows] = jnp.log2(l) + m * c if shifted else jnp.log2(l)
                st = after
            return carry

        lax.fori_loop(0, heads // 2, pair, 0)

    pl.when(small)(lambda: run(False))
    pl.when(jnp.logical_not(small))(lambda: run(True))
    o_ref[0] = ot_ref[...].T.astype(bf16)


def attn_fwd(qkv, heads, blk=256):
    n, seq, wide = qkv.shape
    width = wide // 6
    spec = lambda j: pl.BlockSpec((1, seq, width), lambda b, h: (b, 0, 3 * h + j))
    return pl.pallas_call(
        partial(attn_fwd_kernel, blk=blk, heads=heads),
        grid=(n, 2),
        in_specs=[spec(0), spec(1), spec(2)],
        out_specs=[
            pl.BlockSpec((1, seq, width), lambda b, h: (b, 0, h)),
            pl.BlockSpec((1, 1, heads, seq), lambda b, h: (b, h, 0, 0)),
        ],
        out_shape=[
            jax.ShapeDtypeStruct((n, seq, 2 * width), bf16),
            jax.ShapeDtypeStruct((n, 2, heads, seq), f32),
        ],
        scratch_shapes=[pltpu.VMEM((width, seq), f32)],
        compiler_params=pltpu.CompilerParams(vmem_limit_bytes=56 << 20),
        cost_estimate=pl.CostEstimate(
            flops=8 * n * seq * seq * width,
            bytes_accessed=16 * n * seq * width,
            transcendentals=2 * n * heads * seq * seq,
        ),
        name="attention_forward",
    )(qkv, qkv, qkv)


def attn_bwd_kernel(
    q_ref, k_ref, v_ref, do_ref, o_ref, lse_ref, dqkv_ref,
    dqt_ref, delta_ref, pt_ref, dst_ref, *, blk, heads
):
    seq, width = q_ref.shape[1:]
    scale = HEAD_DIM ** -0.5
    c = scale * LOG2E
    dqt_ref[...] = k_ref[0].astype(f32).T
    prod = do_ref[0].astype(f32) * o_ref[0].astype(f32)
    high = prod.astype(bf16)
    low = (prod - high.astype(f32)).astype(bf16)
    member = head_members(heads, width)
    delta_ref[...] = lax.dot_general(member, high, NT, preferred_element_type=f32) + lax.dot_general(
        member, low, NT, preferred_element_type=f32
    )
    lanes = lax.broadcasted_iota(jnp.int32, (seq, WINDOW), 1)
    edge = heads * HEAD_DIM // 128 * 128
    for part in (1, 2):
        dqkv_ref[0, :, part * width + edge : (part + 1) * width] = jnp.zeros((seq, width - edge), bf16)

    def one(head, carry):
        start, off = head_window(head * HEAD_DIM, width)
        window = pl.ds(start, WINDOW)
        mask = (lanes >= off) & (lanes < off + HEAD_DIM)
        keys = k_ref[0, :, window]
        values = v_ref[0, :, window]
        qm = q_ref[0, :, window]
        qm = jnp.where(mask, qm, jnp.zeros_like(qm))
        dom = do_ref[0, :, window]
        dom = jnp.where(mask, dom, jnp.zeros_like(dom))
        mine = pl.ds(pl.multiple_of(head * HEAD_DIM, 8), HEAD_DIM)
        kt = dqt_ref[mine, :].astype(bf16)
        for b in range(seq // blk):
            rows = slice(b * blk, (b + 1) * blk)
            st = lax.dot_general(keys, qm[rows], NT, preferred_element_type=f32)
            dpt = lax.dot_general(values, dom[rows], NT, preferred_element_type=f32)
            p = jnp.exp2(st * c - lse_ref[0, 0, pl.ds(head, 1), rows])
            dst = (p * (dpt - delta_ref[pl.ds(head, 1), rows])).astype(bf16)
            pt_ref[:, rows] = p.astype(bf16)
            dst_ref[:, rows] = dst
            dqt_ref[mine, rows] = jnp.dot(kt, dst, preferred_element_type=f32) * scale
        dk = jnp.dot(dst_ref[...], qm, preferred_element_type=f32) * scale
        dv = jnp.dot(pt_ref[...], dom, preferred_element_type=f32)
        kwin = pl.ds(pl.multiple_of(width + start, 128), WINDOW)
        vwin = pl.ds(pl.multiple_of(2 * width + start, 128), WINDOW)
        dqkv_ref[0, :, kwin] = jnp.where(mask, dk.astype(bf16), dqkv_ref[0, :, kwin])
        dqkv_ref[0, :, vwin] = jnp.where(mask, dv.astype(bf16), dqkv_ref[0, :, vwin])
        return carry

    lax.fori_loop(0, heads, one, 0)
    dqkv_ref[0, :, :width] = dqt_ref[...].T.astype(bf16)


def attn_bwd(qkv, grad, mixed, lse, heads, blk=256):
    n, seq, wide = qkv.shape
    width = wide // 6
    spec = lambda j: pl.BlockSpec((1, seq, width), lambda b, h: (b, 0, 3 * h + j))
    out = pl.BlockSpec((1, seq, width), lambda b, h: (b, 0, h))
    return pl.pallas_call(
        partial(attn_bwd_kernel, blk=blk, heads=heads),
        grid=(n, 2),
        in_specs=[
            spec(0), spec(1), spec(2), out, out,
            pl.BlockSpec((1, 1, heads, seq), lambda b, h: (b, h, 0, 0)),
        ],
        out_specs=pl.BlockSpec((1, seq, 3 * width), lambda b, h: (b, 0, h)),
        out_shape=jax.ShapeDtypeStruct(qkv.shape, bf16),
        scratch_shapes=[
            pltpu.VMEM((width, seq), f32),
            pltpu.VMEM((heads, seq), f32),
            pltpu.VMEM((seq, seq), bf16),
            pltpu.VMEM((seq, seq), bf16),
        ],
        compiler_params=pltpu.CompilerParams(vmem_limit_bytes=56 << 20),
        cost_estimate=pl.CostEstimate(
            flops=20 * n * seq * seq * width,
            bytes_accessed=32 * n * seq * width,
            transcendentals=2 * n * heads * seq * seq,
        ),
        name="attention_backward",
    )(qkv, qkv, qkv, grad, mixed, lse)


CORES = 2
ROWS = 2


def place(rank):
    return rank // (ROWS * CORES), rank // CORES % ROWS, rank % CORES


def rank_of(z, y, core):
    return (z * ROWS + y) * CORES + core


def greet(side):
    rank = lax.axis_index("dp")
    groups = lax.axis_size("dp")
    barrier = pltpu.get_barrier_semaphore()
    for step in range(1, groups):
        pl.semaphore_signal(barrier, inc=1, device_id={"dp": lax.rem(rank + step, groups)}, device_id_type=MESH)
    pl.semaphore_signal(barrier, inc=1, device_id={"tensor": 1 - side}, device_id_type=MESH)
    pl.semaphore_wait(barrier, groups)


class Spread:
    def __init__(self, source, out, sends, arrivals, lanes=None):
        self.source, self.out, self.sends, self.arrivals = source, out, sends, arrivals
        self.lanes = lanes
        self.rank = lax.axis_index("dp")
        self.z, self.y, self.core = place(self.rank)
        self.depth = lax.axis_size("dp") // (ROWS * CORES)
        self.started = []

    def block(self, origin):
        return self.out.at[origin] if self.lanes is None else self.out.at[origin, :, self.lanes]

    def copy(self, origin, edge, target, source=None):
        return pltpu.make_async_remote_copy(
            src_ref=self.block(origin) if source is None else source,
            dst_ref=self.block(origin),
            send_sem=self.sends.at[origin, edge],
            recv_sem=self.arrivals.at[origin],
            device_id={"dp": target},
            device_id_type=MESH,
        )

    def send(self, origin, edge, target, source=None, when=None):
        sent = self.copy(origin, edge, target, source)
        if when is None:
            sent.start()
        else:
            pl.when(when)(sent.start)
        self.started.append((sent, when))

    def arrive(self, origin):
        self.copy(origin, 0, rank_of(self.z, 1 - self.y, self.core)).wait_recv()

    def up(self):
        return rank_of(self.z + 1, self.y, self.core)

    def down(self):
        return rank_of(self.z - 1, self.y, self.core)

    def across(self):
        return rank_of(self.z, 1 - self.y, self.core)

    def sibling(self):
        return rank_of(self.z, self.y, 1 - self.core)

    def begin(self):
        rank, source = self.rank, self.source
        self.send(rank, 0, self.up(), source, self.z < self.depth - 1)
        self.send(rank, 3, self.down(), source, self.z > 0)
        self.send(rank, 1, self.across(), source)
        self.send(rank, 2, self.sibling(), source)

    def relay(self, hop):
        for toward, there in ((1, self.z >= hop), (-1, self.z + hop < self.depth)):
            origin = rank_of(self.z - toward * hop, self.y, self.core)
            further = (self.z < self.depth - 1) if toward > 0 else (self.z > 0)
            pl.when(there)(lambda: self.arrive(origin))
            self.send(
                origin, 0, self.up() if toward > 0 else self.down(), when=there & further
            )
            self.send(origin, 1, self.across(), when=there)
            self.send(origin, 2, self.sibling(), when=there)

    def relay_across(self, hop):
        for toward, there in ((1, self.z >= hop), (-1, self.z + hop < self.depth)):
            if hop == 0 and toward < 0:
                continue
            origin = rank_of(self.z - toward * hop, 1 - self.y, self.core)
            pl.when(there)(lambda: self.arrive(origin))
            self.send(origin, 2, self.sibling(), when=there)

    def finish(self):
        for z in range(self.depth):
            for y in range(ROWS):
                self.arrive(rank_of(z, y, 1 - self.core))
        for sent, when in self.started:
            if when is None:
                sent.wait_send()
            else:
                pl.when(when)(sent.wait_send)


def run_spreads(spreads):
    depth = spreads[0].depth
    for hop in range(1, depth):
        for s in spreads:
            s.relay(hop)
        for s in spreads:
            s.relay_across(hop - 1)
    for s in spreads:
        s.relay_across(depth - 1)
    for s in spreads:
        s.finish()


class Exchange:
    def __init__(self, source, out, sends, arrivals):
        self.source, self.out, self.sends, self.arrivals = source, out, sends, arrivals
        self.rank = lax.axis_index("dp")
        self.groups = lax.axis_size("dp")

    def copy(self, step):
        peer = lax.rem(self.rank + step, self.groups)
        return pltpu.make_async_remote_copy(
            src_ref=self.source.at[peer],
            dst_ref=self.out.at[self.rank],
            send_sem=self.sends.at[step],
            recv_sem=self.arrivals.at[self.rank],
            device_id={"dp": peer},
            device_id_type=MESH,
        )

    def begin(self):
        self.out[self.rank] = self.source[self.rank]
        for step in range(1, self.groups):
            self.copy(step).start()

    def finish(self):
        for step in range(1, self.groups):
            peer = lax.rem(self.rank + step, self.groups)
            pltpu.make_async_remote_copy(
                src_ref=self.source.at[peer],
                dst_ref=self.out.at[peer],
                send_sem=self.sends.at[step],
                recv_sem=self.arrivals.at[peer],
                device_id={"dp": peer},
                device_id_type=MESH,
            ).wait_recv()

    def drain(self):
        for step in range(1, self.groups):
            self.copy(step).wait_send()


def to_partner(source, target, side, sends, arrivals, k):
    return pltpu.make_async_remote_copy(
        src_ref=source,
        dst_ref=target,
        send_sem=sends.at[k],
        recv_sem=arrivals.at[k],
        device_id={"tensor": 1 - side},
        device_id_type=MESH,
    )


def opening_kernel(
    cond_ref, mod_w_ref, mod_bias_ref, head_ref, rest_ref, latent_ref,
    head_out, rest_out, latent_out, mod_out, cond_out,
    part_ref, mod_in,
    x_send, x_recv, c_send, c_recv, m_send, m_recv, h_send, h_recv, local_sem,
):
    side = lax.axis_index("tensor")
    rank = lax.axis_index("dp")
    own = latent_out.shape[0]
    greet(side)
    conds = Exchange(cond_ref, cond_out, c_send, c_recv)
    conds.begin()
    lanes = head_ref.shape[1]
    mine = Spread(head_ref, head_out, h_send.at[0], h_recv.at[0], pl.ds(0, lanes))
    other = Spread(None, head_out, h_send.at[1], h_recv.at[1], pl.ds(lanes, lanes))
    head_swap = to_partner(head_ref, other.block(rank), side, x_send, x_recv, 0)
    head_swap.start()
    mine.begin()
    latents = to_partner(
        latent_ref.at[pl.ds((1 - side) * own, own)], latent_out, side, x_send, x_recv, 1
    )
    latents.start()
    rest = to_partner(rest_ref, rest_out, side, x_send, x_recv, 3)
    rest.start()
    keep = pltpu.make_async_copy(head_ref, mine.block(rank), local_sem)
    keep.start()
    conds.finish()
    groups, rows, lanes = cond_out.shape
    half = mod_bias_ref.shape[1]
    low = cond_out[...].reshape(groups * rows, lanes).astype(bf16)
    front = lax.broadcasted_iota(jnp.int32, (groups * rows, half), 0) % rows < rows // 2
    part_ref[...] = jnp.where(
        front,
        jnp.dot(low, mod_w_ref[0], preferred_element_type=f32),
        jnp.dot(low, mod_w_ref[1], preferred_element_type=f32),
    ).reshape(groups, rows, half)
    mods = Exchange(part_ref, mod_in, m_send, m_recv)
    mods.begin()
    head_swap.wait_recv()
    other.begin()
    mine.relay(1)
    mods.finish()
    mod_out[0] = jnp.sum(mod_in[...], axis=0) + mod_bias_ref[...]
    mod_swap = to_partner(mod_out.at[0], mod_out.at[1], side, x_send, x_recv, 2)
    mod_swap.start()
    other.relay(1)
    mine.relay_across(0)
    other.relay_across(0)
    depth = mine.depth
    for hop in range(2, depth):
        for s in (mine, other):
            s.relay(hop)
            s.relay_across(hop - 1)
    for s in (mine, other):
        s.relay_across(depth - 1)
    keep.wait()
    mine.finish()
    other.finish()
    mod_swap.wait()
    latents.wait()
    rest.wait()
    head_swap.wait_send()
    conds.drain()
    mods.drain()


def opening(cond_low, mod_weight, mod_bias, head, rest, latent):
    groups = lax.axis_size("dp")
    count, half_seq, width = latent.shape
    depth = cond_low.shape[1] // groups
    half = mod_weight.shape[1] * mod_weight.shape[2] // 2
    blocks = cond_low.astype(f32).reshape(count, groups, depth).transpose(1, 0, 2)
    blocks = jnp.concatenate([blocks, blocks], axis=1)
    blocks = jnp.pad(blocks, ((0, 0), (0, 0), (0, 128 - depth)))
    weights = jnp.pad(mod_weight.reshape(depth, 2, half), ((0, 128 - depth), (0, 0), (0, 0))).transpose(1, 0, 2)
    bias = jnp.repeat(mod_bias.astype(f32).reshape(2, half), count, axis=0)
    dma = pltpu.SemaphoreType.DMA
    vmem = pl.BlockSpec(memory_space=pltpu.VMEM)
    anywhere = pl.BlockSpec(memory_space=pl.ANY)
    return pl.pallas_call(
        opening_kernel,
        in_specs=[vmem, vmem, vmem, anywhere, anywhere, anywhere],
        out_specs=[anywhere, anywhere, anywhere, vmem, vmem],
        out_shape=[
            jax.ShapeDtypeStruct((groups, depth, 2 * head.shape[1]), bf16),
            jax.ShapeDtypeStruct(rest.shape, bf16),
            jax.ShapeDtypeStruct((count // 2, half_seq, width), bf16),
            jax.ShapeDtypeStruct((2, 2 * count, half), f32),
            jax.ShapeDtypeStruct(blocks.shape, f32),
        ],
        scratch_shapes=[
            pltpu.VMEM((groups, 2 * count, half), f32),
            pltpu.VMEM((groups, 2 * count, half), f32),
            dma((4,)), dma((4,)),
            dma((groups,)), dma((groups,)),
            dma((groups,)), dma((groups,)),
            dma((2, groups, 4)), dma((2, groups)),
            dma,
        ],
        compiler_params=pltpu.CompilerParams(collective_id=0, has_side_effects=True, vmem_limit_bytes=32 << 20),
        name="opening",
    )(blocks, weights, bias, head, rest, latent)


def closing_kernel(
    mod_ref, bias_ref, mod_w_ref,
    mod_out, bias_out, cond_out,
    mod_unit, bias_unit, bias_in, part_ref, cond_in,
    x_send, x_recv, m_send, m_recv, b_send, b_recv, c_send, c_recv,
):
    side = lax.axis_index("tensor")
    rank = lax.axis_index("dp")
    greet(side)
    rows = mod_ref.shape[1]
    mod_swap = to_partner(mod_ref.at[1], mod_unit.at[1], side, x_send, x_recv, 0)
    mod_swap.start()
    bias_swap = to_partner(bias_ref.at[1], bias_unit.at[1], side, x_send, x_recv, 1)
    bias_swap.start()
    mod_swap.wait()
    bias_swap.wait()
    mod_out[rank] = mod_ref[0] + mod_unit[1]
    bias_in[rank] = bias_ref[0] + bias_unit[1]
    mods = Spread(None, mod_out, m_send, m_recv)
    biases = Spread(None, bias_in, b_send, b_recv)
    mods.begin()
    biases.begin()
    run_spreads([mods, biases])
    bias_out[...] = jnp.sum(bias_in[...], axis=0)
    groups, rows, half = mod_out.shape
    low = mod_out[...].reshape(groups * rows, half).astype(bf16)
    lanes = mod_w_ref.shape[1]
    front = lax.broadcasted_iota(jnp.int32, (groups * rows, lanes), 0) % rows < rows // 2
    part_ref[...] = jnp.where(
        front,
        lax.dot_general(low, mod_w_ref[0], NT, preferred_element_type=f32),
        lax.dot_general(low, mod_w_ref[1], NT, preferred_element_type=f32),
    ).reshape(groups, rows, lanes)
    conds = Exchange(part_ref, cond_in, c_send, c_recv)
    conds.begin()
    conds.finish()
    cond_out[0] = cond_in[...]
    cond_swap = to_partner(cond_out.at[0], cond_out.at[1], side, x_send, x_recv, 2)
    cond_swap.start()
    cond_swap.wait()
    conds.drain()


def closing(mod_pair, bias_pair, mod_weight):
    groups = lax.axis_size("dp")
    rows, half = mod_pair.shape[1:]
    depth = mod_weight.shape[0]
    weights = jnp.pad(mod_weight.reshape(depth, 2, half), ((0, 128 - depth), (0, 0), (0, 0))).transpose(1, 0, 2)
    dma = pltpu.SemaphoreType.DMA
    vmem = pl.BlockSpec(memory_space=pltpu.VMEM)
    lines = bias_pair.shape[1]
    return pl.pallas_call(
        closing_kernel,
        in_specs=[vmem, vmem, vmem],
        out_specs=[vmem, vmem, vmem],
        out_shape=[
            jax.ShapeDtypeStruct((groups, rows, half), f32),
            jax.ShapeDtypeStruct((lines, 128), f32),
            jax.ShapeDtypeStruct((2, groups, rows, 128), f32),
        ],
        scratch_shapes=[
            pltpu.VMEM((2, rows, half), f32),
            pltpu.VMEM((2, lines, 128), f32),
            pltpu.VMEM((groups, lines, 128), f32),
            pltpu.VMEM((groups, rows, 128), f32),
            pltpu.VMEM((groups, rows, 128), f32),
            dma((3,)), dma((3,)),
            dma((groups, 4)), dma((groups,)),
            dma((groups, 4)), dma((groups,)),
            dma((groups,)), dma((groups,)),
        ],
        compiler_params=pltpu.CompilerParams(collective_id=1, has_side_effects=True, vmem_limit_bytes=32 << 20),
        name="closing",
    )(mod_pair, bias_pair, weights)


def normed(values):
    centred = values - jnp.mean(values, axis=-1, keepdims=True)
    variance = jnp.mean(centred * centred, axis=-1, keepdims=True)
    inverse = lax.rsqrt(variance + EPSILON)
    return centred * inverse, inverse


def normed_back(grad, norm, inverse):
    return inverse * (
        grad
        - jnp.mean(grad, axis=-1, keepdims=True)
        - norm * jnp.mean(grad * norm, axis=-1, keepdims=True)
    )


def mm(spec, a, b):
    return jnp.einsum(spec, a, b, preferred_element_type=f32)


def body_by_latents(
    latent,
    condition,
    cotangent,
    mod_weight,
    mod_bias,
    head_weight,
    head_bias,
    mix_weight,
    branch_bias,
    up_weight,
    up_bias,
    down_weight,
):
    side = lax.axis_index("tensor")
    rank = lax.axis_index("dp")
    groups = lax.axis_size("dp")
    count, half_seq, width = latent.shape
    own = count // 2
    cols = width // 2
    depth = head_weight.shape[0]
    hidden = 2 * up_weight.shape[1]

    def swap(a):
        return lax.ppermute(a, "tensor", [(0, 1), (1, 0)])

    def with_other(a, axis):
        return jnp.concatenate([a, swap(a)], axis=axis)

    def in_order(mine, other, axis):
        return jnp.where(
            side == 0,
            jnp.concatenate([mine, other], axis=axis),
            jnp.concatenate([other, mine], axis=axis),
        )

    def own_latents(a, axis=0):
        return lax.dynamic_slice_in_dim(a, side * own, own, axis)

    def other_latents(a, axis=0):
        return lax.dynamic_slice_in_dim(a, (1 - side) * own, own, axis)

    def take(a):
        return jnp.concatenate([own_latents(a), swap(other_latents(a))], axis=1)

    def give(a):
        return in_order(a[:, :half_seq], swap(a[:, half_seq:]), 0)

    cond_f = condition.astype(f32)
    cond_low = jax.nn.silu(cond_f).astype(bf16)
    heads = cols // HEAD_DIM
    room = -(-cols // 128) * 128

    def roomy(a):
        return jnp.pad(a, [(0, 0)] * (a.ndim - 1) + [(0, room - cols)])

    head_shard = roomy(head_weight).reshape(depth, 3 * room)
    shards = jnp.concatenate([roomy(mix_weight.T), up_weight, down_weight.T], axis=1)
    head_all, shards_in, latent_in, mod_parts, cond_blocks = opening(
        cond_low, mod_weight, mod_bias, head_shard, shards, latent
    )
    head_all = head_all.reshape(width, 6 * room)
    mod_parts = mod_parts.reshape(2, 2, count, 3, cols)
    mod_parts = own_latents(mod_parts, 2).transpose(0, 2, 1, 3, 4).reshape(2, own, 6, cols)
    modulation = in_order(mod_parts[0], mod_parts[1], 2)
    cond_cols = cond_blocks[:, :count, :depth].reshape(groups * count, depth).astype(bf16)
    branch = branch_bias.astype(f32)
    branch_all = in_order(branch, swap(branch), 1)
    row = lambda k: modulation[:, k][:, None, :]
    shift_a, scale_a, gate_a, shift_m, scale_m, gate_m = [row(k) for k in range(6)]

    cuts = (0, room, room + hidden // 2, room + hidden)
    pieces = [a[:, lo:hi] for lo, hi in zip(cuts, cuts[1:]) for a in (shards, shards_in)]
    rest_all = lax.all_gather(jnp.concatenate(pieces, axis=1), "dp", axis=0, tiled=True)
    mix_t = rest_all[:, : 2 * room]
    up_all = rest_all[:, 2 * room : 2 * room + hidden]
    down_t = rest_all[:, 2 * room + hidden :]
    up_bias_f = with_other(up_bias.astype(f32), 0)

    lat = jnp.concatenate([own_latents(latent), latent_in], axis=1)
    later, _ = lax.optimization_barrier((other_latents(cotangent), latent_in))
    upstream_low = jnp.concatenate([own_latents(cotangent), swap(later)], axis=1)
    lat_f = lat.astype(f32)
    norm1, inv1 = normed(lat_f)
    attn_in = (norm1 * (1.0 + scale_a) + shift_a).astype(bf16)
    head_bias_f = roomy(head_bias.astype(f32))
    empty = jnp.zeros((room,), f32)
    qkv_bias = with_other(jnp.concatenate([head_bias_f[0], empty, head_bias_f[1]]), 0)
    qkv = (mm("bsd,dc->bsc", attn_in, head_all) + qkv_bias).astype(bf16)
    mixed, logsum = attn_fwd(qkv, heads)
    attn_out = mm("bsc,dc->bsd", mixed, mix_t) + branch_all[0]
    first = lat_f + gate_a * attn_out
    norm2, inv2 = normed(first)
    mlp_in = (norm2 * (1.0 + scale_m) + shift_m).astype(bf16)
    pre_act = mm("bsd,df->bsf", mlp_in, up_all) + up_bias_f
    act, gelu_back = jax.vjp(gelu_tanh, pre_act)
    act = act.astype(bf16)
    mlp_out = mm("bsf,df->bsd", act, down_t) + branch_all[1]
    block_out = give((first + gate_m * mlp_out).astype(bf16))

    upstream = upstream_low.astype(f32)
    gate_m_grad = jnp.sum(upstream * mlp_out, axis=1)
    tail_bias_grad = jnp.sum(gate_m[:, 0] * jnp.sum(upstream, axis=1), axis=0)
    mlp_grad = (gate_m * upstream).astype(bf16)
    down_grad = mm("bsd,bsf->df", mlp_grad, act).astype(bf16)
    down_grad, mlp_grad = lax.optimization_barrier((down_grad, mlp_grad))
    down_sum = lax.psum_scatter(down_grad, "dp", scatter_dimension=0, tiled=True)
    pre_grad = gelu_back(mm("bsd,df->bsf", mlp_grad, down_t))[0].astype(bf16)
    up_bias_term = jnp.sum(pre_grad, axis=(0, 1), dtype=f32)
    up_grad = mm("bsd,bsf->df", mlp_in, pre_grad).astype(bf16)
    up_grad, pre_grad = lax.optimization_barrier((up_grad, pre_grad))
    up_sum = lax.psum_scatter(up_grad, "dp", scatter_dimension=0, tiled=True)
    mlp_in_grad = mm("bsf,df->bsd", pre_grad, up_all)
    shift_m_grad = jnp.sum(mlp_in_grad, axis=1)
    scale_m_grad = jnp.sum(mlp_in_grad * norm2, axis=1)
    first_grad = upstream + normed_back(mlp_in_grad * (1.0 + scale_m), norm2, inv2)
    gate_a_grad = jnp.sum(first_grad * attn_out, axis=1)
    attn_bias_grad = jnp.sum(gate_a[:, 0] * jnp.sum(first_grad, axis=1), axis=0)
    attn_grad = (gate_a * first_grad).astype(bf16)
    mixed_grad = mm("bsd,dc->bsc", attn_grad, mix_t).astype(bf16)
    mix_grad = mm("bsd,bsc->dc", attn_grad, mixed).astype(bf16)
    mix_grad, mixed_grad = lax.optimization_barrier((mix_grad, mixed_grad))
    mix_sum = lax.psum_scatter(mix_grad, "dp", scatter_dimension=0, tiled=True)
    qkv_grad = attn_bwd(qkv, mixed_grad, mixed, logsum, heads)
    head_grad = mm("bsd,bsc->dc", attn_in, qkv_grad).astype(bf16)
    head_grad, qkv_grad = lax.optimization_barrier((head_grad, qkv_grad))
    head_sum = lax.psum_scatter(head_grad, "dp", scatter_dimension=0, tiled=True)
    qkv_bias_term = jnp.sum(qkv_grad, axis=(0, 1), dtype=f32)
    attn_in_grad = mm("bsc,dc->bsd", qkv_grad, head_all)
    shift_a_grad = jnp.sum(attn_in_grad, axis=1)
    scale_a_grad = jnp.sum(attn_in_grad * norm1, axis=1)
    lat_grad = first_grad + normed_back(attn_in_grad * (1.0 + scale_a), norm1, inv1)
    latent_grad = give(lat_grad.astype(bf16))

    mod_low = jnp.stack(
        [shift_a_grad, scale_a_grad, gate_a_grad, shift_m_grad, scale_m_grad, gate_m_grad], axis=1
    ).astype(bf16)
    branch_term = jnp.stack([attn_bias_grad, tail_bias_grad])
    head_term = qkv_bias_term.reshape(2, 3, room)[:, 0::2, :cols]
    ups = up_bias_term.reshape(2, hidden // 2)

    def mod_share(owner):
        mine = lax.dynamic_slice_in_dim(mod_low.astype(f32), owner * cols, cols, 2)
        mine = mine.reshape(own, 2, 3 * cols).transpose(1, 0, 2)
        empty = jnp.zeros((2, count, 3 * cols), f32)
        return lax.dynamic_update_slice_in_dim(empty, mine, side * own, 1).reshape(2 * count, 3 * cols)

    def bias_share(owner, k):
        branch_cols = lax.dynamic_slice_in_dim(branch_term, owner * cols, cols, 1)
        flat = jnp.concatenate([head_term[k].reshape(-1), branch_cols.reshape(-1), ups[k]])
        return flat.reshape(-1, 128)

    mod_blocks, biases, cond_parts = closing(
        jnp.stack([mod_share(side), mod_share(1 - side)]),
        jnp.stack([bias_share(side, 0), bias_share(1 - side, 1)]),
        mod_weight,
    )
    biases = biases.reshape(-1)
    mod_rows = mod_blocks.astype(bf16).reshape(groups, 2, count, 3, cols)
    mod_rows = mod_rows.transpose(0, 2, 1, 3, 4).reshape(groups * count, 6, cols)
    mod_weight_grad = mm("bd,bkc->dkc", cond_cols, mod_rows)
    mod_bias_grad = jnp.sum(mod_rows, axis=0, dtype=f32)
    cond_act = jnp.sum(cond_parts[..., :depth].reshape(2, groups, 2, count, depth), axis=(0, 2))
    cond_act = cond_act.transpose(1, 0, 2).reshape(count, groups * depth)
    gate = jax.nn.sigmoid(cond_f)
    condition_grad = cond_act * (gate * (1.0 + cond_f * (1.0 - gate)))

    def joined(summed, axis):
        mine, other = jnp.split(summed, 2, axis=axis)
        return mine.astype(f32) + swap(other).astype(f32)

    head_weight_grad = joined(head_sum, 1).reshape(depth, 3, room)[..., :cols]
    mix_weight_grad = joined(mix_sum, 1)[:, :cols].T
    up_weight_grad = joined(up_sum, 1)
    down_weight_grad = joined(down_sum, 1).T
    return (
        block_out,
        latent_grad,
        condition_grad,
        mod_weight_grad,
        mod_bias_grad,
        head_weight_grad,
        biases[: 2 * cols].reshape(2, cols),
        mix_weight_grad,
        biases[2 * cols : 4 * cols].reshape(2, cols),
        up_weight_grad,
        biases[4 * cols :],
        down_weight_grad,
    )


def solution(mesh):
    placed = (
        P("dp", "tensor", None),
        P("dp", None),
        P("dp", "tensor", None),
        P("dp", None, "tensor"),
        P(None, "tensor"),
        P("dp", None, "tensor"),
        P(None, "tensor"),
        P("tensor", "dp"),
        P(None, "tensor"),
        P("dp", "tensor"),
        P("tensor"),
        P("tensor", "dp"),
    )
    whole_latents = dict(mesh.shape) == {"dp": 16, "tensor": 2}
    return jax.shard_map(
        body_by_latents if whole_latents else body_by_heads,
        mesh=mesh,
        in_specs=placed,
        out_specs=(
            P("dp", "tensor", None),
            P("dp", "tensor", None),
            P("dp", None),
            P("dp", None, "tensor"),
            P(None, "tensor"),
            P("dp", None, "tensor"),
            P(None, "tensor"),
            P("tensor", "dp"),
            P(None, "tensor"),
            P("dp", "tensor"),
            P("tensor"),
            P("tensor", "dp"),
        ),
        check_vma=False,
    )
```

```python
from functools import partial

import jax
import jax.numpy as jnp
from jax import lax
from jax.experimental import pallas as pl
from jax.experimental.pallas import tpu as pltpu
from jax.sharding import PartitionSpec as P

SEQ = 1024
HEAD_DIM = 72
MICRO = 4
LOG2E = 1.4426950408889634
WINDOW = 256
f32 = jnp.float32
bf16 = jnp.bfloat16
NT = (((1,), (1,)), ((), ()))
MESH = pl.DeviceIdType.MESH


EPSILON = 1e-06


def layer_norm(values):
    centred = values - jnp.mean(values, axis=-1, keepdims=True)
    variance = jnp.mean(centred * centred, axis=-1, keepdims=True)
    return centred * lax.rsqrt(variance + EPSILON)


def modulate(values, shift, scale):
    return layer_norm(values) * (1.0 + scale[:, None, :]) + shift[:, None, :]


def gelu_tanh(values):
    return jax.nn.gelu(values, approximate=True)


def fetch_weights(mod_weight, head_weight, mix_weight, up_weight, down_weight):
    return (
        lax.all_gather(mod_weight, "dp", axis=0, tiled=True),
        lax.all_gather(head_weight, "dp", axis=0, tiled=True),
        lax.all_gather(mix_weight, "dp", axis=1, tiled=True),
        lax.all_gather(up_weight, "dp", axis=0, tiled=True),
        lax.all_gather(down_weight, "dp", axis=1, tiled=True),
    )


def reduce_weights(grads):
    return (
        lax.psum_scatter(
            grads[0].astype(jnp.bfloat16), "dp", scatter_dimension=0, tiled=True
        ).astype(jnp.float32),
        lax.psum_scatter(
            grads[1].astype(jnp.bfloat16), "dp", scatter_dimension=0, tiled=True
        ).astype(jnp.float32),
        lax.psum_scatter(
            grads[2].astype(jnp.bfloat16), "dp", scatter_dimension=1, tiled=True
        ).astype(jnp.float32),
        lax.psum_scatter(
            grads[3].astype(jnp.bfloat16), "dp", scatter_dimension=0, tiled=True
        ).astype(jnp.float32),
        lax.psum_scatter(
            grads[4].astype(jnp.bfloat16), "dp", scatter_dimension=1, tiled=True
        ).astype(jnp.float32),
    )


def attend_forward(queries, keys, values, block_rows, scale_factor):
    seq_len = queries.shape[0]
    blocked = queries.reshape(seq_len // block_rows, block_rows, queries.shape[1], queries.shape[2])

    def one_block(query_block):
        scores = (
            jnp.einsum("qhd,khd->hqk", query_block, keys, preferred_element_type=jnp.float32)
            * scale_factor
        )
        peak = jnp.max(scores, axis=-1, keepdims=True)
        raised = jnp.exp(scores - peak)
        total = jnp.sum(raised, axis=-1, keepdims=True)
        weights = (raised / total).astype(jnp.bfloat16)
        mixed = jnp.einsum("hqk,khd->qhd", weights, values, preferred_element_type=jnp.float32)
        return (mixed, (peak + jnp.log(total))[..., 0])

    mixed, logsum = lax.map(one_block, blocked)
    return (mixed.reshape(queries.shape), logsum)


def attend_backward(queries, keys, values, grad_mixed, logsum, block_rows, scale_factor):
    seq_len = queries.shape[0]
    block_shape = (seq_len // block_rows, block_rows, queries.shape[1], queries.shape[2])

    def one_block(carried, pieces):
        key_sum, value_sum = carried
        query_block, grad_block, logsum_block = pieces
        scores = (
            jnp.einsum("qhd,khd->hqk", query_block, keys, preferred_element_type=jnp.float32)
            * scale_factor
        )
        probs = jnp.exp(scores - logsum_block[..., None])
        prob_grad = jnp.einsum(
            "qhd,khd->hqk", grad_block, values, preferred_element_type=jnp.float32
        )
        inner = jnp.sum(probs * prob_grad, axis=-1, keepdims=True)
        score_grad = (probs * (prob_grad - inner)).astype(jnp.bfloat16)
        query_grad = (
            jnp.einsum("hqk,khd->qhd", score_grad, keys, preferred_element_type=jnp.float32)
            * scale_factor
        )
        key_sum = (
            key_sum
            + jnp.einsum(
                "hqk,qhd->khd", score_grad, query_block, preferred_element_type=jnp.float32
            )
            * scale_factor
        )
        value_sum = value_sum + jnp.einsum(
            "hqk,qhd->khd",
            probs.astype(jnp.bfloat16),
            grad_block,
            preferred_element_type=jnp.float32,
        )
        return ((key_sum, value_sum), query_grad)

    empty = jnp.zeros(keys.shape, jnp.float32)
    (key_grad, value_grad), query_grads = lax.scan(
        one_block,
        (empty, empty),
        (queries.reshape(block_shape), grad_mixed.reshape(block_shape), logsum),
    )
    return (query_grads.reshape(queries.shape), key_grad, value_grad)


def body_by_heads(
    latent,
    condition,
    cotangent,
    mod_weight,
    mod_bias,
    head_weight,
    head_bias,
    mix_weight,
    branch_bias,
    up_weight,
    up_bias,
    down_weight,
):
    per_group = latent.shape[0] // MICRO
    seq_len = SEQ
    head_cols = head_weight.shape[2]
    local_heads = head_cols // HEAD_DIM
    block_rows = min(512, seq_len)
    scale_factor = HEAD_DIM ** (-0.5)
    attend_fwd = jax.vmap(partial(attend_forward, block_rows=block_rows, scale_factor=scale_factor))
    attend_bwd = jax.vmap(
        partial(attend_backward, block_rows=block_rows, scale_factor=scale_factor)
    )
    head_bias_f = head_bias.astype(jnp.float32)
    up_bias_f = up_bias.astype(jnp.float32)
    mod_bias_f = mod_bias.astype(jnp.float32)
    branch_bias_f = branch_bias.astype(jnp.float32)
    bias_totals = (
        jnp.zeros(mod_bias.shape, jnp.float32),
        jnp.zeros(head_bias.shape, jnp.float32),
        jnp.zeros(up_bias.shape, jnp.float32),
        jnp.zeros(branch_bias.shape, jnp.float32),
    )
    grad_sums = None
    block_outs = []
    latent_grads = []
    condition_grads = []
    for micro_step in range(MICRO):
        row_start = micro_step * per_group
        row_stop = row_start + per_group
        mod_full, head_full, mix_full, up_full, down_full = fetch_weights(
            mod_weight, head_weight, mix_weight, up_weight, down_weight
        )
        lat_part = latent[row_start:row_stop].astype(jnp.float32)
        cond_part = condition[row_start:row_stop].astype(jnp.float32)
        cond_act, silu_back = jax.vjp(jax.nn.silu, cond_part)
        cond_low = cond_act.astype(jnp.bfloat16)
        mod_cols = (
            jnp.einsum("bd,dkc->bkc", cond_low, mod_full, preferred_element_type=jnp.float32)
            + mod_bias_f
        )
        mod_all, bias_all = (
            lax.all_gather(mod_cols, "tensor", axis=2, tiled=True),
            lax.all_gather(branch_bias_f, "tensor", axis=1, tiled=True),
        )
        norm_first, first_back = jax.vjp(modulate, lat_part, mod_all[:, 0], mod_all[:, 1])
        attn_rows = lax.all_gather(norm_first.astype(jnp.bfloat16), "tensor", axis=1, tiled=True)
        projected = jnp.einsum(
            "bsd,dkc->bskc", attn_rows, head_full, preferred_element_type=jnp.float32
        )
        head_shape = (per_group, seq_len, local_heads, HEAD_DIM)
        query_heads = (projected[:, :, 0] + head_bias_f[0]).astype(jnp.bfloat16).reshape(head_shape)
        key_heads = projected[:, :, 1].astype(jnp.bfloat16).reshape(head_shape)
        value_heads = (projected[:, :, 2] + head_bias_f[1]).astype(jnp.bfloat16).reshape(head_shape)
        mixed, logsum = attend_fwd(query_heads, key_heads, value_heads)
        mixed_low = mixed.reshape(per_group, seq_len, head_cols).astype(jnp.bfloat16)
        attn_part = jnp.einsum(
            "bsc,cd->bsd", mixed_low, mix_full, preferred_element_type=jnp.float32
        )
        attn_local = lax.psum_scatter(
            attn_part.astype(jnp.bfloat16), "tensor", scatter_dimension=1, tiled=True
        ).astype(jnp.float32)
        gate_attn = mod_all[:, 2][:, None, :]
        gate_mlp = mod_all[:, 5][:, None, :]
        first = lat_part + gate_attn * (attn_local + bias_all[0])
        norm_second, second_back = jax.vjp(modulate, first, mod_all[:, 3], mod_all[:, 4])
        mlp_rows = lax.all_gather(norm_second.astype(jnp.bfloat16), "tensor", axis=1, tiled=True)
        pre_act = (
            jnp.einsum("bsd,df->bsf", mlp_rows, up_full, preferred_element_type=jnp.float32)
            + up_bias_f
        )
        act_value, gelu_back = jax.vjp(gelu_tanh, pre_act)
        act_low = act_value.astype(jnp.bfloat16)
        mlp_part = jnp.einsum("bsf,fd->bsd", act_low, down_full, preferred_element_type=jnp.float32)
        mlp_local = lax.psum_scatter(
            mlp_part.astype(jnp.bfloat16), "tensor", scatter_dimension=1, tiled=True
        ).astype(jnp.float32)
        block_outs.append((first + gate_mlp * (mlp_local + bias_all[1])).astype(jnp.bfloat16))
        mod_full, head_full, mix_full, up_full, down_full = fetch_weights(
            mod_weight, head_weight, mix_weight, up_weight, down_weight
        )
        upstream = cotangent[row_start:row_stop].astype(jnp.float32)
        gate_m_grad = jnp.sum(upstream * (mlp_local + bias_all[1]), axis=1)
        tail_bias_grad = jnp.sum(gate_mlp * upstream, axis=(0, 1))
        mlp_grad = lax.all_gather(
            (gate_mlp * upstream).astype(jnp.bfloat16), "tensor", axis=1, tiled=True
        )
        down_grad = jnp.einsum("bsf,bsd->fd", act_low, mlp_grad, preferred_element_type=jnp.float32)
        act_grad = jnp.einsum(
            "bsd,fd->bsf", mlp_grad, down_full, preferred_element_type=jnp.float32
        )
        pre_grad = gelu_back(act_grad)[0].astype(jnp.bfloat16)
        up_bias_term = jnp.sum(pre_grad, axis=(0, 1), dtype=jnp.float32)
        up_grad = jnp.einsum("bsd,bsf->df", mlp_rows, pre_grad, preferred_element_type=jnp.float32)
        mlp_in_part = jnp.einsum(
            "bsf,df->bsd", pre_grad, up_full, preferred_element_type=jnp.float32
        )
        mlp_in_grad = lax.psum_scatter(
            mlp_in_part.astype(jnp.bfloat16), "tensor", scatter_dimension=1, tiled=True
        ).astype(jnp.float32)
        first_grad, shift_m_grad, scale_m_grad = second_back(mlp_in_grad)
        first_grad = first_grad + upstream
        gate_a_grad = jnp.sum(first_grad * (attn_local + bias_all[0]), axis=1)
        attn_bias_grad = jnp.sum(gate_attn * first_grad, axis=(0, 1))
        attn_branch_grad = (gate_attn * first_grad).astype(jnp.bfloat16)
        attn_grad = lax.all_gather(attn_branch_grad, "tensor", axis=1, tiled=True)
        mix_grad = jnp.einsum(
            "bsc,bsd->cd", mixed_low, attn_grad, preferred_element_type=jnp.float32
        )
        mixed_grad = jnp.einsum(
            "bsd,cd->bsc", attn_grad, mix_full, preferred_element_type=jnp.float32
        ).astype(jnp.bfloat16)
        query_grad, key_grad, value_grad = attend_bwd(
            query_heads, key_heads, value_heads, mixed_grad.reshape(head_shape), logsum
        )
        head_grads = (
            jnp.stack([query_grad, key_grad, value_grad], axis=2)
            .reshape(per_group, seq_len, 3, head_cols)
            .astype(jnp.bfloat16)
        )
        head_bias_term = jnp.sum(head_grads[:, :, 0::2], axis=(0, 1), dtype=jnp.float32)
        head_grad = jnp.einsum(
            "bsd,bskc->dkc", attn_rows, head_grads, preferred_element_type=jnp.float32
        )
        attn_in_part = jnp.einsum(
            "bskc,dkc->bsd", head_grads, head_full, preferred_element_type=jnp.float32
        )
        attn_in_grad = lax.psum_scatter(
            attn_in_part.astype(jnp.bfloat16), "tensor", scatter_dimension=1, tiled=True
        ).astype(jnp.float32)
        lat_grad, shift_a_grad, scale_a_grad = first_back(attn_in_grad)
        latent_grads.append((lat_grad + first_grad).astype(jnp.bfloat16))
        mod_terms = jnp.stack(
            [shift_a_grad, scale_a_grad, gate_a_grad, shift_m_grad, scale_m_grad, gate_m_grad],
            axis=1,
        )
        branch_terms = jnp.stack([attn_bias_grad, tail_bias_grad], axis=0)
        mod_grad_cols, branch_grad_cols = (
            lax.psum_scatter(
                mod_terms.astype(jnp.bfloat16), "tensor", scatter_dimension=2, tiled=True
            ).astype(jnp.float32),
            lax.psum_scatter(
                branch_terms.astype(jnp.bfloat16), "tensor", scatter_dimension=1, tiled=True
            ).astype(jnp.float32),
        )
        mod_grad_low = mod_grad_cols.astype(jnp.bfloat16)
        mod_grad = jnp.einsum(
            "bd,bkc->dkc", cond_low, mod_grad_low, preferred_element_type=jnp.float32
        )
        mod_bias_term = jnp.sum(mod_grad_low, axis=0, dtype=jnp.float32)
        cond_part_grad = jnp.einsum(
            "bkc,dkc->bd", mod_grad_low, mod_full, preferred_element_type=jnp.float32
        )
        cond_act_grad = lax.psum(cond_part_grad, "tensor")
        condition_grads.append(silu_back(cond_act_grad)[0])
        bias_totals = (
            bias_totals[0] + mod_bias_term,
            bias_totals[1] + head_bias_term,
            bias_totals[2] + up_bias_term,
            bias_totals[3] + branch_grad_cols,
        )
        weight_terms = (mod_grad, head_grad, mix_grad, up_grad, down_grad)
        grad_sums = (
            weight_terms if grad_sums is None else jax.tree.map(jnp.add, grad_sums, weight_terms)
        )
    grad_sums = reduce_weights(grad_sums)
    bias_sums = lax.psum((bias_totals[0], bias_totals[1], bias_totals[2], bias_totals[3]), "dp")
    return (
        jnp.concatenate(block_outs, axis=0),
        jnp.concatenate(latent_grads, axis=0),
        jnp.concatenate(condition_grads, axis=0),
        grad_sums[0],
        bias_sums[0],
        grad_sums[1],
        bias_sums[1],
        grad_sums[2],
        bias_sums[3],
        grad_sums[3],
        bias_sums[2],
        grad_sums[4],
    )


def head_window(col, width):
    start = jnp.minimum(col // 128 * 128, width - WINDOW)
    return pl.multiple_of(start, 128), col - start


def head_members(heads, width):
    col = lax.broadcasted_iota(jnp.int32, (heads, width), 1)
    first = lax.broadcasted_iota(jnp.int32, (heads, width), 0) * HEAD_DIM
    return jnp.where((col >= first) & (col < first + HEAD_DIM), 1.0, 0.0).astype(bf16)


def attn_fwd_kernel(q_ref, k_ref, v_ref, o_ref, lse_ref, ot_ref, *, blk, heads):
    seq, width = q_ref.shape[1:]
    c = HEAD_DIM ** -0.5 * LOG2E
    ot_ref[...] = v_ref[0].astype(f32).T
    lanes = lax.broadcasted_iota(jnp.int32, (blk, WINDOW), 1)
    ones = jnp.ones((8, seq), f32)
    member = head_members(heads, width)
    longest = [
        jnp.max(
            lax.dot_general(member, ref[0] * ref[0], NT, preferred_element_type=f32),
            axis=1,
            keepdims=True,
        )
        for ref in (q_ref, k_ref)
    ]
    small = jnp.max(longest[0] * longest[1]) * (1.1 * c * c) < 60.0 * 60.0

    def run(shifted):
        def pair(i, carry):
            steps = [(2 * i + odd, b) for odd in range(2) for b in range(seq // blk)]

            def scores(head, b):
                start, off = head_window(head * HEAD_DIM, width)
                mask = (lanes >= off) & (lanes < off + HEAD_DIM)
                qb = q_ref[0, b * blk : (b + 1) * blk, pl.ds(start, WINDOW)]
                qb = jnp.where(mask, qb, jnp.zeros_like(qb))
                return lax.dot_general(
                    k_ref[0, :, pl.ds(start, WINDOW)], qb, NT, preferred_element_type=f32
                )

            st = scores(*steps[0])
            vt = None
            for n, (head, b) in enumerate(steps):
                after = scores(*steps[n + 1]) if n + 1 < len(steps) else None
                mine = pl.ds(pl.multiple_of(head * HEAD_DIM, 8), HEAD_DIM)
                if b == 0:
                    vt = jnp.concatenate([ot_ref[mine, :], ones], axis=0).astype(bf16)
                rows = slice(b * blk, (b + 1) * blk)
                if shifted:
                    m = jnp.max(st, axis=0, keepdims=True)
                    p = jnp.exp2((st - m) * c).astype(bf16)
                else:
                    p = jnp.exp2(st * c).astype(bf16)
                ot = jnp.dot(vt, p, preferred_element_type=f32)
                l = ot[HEAD_DIM : HEAD_DIM + 1]
                ot_ref[mine, rows] = ot[:HEAD_DIM] * (1.0 / l)
                lse_ref[0, 0, pl.ds(head, 1), rows] = jnp.log2(l) + m * c if shifted else jnp.log2(l)
                st = after
            return carry

        lax.fori_loop(0, heads // 2, pair, 0)

    pl.when(small)(lambda: run(False))
    pl.when(jnp.logical_not(small))(lambda: run(True))
    o_ref[0] = ot_ref[...].T.astype(bf16)


def attn_fwd(qkv, heads, blk=256):
    n, seq, wide = qkv.shape
    width = wide // 6
    spec = lambda j: pl.BlockSpec((1, seq, width), lambda b, h: (b, 0, 3 * h + j))
    return pl.pallas_call(
        partial(attn_fwd_kernel, blk=blk, heads=heads),
        grid=(n, 2),
        in_specs=[spec(0), spec(1), spec(2)],
        out_specs=[
            pl.BlockSpec((1, seq, width), lambda b, h: (b, 0, h)),
            pl.BlockSpec((1, 1, heads, seq), lambda b, h: (b, h, 0, 0)),
        ],
        out_shape=[
            jax.ShapeDtypeStruct((n, seq, 2 * width), bf16),
            jax.ShapeDtypeStruct((n, 2, heads, seq), f32),
        ],
        scratch_shapes=[pltpu.VMEM((width, seq), f32)],
        compiler_params=pltpu.CompilerParams(vmem_limit_bytes=56 << 20),
        cost_estimate=pl.CostEstimate(
            flops=8 * n * seq * seq * width,
            bytes_accessed=16 * n * seq * width,
            transcendentals=2 * n * heads * seq * seq,
        ),
        name="attention_forward",
    )(qkv, qkv, qkv)


def attn_bwd_kernel(
    q_ref, k_ref, v_ref, do_ref, o_ref, lse_ref, dqkv_ref,
    dqt_ref, delta_ref, pt_ref, dst_ref, *, blk, heads
):
    seq, width = q_ref.shape[1:]
    scale = HEAD_DIM ** -0.5
    c = scale * LOG2E
    dqt_ref[...] = k_ref[0].astype(f32).T
    prod = do_ref[0].astype(f32) * o_ref[0].astype(f32)
    high = prod.astype(bf16)
    low = (prod - high.astype(f32)).astype(bf16)
    member = head_members(heads, width)
    delta_ref[...] = lax.dot_general(member, high, NT, preferred_element_type=f32) + lax.dot_general(
        member, low, NT, preferred_element_type=f32
    )
    lanes = lax.broadcasted_iota(jnp.int32, (seq, WINDOW), 1)
    edge = heads * HEAD_DIM // 128 * 128
    for part in (1, 2):
        dqkv_ref[0, :, part * width + edge : (part + 1) * width] = jnp.zeros((seq, width - edge), bf16)

    def one(head, carry):
        start, off = head_window(head * HEAD_DIM, width)
        window = pl.ds(start, WINDOW)
        mask = (lanes >= off) & (lanes < off + HEAD_DIM)
        keys = k_ref[0, :, window]
        values = v_ref[0, :, window]
        qm = q_ref[0, :, window]
        qm = jnp.where(mask, qm, jnp.zeros_like(qm))
        dom = do_ref[0, :, window]
        dom = jnp.where(mask, dom, jnp.zeros_like(dom))
        mine = pl.ds(pl.multiple_of(head * HEAD_DIM, 8), HEAD_DIM)
        kt = dqt_ref[mine, :].astype(bf16)
        for b in range(seq // blk):
            rows = slice(b * blk, (b + 1) * blk)
            st = lax.dot_general(keys, qm[rows], NT, preferred_element_type=f32)
            dpt = lax.dot_general(values, dom[rows], NT, preferred_element_type=f32)
            p = jnp.exp2(st * c - lse_ref[0, 0, pl.ds(head, 1), rows])
            dst = (p * (dpt - delta_ref[pl.ds(head, 1), rows])).astype(bf16)
            pt_ref[:, rows] = p.astype(bf16)
            dst_ref[:, rows] = dst
            dqt_ref[mine, rows] = jnp.dot(kt, dst, preferred_element_type=f32) * scale
        dk = jnp.dot(dst_ref[...], qm, preferred_element_type=f32) * scale
        dv = jnp.dot(pt_ref[...], dom, preferred_element_type=f32)
        kwin = pl.ds(pl.multiple_of(width + start, 128), WINDOW)
        vwin = pl.ds(pl.multiple_of(2 * width + start, 128), WINDOW)
        dqkv_ref[0, :, kwin] = jnp.where(mask, dk.astype(bf16), dqkv_ref[0, :, kwin])
        dqkv_ref[0, :, vwin] = jnp.where(mask, dv.astype(bf16), dqkv_ref[0, :, vwin])
        return carry

    lax.fori_loop(0, heads, one, 0)
    dqkv_ref[0, :, :width] = dqt_ref[...].T.astype(bf16)


def attn_bwd(qkv, grad, mixed, lse, heads, blk=256):
    n, seq, wide = qkv.shape
    width = wide // 6
    spec = lambda j: pl.BlockSpec((1, seq, width), lambda b, h: (b, 0, 3 * h + j))
    out = pl.BlockSpec((1, seq, width), lambda b, h: (b, 0, h))
    return pl.pallas_call(
        partial(attn_bwd_kernel, blk=blk, heads=heads),
        grid=(n, 2),
        in_specs=[
            spec(0), spec(1), spec(2), out, out,
            pl.BlockSpec((1, 1, heads, seq), lambda b, h: (b, h, 0, 0)),
        ],
        out_specs=pl.BlockSpec((1, seq, 3 * width), lambda b, h: (b, 0, h)),
        out_shape=jax.ShapeDtypeStruct(qkv.shape, bf16),
        scratch_shapes=[
            pltpu.VMEM((width, seq), f32),
            pltpu.VMEM((heads, seq), f32),
            pltpu.VMEM((seq, seq), bf16),
            pltpu.VMEM((seq, seq), bf16),
        ],
        compiler_params=pltpu.CompilerParams(vmem_limit_bytes=56 << 20),
        cost_estimate=pl.CostEstimate(flops=0, bytes_accessed=0, transcendentals=0),
        name="attention_backward",
    )(qkv, qkv, qkv, grad, mixed, lse)


def gelu_with_slope(u):
    k, cubic = 0.7978845608028654, 0.7978845608028654 * 0.044715
    square = u * u
    half = 0.5 + 0.5 * jnp.tanh(u * (k + cubic * square))
    value = u * half
    return value, half + value * (1.0 - half) * (2.0 * k + 6.0 * cubic * square)


def tile_steps(rows, cols, sub_rows, sub_cols):
    return [
        (slice(i, i + sub_rows), slice(j, j + sub_cols))
        for j in range(0, cols, sub_cols)
        for i in range(0, rows, sub_rows)
    ]


def up_forward_kernel(x_ref, w_ref, b_ref, act_ref, slope_ref):
    steps = tile_steps(*act_ref.shape, 256, 256)
    product = lambda r, c: jnp.dot(x_ref[r, :], w_ref[:, c], preferred_element_type=f32)
    now = product(*steps[0])
    for n, (r, c) in enumerate(steps):
        later = product(*steps[n + 1]) if n + 1 < len(steps) else None
        value, slope = gelu_with_slope(now + b_ref[:, c])
        act_ref[r, c] = value.astype(bf16)
        slope_ref[r, c] = slope.astype(bf16)
        now = later


def up_forward(x, w, bias):
    count, seq, depth = x.shape
    hidden = bias.shape[0]
    rows, cols = 1024, hidden // 3
    tile = pl.BlockSpec((rows, cols), lambda j, i: (i, j))
    act, slope = pl.pallas_call(
        up_forward_kernel,
        grid=(hidden // cols, count * seq // rows),
        in_specs=[
            pl.BlockSpec((rows, depth), lambda j, i: (i, 0)),
            pl.BlockSpec((depth, cols), lambda j, i: (0, j)),
            pl.BlockSpec((1, cols), lambda j, i: (0, j)),
        ],
        out_specs=[tile, tile],
        out_shape=[jax.ShapeDtypeStruct((count * seq, hidden), bf16)] * 2,
        compiler_params=pltpu.CompilerParams(vmem_limit_bytes=56 << 20),
        cost_estimate=pl.CostEstimate(
            flops=2 * count * seq * depth * hidden,
            bytes_accessed=4 * count * seq * hidden,
            transcendentals=count * seq * hidden,
        ),
        name="up_forward",
    )(x.reshape(count * seq, depth), w, bias.reshape(1, hidden))
    return act.reshape(count, seq, hidden), slope.reshape(count, seq, hidden)


def down_backward_kernel(g_ref, w_ref, slope_ref, out_ref, sum_ref):
    steps = tile_steps(*out_ref.shape, out_ref.shape[0], 256)
    product = lambda r, c: jnp.dot(g_ref[r, :], w_ref[:, c], preferred_element_type=f32)

    @pl.when(pl.program_id(1) == 0)
    def _():
        sum_ref[...] = jnp.zeros_like(sum_ref)

    now = product(*steps[0])
    for n, (r, c) in enumerate(steps):
        later = product(*steps[n + 1]) if n + 1 < len(steps) else None
        grad = (now * slope_ref[r, c].astype(f32)).astype(bf16)
        out_ref[r, c] = grad
        sum_ref[:, c] += jnp.sum(grad.astype(f32), axis=0, keepdims=True)
        now = later


def down_backward(g, w, slope):
    count, seq, depth = g.shape
    hidden = slope.shape[2]
    rows, cols = 1024, hidden // 3
    ahead = hidden // cols
    tile = pl.BlockSpec((rows, cols), lambda j, i: (i, j))
    grad, total = pl.pallas_call(
        down_backward_kernel,
        grid=(hidden // cols, count * seq // rows),
        in_specs=[
            pl.BlockSpec((rows, depth), lambda j, i: (i, 0)),
            pl.BlockSpec((depth, cols), lambda j, i: (0, ahead + j)),
            tile,
        ],
        out_specs=[tile, pl.BlockSpec((1, cols), lambda j, i: (0, j))],
        out_shape=[
            jax.ShapeDtypeStruct((count * seq, hidden), bf16),
            jax.ShapeDtypeStruct((1, hidden), f32),
        ],
        compiler_params=pltpu.CompilerParams(vmem_limit_bytes=56 << 20),
        cost_estimate=pl.CostEstimate(
            flops=2 * count * seq * depth * hidden,
            bytes_accessed=4 * count * seq * hidden,
            transcendentals=0,
        ),
        name="down_backward",
    )(g.reshape(count * seq, depth), w, slope.reshape(count * seq, hidden))
    return grad.reshape(count, seq, hidden), total[0]


CORES = 2
ROWS = 2


def place(rank):
    return rank // (ROWS * CORES), rank // CORES % ROWS, rank % CORES


def rank_of(z, y, core):
    return (z * ROWS + y) * CORES + core


def greet(side):
    rank = lax.axis_index("dp")
    groups = lax.axis_size("dp")
    barrier = pltpu.get_barrier_semaphore()
    for step in range(1, groups):
        pl.semaphore_signal(barrier, inc=1, device_id={"dp": lax.rem(rank + step, groups)}, device_id_type=MESH)
    pl.semaphore_signal(barrier, inc=1, device_id={"tensor": 1 - side}, device_id_type=MESH)
    pl.semaphore_wait(barrier, groups)


class Spread:
    def __init__(self, source, out, sends, arrivals, lanes=None):
        self.source, self.out, self.sends, self.arrivals = source, out, sends, arrivals
        self.lanes = lanes
        self.rank = lax.axis_index("dp")
        self.z, self.y, self.core = place(self.rank)
        self.depth = lax.axis_size("dp") // (ROWS * CORES)
        self.started = []

    def block(self, origin):
        return self.out.at[origin] if self.lanes is None else self.out.at[origin, :, self.lanes]

    def copy(self, origin, edge, target, source=None):
        return pltpu.make_async_remote_copy(
            src_ref=self.block(origin) if source is None else source,
            dst_ref=self.block(origin),
            send_sem=self.sends.at[origin, edge],
            recv_sem=self.arrivals.at[origin],
            device_id={"dp": target},
            device_id_type=MESH,
        )

    def send(self, origin, edge, target, source=None, when=None):
        sent = self.copy(origin, edge, target, source)
        if when is None:
            sent.start()
        else:
            pl.when(when)(sent.start)
        self.started.append((sent, when))

    def arrive(self, origin):
        self.copy(origin, 0, rank_of(self.z, 1 - self.y, self.core)).wait_recv()

    def up(self):
        return rank_of(self.z + 1, self.y, self.core)

    def down(self):
        return rank_of(self.z - 1, self.y, self.core)

    def across(self):
        return rank_of(self.z, 1 - self.y, self.core)

    def sibling(self):
        return rank_of(self.z, self.y, 1 - self.core)

    def begin(self):
        rank, source = self.rank, self.source
        self.send(rank, 0, self.up(), source, self.z < self.depth - 1)
        self.send(rank, 3, self.down(), source, self.z > 0)
        self.send(rank, 1, self.across(), source)
        self.send(rank, 2, self.sibling(), source)

    def relay(self, hop):
        for toward, there in ((1, self.z >= hop), (-1, self.z + hop < self.depth)):
            origin = rank_of(self.z - toward * hop, self.y, self.core)
            further = (self.z < self.depth - 1) if toward > 0 else (self.z > 0)
            pl.when(there)(lambda: self.arrive(origin))
            self.send(
                origin, 0, self.up() if toward > 0 else self.down(), when=there & further
            )
            self.send(origin, 1, self.across(), when=there)
            self.send(origin, 2, self.sibling(), when=there)

    def relay_across(self, hop):
        for toward, there in ((1, self.z >= hop), (-1, self.z + hop < self.depth)):
            if hop == 0 and toward < 0:
                continue
            origin = rank_of(self.z - toward * hop, 1 - self.y, self.core)
            pl.when(there)(lambda: self.arrive(origin))
            self.send(origin, 2, self.sibling(), when=there)

    def finish(self):
        for z in range(self.depth):
            for y in range(ROWS):
                self.arrive(rank_of(z, y, 1 - self.core))
        for sent, when in self.started:
            if when is None:
                sent.wait_send()
            else:
                pl.when(when)(sent.wait_send)


class DirectSpread:
    def __init__(self, out, sends, arrivals):
        self.out, self.sends, self.arrivals = out, sends, arrivals
        self.rank = lax.axis_index("dp")
        self.groups = lax.axis_size("dp")
        self.sibling = self.rank + 1 - 2 * lax.rem(self.rank, CORES)
        self.steps = range(CORES, self.groups, CORES)

    def copy(self, origin, send, target):
        return pltpu.make_async_remote_copy(
            src_ref=self.out.at[origin],
            dst_ref=self.out.at[origin],
            send_sem=self.sends.at[send],
            recv_sem=self.arrivals.at[origin],
            device_id={"dp": target},
            device_id_type=MESH,
        )

    def peer(self, step):
        return lax.rem(self.rank + step, self.groups)

    def begin(self):
        for step in self.steps:
            self.copy(self.rank, step, self.peer(step)).start()
        self.copy(self.rank, 0, self.sibling).start()

    def relay(self):
        for step in self.steps:
            origin = self.peer(step)
            self.copy(origin, step, origin).wait_recv()
            self.copy(origin, step + 1, self.sibling).start()

    def finish(self):
        for step in range(0, self.groups, CORES):
            origin = lax.rem(self.sibling + step, self.groups)
            self.copy(origin, 0, self.sibling).wait_recv()
        for step in self.steps:
            self.copy(self.rank, step, self.peer(step)).wait_send()
            self.copy(self.peer(step), step + 1, self.sibling).wait_send()
        self.copy(self.rank, 0, self.sibling).wait_send()


class Exchange:
    def __init__(self, source, out, sends, arrivals):
        self.source, self.out, self.sends, self.arrivals = source, out, sends, arrivals
        self.rank = lax.axis_index("dp")
        self.groups = lax.axis_size("dp")

    def copy(self, step):
        peer = lax.rem(self.rank + step, self.groups)
        return pltpu.make_async_remote_copy(
            src_ref=self.source.at[peer],
            dst_ref=self.out.at[self.rank],
            send_sem=self.sends.at[step],
            recv_sem=self.arrivals.at[self.rank],
            device_id={"dp": peer},
            device_id_type=MESH,
        )

    def begin(self):
        self.out[self.rank] = self.source[self.rank]
        for step in range(1, self.groups):
            self.copy(step).start()

    def finish(self):
        for step in range(1, self.groups):
            peer = lax.rem(self.rank + step, self.groups)
            pltpu.make_async_remote_copy(
                src_ref=self.source.at[peer],
                dst_ref=self.out.at[peer],
                send_sem=self.sends.at[step],
                recv_sem=self.arrivals.at[peer],
                device_id={"dp": peer},
                device_id_type=MESH,
            ).wait_recv()

    def drain(self):
        for step in range(1, self.groups):
            self.copy(step).wait_send()


def to_partner(source, target, side, sends, arrivals, k):
    return pltpu.make_async_remote_copy(
        src_ref=source,
        dst_ref=target,
        send_sem=sends.at[k],
        recv_sem=arrivals.at[k],
        device_id={"tensor": 1 - side},
        device_id_type=MESH,
    )


def opening_kernel(
    cond_ref, mod_w_ref, mod_bias_ref, bias_ref, head_ref, rest_ref, latent_ref,
    head_out, rest_out, latent_out, mod_out, cond_out, bias_out,
    part_ref, mod_in,
    x_send, x_recv, c_send, c_recv, m_send, m_recv, h_send, h_recv, local_sem,
):
    side = lax.axis_index("tensor")
    rank = lax.axis_index("dp")
    own = latent_out.shape[0]
    greet(side)
    conds = Exchange(cond_ref, cond_out, c_send, c_recv)
    conds.begin()
    lanes = head_ref.shape[1]
    mine = Spread(head_ref, head_out, h_send.at[0], h_recv.at[0], pl.ds(0, lanes))
    other = Spread(None, head_out, h_send.at[1], h_recv.at[1], pl.ds(lanes, lanes))
    head_swap = to_partner(head_ref, other.block(rank), side, x_send, x_recv, 0)
    head_swap.start()
    mine.begin()
    biases = to_partner(bias_ref, bias_out, side, x_send, x_recv, 4)
    biases.start()
    latents = to_partner(
        latent_ref.at[pl.ds((1 - side) * own, own)], latent_out, side, x_send, x_recv, 1
    )
    latents.start()
    rest = to_partner(rest_ref, rest_out, side, x_send, x_recv, 3)
    rest.start()
    keep = pltpu.make_async_copy(head_ref, mine.block(rank), local_sem)
    keep.start()
    conds.finish()
    groups, rows, lanes = cond_out.shape
    half = mod_bias_ref.shape[1]
    low = cond_out[...].reshape(groups * rows, lanes).astype(bf16)
    front = lax.broadcasted_iota(jnp.int32, (groups * rows, half), 0) % rows < rows // 2
    part_ref[...] = jnp.where(
        front,
        jnp.dot(low, mod_w_ref[0], preferred_element_type=f32),
        jnp.dot(low, mod_w_ref[1], preferred_element_type=f32),
    ).reshape(groups, rows, half)
    mods = Exchange(part_ref, mod_in, m_send, m_recv)
    mods.begin()
    head_swap.wait_recv()
    other.begin()
    mine.relay(1)
    mods.finish()
    mod_out[0] = jnp.sum(mod_in[...], axis=0) + mod_bias_ref[...]
    mod_swap = to_partner(mod_out.at[0], mod_out.at[1], side, x_send, x_recv, 2)
    mod_swap.start()
    other.relay(1)
    mine.relay_across(0)
    other.relay_across(0)
    depth = mine.depth
    for hop in range(2, depth):
        for s in (mine, other):
            s.relay(hop)
            s.relay_across(hop - 1)
    for s in (mine, other):
        s.relay_across(depth - 1)
    keep.wait()
    mine.finish()
    other.finish()
    mod_swap.wait()
    latents.wait()
    rest.wait()
    biases.wait()
    head_swap.wait_send()
    conds.drain()
    mods.drain()


def opening(cond_low, mod_weight, mod_bias, biases, head, rest, latent):
    groups = lax.axis_size("dp")
    count, half_seq, width = latent.shape
    depth = cond_low.shape[1] // groups
    half = mod_weight.shape[1] * mod_weight.shape[2] // 2
    blocks = cond_low.astype(f32).reshape(count, groups, depth).transpose(1, 0, 2)
    blocks = jnp.concatenate([blocks, blocks], axis=1)
    blocks = jnp.pad(blocks, ((0, 0), (0, 0), (0, 128 - depth)))
    weights = jnp.pad(mod_weight.reshape(depth, 2, half), ((0, 128 - depth), (0, 0), (0, 0))).transpose(1, 0, 2)
    bias = jnp.repeat(mod_bias.astype(f32).reshape(2, half), count, axis=0)
    dma = pltpu.SemaphoreType.DMA
    vmem = pl.BlockSpec(memory_space=pltpu.VMEM)
    anywhere = pl.BlockSpec(memory_space=pl.ANY)
    return pl.pallas_call(
        opening_kernel,
        in_specs=[vmem, vmem, vmem, vmem, anywhere, anywhere, anywhere],
        out_specs=[anywhere, anywhere, anywhere, vmem, vmem, vmem],
        out_shape=[
            jax.ShapeDtypeStruct((groups, depth, 2 * head.shape[1]), bf16),
            jax.ShapeDtypeStruct(rest.shape, bf16),
            jax.ShapeDtypeStruct((count // 2, half_seq, width), bf16),
            jax.ShapeDtypeStruct((2, 2 * count, half), f32),
            jax.ShapeDtypeStruct(blocks.shape, f32),
            jax.ShapeDtypeStruct(biases.shape, f32),
        ],
        scratch_shapes=[
            pltpu.VMEM((groups, 2 * count, half), f32),
            pltpu.VMEM((groups, 2 * count, half), f32),
            dma((5,)), dma((5,)),
            dma((groups,)), dma((groups,)),
            dma((groups,)), dma((groups,)),
            dma((2, groups, 4)), dma((2, groups)),
            dma,
        ],
        compiler_params=pltpu.CompilerParams(collective_id=0, has_side_effects=True, vmem_limit_bytes=32 << 20),
        name="opening",
    )(blocks, weights, bias, biases, head, rest, latent)


def closing_kernel(
    mod_ref, bias_ref, mod_w_ref,
    mod_out, bias_out, cond_out,
    mod_unit, bias_unit, bias_in, part_ref, cond_in,
    x_send, x_recv, m_send, m_recv, b_send, b_recv, c_send, c_recv,
):
    side = lax.axis_index("tensor")
    rank = lax.axis_index("dp")
    greet(side)
    rows = mod_ref.shape[1]
    mod_swap = to_partner(mod_ref.at[1], mod_unit.at[1], side, x_send, x_recv, 0)
    mod_swap.start()
    bias_swap = to_partner(bias_ref.at[1], bias_unit.at[1], side, x_send, x_recv, 1)
    bias_swap.start()
    mod_swap.wait()
    bias_swap.wait()
    mod_out[rank] = mod_ref[0] + mod_unit[1]
    bias_in[rank] = bias_ref[0] + bias_unit[1]
    mods = DirectSpread(mod_out, m_send, m_recv)
    biases = DirectSpread(bias_in, b_send, b_recv)
    mods.begin()
    biases.begin()
    mods.relay()
    biases.relay()
    mods.finish()
    groups, rows, half = mod_out.shape
    low = mod_out[...].reshape(groups * rows, half).astype(bf16)
    lanes = mod_w_ref.shape[1]
    front = lax.broadcasted_iota(jnp.int32, (groups * rows, lanes), 0) % rows < rows // 2
    part_ref[...] = jnp.where(
        front,
        lax.dot_general(low, mod_w_ref[0], NT, preferred_element_type=f32),
        lax.dot_general(low, mod_w_ref[1], NT, preferred_element_type=f32),
    ).reshape(groups, rows, lanes)
    conds = Exchange(part_ref, cond_in, c_send, c_recv)
    conds.begin()
    biases.finish()
    bias_out[...] = jnp.sum(bias_in[...], axis=0)
    conds.finish()
    cond_out[0] = cond_in[...]
    cond_swap = to_partner(cond_out.at[0], cond_out.at[1], side, x_send, x_recv, 2)
    cond_swap.start()
    cond_swap.wait()
    conds.drain()


def closing(mod_pair, bias_pair, mod_weight):
    groups = lax.axis_size("dp")
    rows, half = mod_pair.shape[1:]
    depth = mod_weight.shape[0]
    weights = jnp.pad(mod_weight.reshape(depth, 2, half), ((0, 128 - depth), (0, 0), (0, 0))).transpose(1, 0, 2)
    dma = pltpu.SemaphoreType.DMA
    vmem = pl.BlockSpec(memory_space=pltpu.VMEM)
    lines = bias_pair.shape[1]
    return pl.pallas_call(
        closing_kernel,
        in_specs=[vmem, vmem, vmem],
        out_specs=[vmem, vmem, vmem],
        out_shape=[
            jax.ShapeDtypeStruct((groups, rows, half), f32),
            jax.ShapeDtypeStruct((lines, 128), f32),
            jax.ShapeDtypeStruct((2, groups, rows, 128), f32),
        ],
        scratch_shapes=[
            pltpu.VMEM((2, rows, half), f32),
            pltpu.VMEM((2, lines, 128), f32),
            pltpu.VMEM((groups, lines, 128), f32),
            pltpu.VMEM((groups, rows, 128), f32),
            pltpu.VMEM((groups, rows, 128), f32),
            dma((3,)), dma((3,)),
            dma((groups,)), dma((groups,)),
            dma((groups,)), dma((groups,)),
            dma((groups,)), dma((groups,)),
        ],
        compiler_params=pltpu.CompilerParams(collective_id=1, has_side_effects=True, vmem_limit_bytes=32 << 20),
        cost_estimate=pl.CostEstimate(flops=0, bytes_accessed=0, transcendentals=0),
        name="closing",
    )(mod_pair, bias_pair, weights)


def normed(values):
    centred = values - jnp.mean(values, axis=-1, keepdims=True)
    variance = jnp.mean(centred * centred, axis=-1, keepdims=True)
    inverse = lax.rsqrt(variance + EPSILON)
    return centred * inverse, inverse


def normed_back(grad, norm, inverse):
    return inverse * (
        grad
        - jnp.mean(grad, axis=-1, keepdims=True)
        - norm * jnp.mean(grad * norm, axis=-1, keepdims=True)
    )


def mm(spec, a, b):
    return jnp.einsum(spec, a, b, preferred_element_type=f32)


def body_by_latents(
    latent,
    condition,
    cotangent,
    mod_weight,
    mod_bias,
    head_weight,
    head_bias,
    mix_weight,
    branch_bias,
    up_weight,
    up_bias,
    down_weight,
):
    side = lax.axis_index("tensor")
    rank = lax.axis_index("dp")
    groups = lax.axis_size("dp")
    count, half_seq, width = latent.shape
    own = count // 2
    cols = width // 2
    depth = head_weight.shape[0]
    hidden = 2 * up_weight.shape[1]

    def swap(a):
        return lax.ppermute(a, "tensor", [(0, 1), (1, 0)])

    def in_order(mine, other, axis):
        return jnp.where(
            side == 0,
            jnp.concatenate([mine, other], axis=axis),
            jnp.concatenate([other, mine], axis=axis),
        )

    def own_latents(a, axis=0):
        return lax.dynamic_slice_in_dim(a, side * own, own, axis)

    def other_latents(a, axis=0):
        return lax.dynamic_slice_in_dim(a, (1 - side) * own, own, axis)

    def placed(a, arrived):
        mine = lax.broadcasted_iota(jnp.int32, (2, 1, 1, 1), 0) == side
        whole = jnp.where(mine, a[None, :, :half_seq], arrived[None])
        return whole.reshape(count, half_seq, width)

    cond_f = condition.astype(f32)
    cond_low = jax.nn.silu(cond_f).astype(bf16)
    heads = cols // HEAD_DIM
    room = -(-cols // 128) * 128

    def roomy(a):
        return jnp.pad(a, [(0, 0)] * (a.ndim - 1) + [(0, room - cols)])

    head_shard = roomy(head_weight).reshape(depth, 3 * room)
    shards = jnp.concatenate([up_weight, down_weight.T, roomy(mix_weight.T)], axis=1)
    branch = branch_bias.astype(f32)
    flat = [a.astype(f32).reshape(-1) for a in (head_bias, branch, up_bias)]
    head_all, shards_in, latent_in, mod_parts, cond_blocks, biases_in = opening(
        cond_low,
        mod_weight,
        mod_bias,
        jnp.concatenate(flat).reshape(-1, 128),
        head_shard,
        shards,
        latent,
    )
    biases_in = biases_in.reshape(-1)
    head_bias_in = biases_in[: 2 * cols].reshape(2, cols)
    branch_in = biases_in[2 * cols : 4 * cols].reshape(2, cols)
    head_all = head_all.reshape(width, 6 * room)
    mod_parts = mod_parts.reshape(2, 2, count, 3, cols)
    mod_parts = own_latents(mod_parts, 2).transpose(0, 2, 1, 3, 4).reshape(2, own, 6, cols)
    modulation = in_order(mod_parts[0], mod_parts[1], 2)
    cond_cols = cond_blocks[:, :count, :depth].reshape(groups * count, depth).astype(bf16)
    branch_all = in_order(branch, branch_in, 1)
    row = lambda k: modulation[:, k][:, None, :]
    shift_a, scale_a, gate_a, shift_m, scale_m, gate_m = [row(k) for k in range(6)]

    cuts = (0, hidden // 2, hidden, hidden + room)
    pieces = [a[:, lo:hi] for lo, hi in zip(cuts, cuts[1:]) for a in (shards, shards_in)]
    rest_all = lax.all_gather(jnp.concatenate(pieces, axis=1), "dp", axis=0, tiled=True)
    up_all = rest_all[:, :hidden]
    down_t = rest_all[:, hidden : 2 * hidden]
    mix_t = rest_all[:, 2 * hidden :]
    up_bias_f = jnp.concatenate([flat[2], biases_in[4 * cols :]])

    lat = jnp.concatenate([own_latents(latent), latent_in], axis=1)
    lat_f = lat.astype(f32)
    norm1, inv1 = normed(lat_f)
    attn_in = (norm1 * (1.0 + scale_a) + shift_a).astype(bf16)
    empty = jnp.zeros((room,), f32)
    qkv_bias = jnp.concatenate(
        [c for b in (roomy(head_bias.astype(f32)), roomy(head_bias_in)) for c in (b[0], empty, b[1])]
    )
    qkv = (mm("bsd,dc->bsc", attn_in, head_all) + qkv_bias).astype(bf16)
    later, qkv = lax.optimization_barrier((other_latents(cotangent), qkv))
    upstream_low = jnp.concatenate([own_latents(cotangent), swap(later)], axis=1)
    mixed, logsum = attn_fwd(qkv, heads)
    attn_out = mm("bsc,dc->bsd", mixed, mix_t) + branch_all[0]
    first = lat_f + gate_a * attn_out
    norm2, inv2 = normed(first)
    mlp_in = (norm2 * (1.0 + scale_m) + shift_m).astype(bf16)
    act, slope = up_forward(mlp_in, rest_all, up_bias_f)
    mlp_out = mm("bsf,df->bsd", act, down_t) + branch_all[1]
    block = (first + gate_m * mlp_out).astype(bf16)
    block_in = swap(block[:, half_seq:])

    upstream = upstream_low.astype(f32)
    gate_m_grad = jnp.sum(upstream * mlp_out, axis=1)
    tail_bias_grad = jnp.sum(gate_m[:, 0] * jnp.sum(upstream, axis=1), axis=0)
    mlp_grad = (gate_m * upstream).astype(bf16)
    down_grad = mm("bsd,bsf->df", mlp_grad, act).astype(bf16)
    down_grad, mlp_grad = lax.optimization_barrier((down_grad, mlp_grad))
    down_sum = lax.psum_scatter(down_grad, "dp", scatter_dimension=0, tiled=True)
    pre_grad, up_bias_term = down_backward(mlp_grad, rest_all, slope)
    up_grad = mm("bsd,bsf->df", mlp_in, pre_grad).astype(bf16)
    up_grad, pre_grad = lax.optimization_barrier((up_grad, pre_grad))
    mlp_in_grad = mm("bsf,df->bsd", pre_grad, up_all)
    shift_m_grad = jnp.sum(mlp_in_grad, axis=1)
    scale_m_grad = jnp.sum(mlp_in_grad * norm2, axis=1)
    first_grad = upstream + normed_back(mlp_in_grad * (1.0 + scale_m), norm2, inv2)
    gate_a_grad = jnp.sum(first_grad * attn_out, axis=1)
    attn_bias_grad = jnp.sum(gate_a[:, 0] * jnp.sum(first_grad, axis=1), axis=0)
    attn_grad = (gate_a * first_grad).astype(bf16)
    mixed_grad = mm("bsd,dc->bsc", attn_grad, mix_t).astype(bf16)
    mix_grad = mm("bsd,bsc->dc", attn_grad, mixed).astype(bf16)
    up_grad = jnp.concatenate([up_grad, mix_grad], axis=1)
    up_grad, mixed_grad = lax.optimization_barrier((up_grad, mixed_grad))
    up_sum = lax.psum_scatter(up_grad, "dp", scatter_dimension=0, tiled=True)
    mixed_grad, down_sum = lax.optimization_barrier((mixed_grad, down_sum))
    qkv_grad = attn_bwd(qkv, mixed_grad, mixed, logsum, heads)
    head_grad = mm("bsd,bsc->dc", attn_in, qkv_grad).astype(bf16)
    head_grad, qkv_grad = lax.optimization_barrier((head_grad, qkv_grad))
    head_sum = lax.psum_scatter(head_grad, "dp", scatter_dimension=0, tiled=True)
    qkv_grad, up_sum, block_in = lax.optimization_barrier((qkv_grad, up_sum, block_in))
    block_out = placed(block, block_in)
    qkv_bias_term = jnp.sum(qkv_grad, axis=(0, 1), dtype=f32)
    attn_in_grad = mm("bsc,dc->bsd", qkv_grad, head_all)
    shift_a_grad = jnp.sum(attn_in_grad, axis=1)
    scale_a_grad = jnp.sum(attn_in_grad * norm1, axis=1)
    lat_grad = first_grad + normed_back(attn_in_grad * (1.0 + scale_a), norm1, inv1)
    lat_grad = lat_grad.astype(bf16)
    lat_grad_in = swap(lat_grad[:, half_seq:])

    mod_low = jnp.stack(
        [shift_a_grad, scale_a_grad, gate_a_grad, shift_m_grad, scale_m_grad, gate_m_grad], axis=1
    ).astype(bf16)
    branch_term = jnp.stack([attn_bias_grad, tail_bias_grad])
    head_term = qkv_bias_term.reshape(2, 3, room)[:, 0::2, :cols]
    ups = up_bias_term.reshape(2, hidden // 2)

    def mod_share(owner):
        mine = lax.dynamic_slice_in_dim(mod_low.astype(f32), owner * cols, cols, 2)
        mine = mine.reshape(own, 2, 3 * cols).transpose(1, 0, 2)
        empty = jnp.zeros((2, count, 3 * cols), f32)
        return lax.dynamic_update_slice_in_dim(empty, mine, side * own, 1).reshape(2 * count, 3 * cols)

    def bias_share(owner, k):
        branch_cols = lax.dynamic_slice_in_dim(branch_term, owner * cols, cols, 1)
        flat = jnp.concatenate([head_term[k].reshape(-1), branch_cols.reshape(-1), ups[k]])
        return flat.reshape(-1, 128)

    mod_pair = jnp.stack([mod_share(side), mod_share(1 - side)])
    mod_pair, lat_grad = lax.optimization_barrier((mod_pair, lat_grad))
    mod_blocks, biases, cond_parts = closing(
        mod_pair,
        jnp.stack([bias_share(side, 0), bias_share(1 - side, 1)]),
        mod_weight,
    )
    latent_grad = placed(lat_grad, lat_grad_in)
    biases = biases.reshape(-1)
    mod_rows = mod_blocks.astype(bf16).reshape(groups, 2, count, 3, cols)
    mod_rows = mod_rows.transpose(0, 2, 1, 3, 4).reshape(groups * count, 6, cols)
    mod_weight_grad = mm("bd,bkc->dkc", cond_cols, mod_rows)
    mod_bias_grad = jnp.sum(mod_rows, axis=0, dtype=f32)
    cond_act = jnp.sum(cond_parts[..., :depth].reshape(2, groups, 2, count, depth), axis=(0, 2))
    cond_act = cond_act.transpose(1, 0, 2).reshape(count, groups * depth)
    gate = jax.nn.sigmoid(cond_f)
    condition_grad = cond_act * (gate * (1.0 + cond_f * (1.0 - gate)))

    def joined(summed, axis):
        mine, other = jnp.split(summed, 2, axis=axis)
        return mine.astype(f32) + swap(other).astype(f32)

    head_weight_grad = joined(head_sum, 1).reshape(depth, 3, room)[..., :cols]
    mix_weight_grad = joined(up_sum[:, hidden:], 1)[:, :cols].T
    up_weight_grad = joined(up_sum[:, :hidden], 1)
    down_weight_grad = joined(down_sum, 1).T
    return (
        block_out,
        latent_grad,
        condition_grad,
        mod_weight_grad,
        mod_bias_grad,
        head_weight_grad,
        biases[: 2 * cols].reshape(2, cols),
        mix_weight_grad,
        biases[2 * cols : 4 * cols].reshape(2, cols),
        up_weight_grad,
        biases[4 * cols :],
        down_weight_grad,
    )


def solution(mesh):
    placed = (
        P("dp", "tensor", None),
        P("dp", None),
        P("dp", "tensor", None),
        P("dp", None, "tensor"),
        P(None, "tensor"),
        P("dp", None, "tensor"),
        P(None, "tensor"),
        P("tensor", "dp"),
        P(None, "tensor"),
        P("dp", "tensor"),
        P("tensor"),
        P("tensor", "dp"),
    )
    whole_latents = dict(mesh.shape) == {"dp": 16, "tensor": 2}
    return jax.shard_map(
        body_by_latents if whole_latents else body_by_heads,
        mesh=mesh,
        in_specs=placed,
        out_specs=(
            P("dp", "tensor", None),
            P("dp", "tensor", None),
            P("dp", None),
            P("dp", None, "tensor"),
            P(None, "tensor"),
            P("dp", None, "tensor"),
            P(None, "tensor"),
            P("tensor", "dp"),
            P(None, "tensor"),
            P("dp", "tensor"),
            P("tensor"),
            P("tensor", "dp"),
        ),
        check_vma=False,
    )
```

```python
from functools import partial

import jax
import jax.numpy as jnp
from jax import lax
from jax.experimental import pallas as pl
from jax.experimental.pallas import tpu as pltpu
from jax.sharding import PartitionSpec as P

SEQ = 1024
HEAD_DIM = 72
MICRO = 4
LOG2E = 1.4426950408889634
WINDOW = 256
f32 = jnp.float32
bf16 = jnp.bfloat16
NT = (((1,), (1,)), ((), ()))
MESH = pl.DeviceIdType.MESH


EPSILON = 1e-06


def layer_norm(values):
    centred = values - jnp.mean(values, axis=-1, keepdims=True)
    variance = jnp.mean(centred * centred, axis=-1, keepdims=True)
    return centred * lax.rsqrt(variance + EPSILON)


def modulate(values, shift, scale):
    return layer_norm(values) * (1.0 + scale[:, None, :]) + shift[:, None, :]


def gelu_tanh(values):
    return jax.nn.gelu(values, approximate=True)


def fetch_weights(mod_weight, head_weight, mix_weight, up_weight, down_weight):
    return (
        lax.all_gather(mod_weight, "dp", axis=0, tiled=True),
        lax.all_gather(head_weight, "dp", axis=0, tiled=True),
        lax.all_gather(mix_weight, "dp", axis=1, tiled=True),
        lax.all_gather(up_weight, "dp", axis=0, tiled=True),
        lax.all_gather(down_weight, "dp", axis=1, tiled=True),
    )


def reduce_weights(grads):
    return (
        lax.psum_scatter(
            grads[0].astype(jnp.bfloat16), "dp", scatter_dimension=0, tiled=True
        ).astype(jnp.float32),
        lax.psum_scatter(
            grads[1].astype(jnp.bfloat16), "dp", scatter_dimension=0, tiled=True
        ).astype(jnp.float32),
        lax.psum_scatter(
            grads[2].astype(jnp.bfloat16), "dp", scatter_dimension=1, tiled=True
        ).astype(jnp.float32),
        lax.psum_scatter(
            grads[3].astype(jnp.bfloat16), "dp", scatter_dimension=0, tiled=True
        ).astype(jnp.float32),
        lax.psum_scatter(
            grads[4].astype(jnp.bfloat16), "dp", scatter_dimension=1, tiled=True
        ).astype(jnp.float32),
    )


def attend_forward(queries, keys, values, block_rows, scale_factor):
    seq_len = queries.shape[0]
    blocked = queries.reshape(seq_len // block_rows, block_rows, queries.shape[1], queries.shape[2])

    def one_block(query_block):
        scores = (
            jnp.einsum("qhd,khd->hqk", query_block, keys, preferred_element_type=jnp.float32)
            * scale_factor
        )
        peak = jnp.max(scores, axis=-1, keepdims=True)
        raised = jnp.exp(scores - peak)
        total = jnp.sum(raised, axis=-1, keepdims=True)
        weights = (raised / total).astype(jnp.bfloat16)
        mixed = jnp.einsum("hqk,khd->qhd", weights, values, preferred_element_type=jnp.float32)
        return (mixed, (peak + jnp.log(total))[..., 0])

    mixed, logsum = lax.map(one_block, blocked)
    return (mixed.reshape(queries.shape), logsum)


def attend_backward(queries, keys, values, grad_mixed, logsum, block_rows, scale_factor):
    seq_len = queries.shape[0]
    block_shape = (seq_len // block_rows, block_rows, queries.shape[1], queries.shape[2])

    def one_block(carried, pieces):
        key_sum, value_sum = carried
        query_block, grad_block, logsum_block = pieces
        scores = (
            jnp.einsum("qhd,khd->hqk", query_block, keys, preferred_element_type=jnp.float32)
            * scale_factor
        )
        probs = jnp.exp(scores - logsum_block[..., None])
        prob_grad = jnp.einsum(
            "qhd,khd->hqk", grad_block, values, preferred_element_type=jnp.float32
        )
        inner = jnp.sum(probs * prob_grad, axis=-1, keepdims=True)
        score_grad = (probs * (prob_grad - inner)).astype(jnp.bfloat16)
        query_grad = (
            jnp.einsum("hqk,khd->qhd", score_grad, keys, preferred_element_type=jnp.float32)
            * scale_factor
        )
        key_sum = (
            key_sum
            + jnp.einsum(
                "hqk,qhd->khd", score_grad, query_block, preferred_element_type=jnp.float32
            )
            * scale_factor
        )
        value_sum = value_sum + jnp.einsum(
            "hqk,qhd->khd",
            probs.astype(jnp.bfloat16),
            grad_block,
            preferred_element_type=jnp.float32,
        )
        return ((key_sum, value_sum), query_grad)

    empty = jnp.zeros(keys.shape, jnp.float32)
    (key_grad, value_grad), query_grads = lax.scan(
        one_block,
        (empty, empty),
        (queries.reshape(block_shape), grad_mixed.reshape(block_shape), logsum),
    )
    return (query_grads.reshape(queries.shape), key_grad, value_grad)


def body_by_heads(
    latent,
    condition,
    cotangent,
    mod_weight,
    mod_bias,
    head_weight,
    head_bias,
    mix_weight,
    branch_bias,
    up_weight,
    up_bias,
    down_weight,
):
    per_group = latent.shape[0] // MICRO
    seq_len = SEQ
    head_cols = head_weight.shape[2]
    local_heads = head_cols // HEAD_DIM
    block_rows = min(512, seq_len)
    scale_factor = HEAD_DIM ** (-0.5)
    attend_fwd = jax.vmap(partial(attend_forward, block_rows=block_rows, scale_factor=scale_factor))
    attend_bwd = jax.vmap(
        partial(attend_backward, block_rows=block_rows, scale_factor=scale_factor)
    )
    head_bias_f = head_bias.astype(jnp.float32)
    up_bias_f = up_bias.astype(jnp.float32)
    mod_bias_f = mod_bias.astype(jnp.float32)
    branch_bias_f = branch_bias.astype(jnp.float32)
    bias_totals = (
        jnp.zeros(mod_bias.shape, jnp.float32),
        jnp.zeros(head_bias.shape, jnp.float32),
        jnp.zeros(up_bias.shape, jnp.float32),
        jnp.zeros(branch_bias.shape, jnp.float32),
    )
    grad_sums = None
    block_outs = []
    latent_grads = []
    condition_grads = []
    for micro_step in range(MICRO):
        row_start = micro_step * per_group
        row_stop = row_start + per_group
        mod_full, head_full, mix_full, up_full, down_full = fetch_weights(
            mod_weight, head_weight, mix_weight, up_weight, down_weight
        )
        lat_part = latent[row_start:row_stop].astype(jnp.float32)
        cond_part = condition[row_start:row_stop].astype(jnp.float32)
        cond_act, silu_back = jax.vjp(jax.nn.silu, cond_part)
        cond_low = cond_act.astype(jnp.bfloat16)
        mod_cols = (
            jnp.einsum("bd,dkc->bkc", cond_low, mod_full, preferred_element_type=jnp.float32)
            + mod_bias_f
        )
        mod_all, bias_all = (
            lax.all_gather(mod_cols, "tensor", axis=2, tiled=True),
            lax.all_gather(branch_bias_f, "tensor", axis=1, tiled=True),
        )
        norm_first, first_back = jax.vjp(modulate, lat_part, mod_all[:, 0], mod_all[:, 1])
        attn_rows = lax.all_gather(norm_first.astype(jnp.bfloat16), "tensor", axis=1, tiled=True)
        projected = jnp.einsum(
            "bsd,dkc->bskc", attn_rows, head_full, preferred_element_type=jnp.float32
        )
        head_shape = (per_group, seq_len, local_heads, HEAD_DIM)
        query_heads = (projected[:, :, 0] + head_bias_f[0]).astype(jnp.bfloat16).reshape(head_shape)
        key_heads = projected[:, :, 1].astype(jnp.bfloat16).reshape(head_shape)
        value_heads = (projected[:, :, 2] + head_bias_f[1]).astype(jnp.bfloat16).reshape(head_shape)
        mixed, logsum = attend_fwd(query_heads, key_heads, value_heads)
        mixed_low = mixed.reshape(per_group, seq_len, head_cols).astype(jnp.bfloat16)
        attn_part = jnp.einsum(
            "bsc,cd->bsd", mixed_low, mix_full, preferred_element_type=jnp.float32
        )
        attn_local = lax.psum_scatter(
            attn_part.astype(jnp.bfloat16), "tensor", scatter_dimension=1, tiled=True
        ).astype(jnp.float32)
        gate_attn = mod_all[:, 2][:, None, :]
        gate_mlp = mod_all[:, 5][:, None, :]
        first = lat_part + gate_attn * (attn_local + bias_all[0])
        norm_second, second_back = jax.vjp(modulate, first, mod_all[:, 3], mod_all[:, 4])
        mlp_rows = lax.all_gather(norm_second.astype(jnp.bfloat16), "tensor", axis=1, tiled=True)
        pre_act = (
            jnp.einsum("bsd,df->bsf", mlp_rows, up_full, preferred_element_type=jnp.float32)
            + up_bias_f
        )
        act_value, gelu_back = jax.vjp(gelu_tanh, pre_act)
        act_low = act_value.astype(jnp.bfloat16)
        mlp_part = jnp.einsum("bsf,fd->bsd", act_low, down_full, preferred_element_type=jnp.float32)
        mlp_local = lax.psum_scatter(
            mlp_part.astype(jnp.bfloat16), "tensor", scatter_dimension=1, tiled=True
        ).astype(jnp.float32)
        block_outs.append((first + gate_mlp * (mlp_local + bias_all[1])).astype(jnp.bfloat16))
        mod_full, head_full, mix_full, up_full, down_full = fetch_weights(
            mod_weight, head_weight, mix_weight, up_weight, down_weight
        )
        upstream = cotangent[row_start:row_stop].astype(jnp.float32)
        gate_m_grad = jnp.sum(upstream * (mlp_local + bias_all[1]), axis=1)
        tail_bias_grad = jnp.sum(gate_mlp * upstream, axis=(0, 1))
        mlp_grad = lax.all_gather(
            (gate_mlp * upstream).astype(jnp.bfloat16), "tensor", axis=1, tiled=True
        )
        down_grad = jnp.einsum("bsf,bsd->fd", act_low, mlp_grad, preferred_element_type=jnp.float32)
        act_grad = jnp.einsum(
            "bsd,fd->bsf", mlp_grad, down_full, preferred_element_type=jnp.float32
        )
        pre_grad = gelu_back(act_grad)[0].astype(jnp.bfloat16)
        up_bias_term = jnp.sum(pre_grad, axis=(0, 1), dtype=jnp.float32)
        up_grad = jnp.einsum("bsd,bsf->df", mlp_rows, pre_grad, preferred_element_type=jnp.float32)
        mlp_in_part = jnp.einsum(
            "bsf,df->bsd", pre_grad, up_full, preferred_element_type=jnp.float32
        )
        mlp_in_grad = lax.psum_scatter(
            mlp_in_part.astype(jnp.bfloat16), "tensor", scatter_dimension=1, tiled=True
        ).astype(jnp.float32)
        first_grad, shift_m_grad, scale_m_grad = second_back(mlp_in_grad)
        first_grad = first_grad + upstream
        gate_a_grad = jnp.sum(first_grad * (attn_local + bias_all[0]), axis=1)
        attn_bias_grad = jnp.sum(gate_attn * first_grad, axis=(0, 1))
        attn_branch_grad = (gate_attn * first_grad).astype(jnp.bfloat16)
        attn_grad = lax.all_gather(attn_branch_grad, "tensor", axis=1, tiled=True)
        mix_grad = jnp.einsum(
            "bsc,bsd->cd", mixed_low, attn_grad, preferred_element_type=jnp.float32
        )
        mixed_grad = jnp.einsum(
            "bsd,cd->bsc", attn_grad, mix_full, preferred_element_type=jnp.float32
        ).astype(jnp.bfloat16)
        query_grad, key_grad, value_grad = attend_bwd(
            query_heads, key_heads, value_heads, mixed_grad.reshape(head_shape), logsum
        )
        head_grads = (
            jnp.stack([query_grad, key_grad, value_grad], axis=2)
            .reshape(per_group, seq_len, 3, head_cols)
            .astype(jnp.bfloat16)
        )
        head_bias_term = jnp.sum(head_grads[:, :, 0::2], axis=(0, 1), dtype=jnp.float32)
        head_grad = jnp.einsum(
            "bsd,bskc->dkc", attn_rows, head_grads, preferred_element_type=jnp.float32
        )
        attn_in_part = jnp.einsum(
            "bskc,dkc->bsd", head_grads, head_full, preferred_element_type=jnp.float32
        )
        attn_in_grad = lax.psum_scatter(
            attn_in_part.astype(jnp.bfloat16), "tensor", scatter_dimension=1, tiled=True
        ).astype(jnp.float32)
        lat_grad, shift_a_grad, scale_a_grad = first_back(attn_in_grad)
        latent_grads.append((lat_grad + first_grad).astype(jnp.bfloat16))
        mod_terms = jnp.stack(
            [shift_a_grad, scale_a_grad, gate_a_grad, shift_m_grad, scale_m_grad, gate_m_grad],
            axis=1,
        )
        branch_terms = jnp.stack([attn_bias_grad, tail_bias_grad], axis=0)
        mod_grad_cols, branch_grad_cols = (
            lax.psum_scatter(
                mod_terms.astype(jnp.bfloat16), "tensor", scatter_dimension=2, tiled=True
            ).astype(jnp.float32),
            lax.psum_scatter(
                branch_terms.astype(jnp.bfloat16), "tensor", scatter_dimension=1, tiled=True
            ).astype(jnp.float32),
        )
        mod_grad_low = mod_grad_cols.astype(jnp.bfloat16)
        mod_grad = jnp.einsum(
            "bd,bkc->dkc", cond_low, mod_grad_low, preferred_element_type=jnp.float32
        )
        mod_bias_term = jnp.sum(mod_grad_low, axis=0, dtype=jnp.float32)
        cond_part_grad = jnp.einsum(
            "bkc,dkc->bd", mod_grad_low, mod_full, preferred_element_type=jnp.float32
        )
        cond_act_grad = lax.psum(cond_part_grad, "tensor")
        condition_grads.append(silu_back(cond_act_grad)[0])
        bias_totals = (
            bias_totals[0] + mod_bias_term,
            bias_totals[1] + head_bias_term,
            bias_totals[2] + up_bias_term,
            bias_totals[3] + branch_grad_cols,
        )
        weight_terms = (mod_grad, head_grad, mix_grad, up_grad, down_grad)
        grad_sums = (
            weight_terms if grad_sums is None else jax.tree.map(jnp.add, grad_sums, weight_terms)
        )
    grad_sums = reduce_weights(grad_sums)
    bias_sums = lax.psum((bias_totals[0], bias_totals[1], bias_totals[2], bias_totals[3]), "dp")
    return (
        jnp.concatenate(block_outs, axis=0),
        jnp.concatenate(latent_grads, axis=0),
        jnp.concatenate(condition_grads, axis=0),
        grad_sums[0],
        bias_sums[0],
        grad_sums[1],
        bias_sums[1],
        grad_sums[2],
        bias_sums[3],
        grad_sums[3],
        bias_sums[2],
        grad_sums[4],
    )


def head_window(col, width):
    start = jnp.minimum(col // 128 * 128, width - WINDOW)
    return pl.multiple_of(start, 128), col - start


def head_members(heads, width):
    col = lax.broadcasted_iota(jnp.int32, (heads, width), 1)
    first = lax.broadcasted_iota(jnp.int32, (heads, width), 0) * HEAD_DIM
    return jnp.where((col >= first) & (col < first + HEAD_DIM), 1.0, 0.0).astype(bf16)


def attn_fwd_kernel(q_ref, k_ref, v_ref, o_ref, lse_ref, ot_ref, *, blk, heads):
    seq, width = q_ref.shape[1:]
    c = HEAD_DIM ** -0.5 * LOG2E
    ot_ref[...] = v_ref[0].astype(f32).T
    lanes = lax.broadcasted_iota(jnp.int32, (blk, WINDOW), 1)
    ones = jnp.ones((8, seq), f32)
    member = head_members(heads, width)
    longest = [
        jnp.max(
            lax.dot_general(member, ref[0] * ref[0], NT, preferred_element_type=f32),
            axis=1,
            keepdims=True,
        )
        for ref in (q_ref, k_ref)
    ]
    small = jnp.max(longest[0] * longest[1]) * (1.1 * c * c) < 60.0 * 60.0

    def run(shifted):
        def pair(i, carry):
            steps = [(2 * i + odd, b) for odd in range(2) for b in range(seq // blk)]

            def scores(head, b):
                start, off = head_window(head * HEAD_DIM, width)
                mask = (lanes >= off) & (lanes < off + HEAD_DIM)
                qb = q_ref[0, b * blk : (b + 1) * blk, pl.ds(start, WINDOW)]
                qb = jnp.where(mask, qb, jnp.zeros_like(qb))
                return lax.dot_general(
                    k_ref[0, :, pl.ds(start, WINDOW)], qb, NT, preferred_element_type=f32
                )

            st = scores(*steps[0])
            vt = None
            for n, (head, b) in enumerate(steps):
                after = scores(*steps[n + 1]) if n + 1 < len(steps) else None
                mine = pl.ds(pl.multiple_of(head * HEAD_DIM, 8), HEAD_DIM)
                if b == 0:
                    vt = jnp.concatenate([ot_ref[mine, :], ones], axis=0).astype(bf16)
                rows = slice(b * blk, (b + 1) * blk)
                if shifted:
                    m = jnp.max(st, axis=0, keepdims=True)
                    p = jnp.exp2((st - m) * c).astype(bf16)
                else:
                    p = jnp.exp2(st * c).astype(bf16)
                ot = jnp.dot(vt, p, preferred_element_type=f32)
                l = ot[HEAD_DIM : HEAD_DIM + 1]
                ot_ref[mine, rows] = ot[:HEAD_DIM] * (1.0 / l)
                lse_ref[0, 0, pl.ds(head, 1), rows] = jnp.log2(l) + m * c if shifted else jnp.log2(l)
                st = after
            return carry

        lax.fori_loop(0, heads // 2, pair, 0)

    pl.when(small)(lambda: run(False))
    pl.when(jnp.logical_not(small))(lambda: run(True))
    o_ref[0] = ot_ref[...].T.astype(bf16)


def attn_fwd(qkv, heads, blk=256):
    n, seq, wide = qkv.shape
    width = wide // 6
    spec = lambda j: pl.BlockSpec((1, seq, width), lambda b, h: (b, 0, 3 * h + j))
    return pl.pallas_call(
        partial(attn_fwd_kernel, blk=blk, heads=heads),
        grid=(n, 2),
        in_specs=[spec(0), spec(1), spec(2)],
        out_specs=[
            pl.BlockSpec((1, seq, width), lambda b, h: (b, 0, h)),
            pl.BlockSpec((1, 1, heads, seq), lambda b, h: (b, h, 0, 0)),
        ],
        out_shape=[
            jax.ShapeDtypeStruct((n, seq, 2 * width), bf16),
            jax.ShapeDtypeStruct((n, 2, heads, seq), f32),
        ],
        scratch_shapes=[pltpu.VMEM((width, seq), f32)],
        compiler_params=pltpu.CompilerParams(vmem_limit_bytes=56 << 20),
        cost_estimate=pl.CostEstimate(
            flops=8 * n * seq * seq * width,
            bytes_accessed=16 * n * seq * width,
            transcendentals=2 * n * heads * seq * seq,
        ),
        name="attention_forward",
    )(qkv, qkv, qkv)


def attn_bwd_kernel(
    q_ref, k_ref, v_ref, do_ref, o_ref, lse_ref, dqkv_ref, sum_ref,
    dqt_ref, delta_ref, pt_ref, dst_ref, *, blk, heads
):
    seq, width = q_ref.shape[1:]
    scale = HEAD_DIM ** -0.5
    c = scale * LOG2E
    dqt_ref[...] = k_ref[0].astype(f32).T
    prod = do_ref[0].astype(f32) * o_ref[0].astype(f32)
    high = prod.astype(bf16)
    low = (prod - high.astype(f32)).astype(bf16)
    member = head_members(heads, width)
    delta_ref[...] = lax.dot_general(member, high, NT, preferred_element_type=f32) + lax.dot_general(
        member, low, NT, preferred_element_type=f32
    )
    lanes = lax.broadcasted_iota(jnp.int32, (seq, WINDOW), 1)
    edge = heads * HEAD_DIM // 128 * 128
    for part in (1, 2):
        dqkv_ref[0, :, part * width + edge : (part + 1) * width] = jnp.zeros((seq, width - edge), bf16)

    def one(head, carry):
        start, off = head_window(head * HEAD_DIM, width)
        window = pl.ds(start, WINDOW)
        mask = (lanes >= off) & (lanes < off + HEAD_DIM)
        keys = k_ref[0, :, window]
        values = v_ref[0, :, window]
        qm = q_ref[0, :, window]
        qm = jnp.where(mask, qm, jnp.zeros_like(qm))
        dom = do_ref[0, :, window]
        dom = jnp.where(mask, dom, jnp.zeros_like(dom))
        mine = pl.ds(pl.multiple_of(head * HEAD_DIM, 8), HEAD_DIM)
        kt = dqt_ref[mine, :].astype(bf16)
        def products(b):
            rows = slice(b * blk, (b + 1) * blk)
            st = lax.dot_general(keys, qm[rows], NT, preferred_element_type=f32)
            return st, lax.dot_general(values, dom[rows], NT, preferred_element_type=f32)

        now = products(0)
        for b in range(seq // blk):
            rows = slice(b * blk, (b + 1) * blk)
            later = products(b + 1) if b + 1 < seq // blk else None
            st, dpt = now
            p = jnp.exp2(st * c - lse_ref[0, 0, pl.ds(head, 1), rows])
            dst = (p * (dpt - delta_ref[pl.ds(head, 1), rows])).astype(bf16)
            pt_ref[:, rows] = p.astype(bf16)
            dst_ref[:, rows] = dst
            dqt_ref[mine, rows] = jnp.dot(kt, dst, preferred_element_type=f32) * scale
            now = later
        dk = jnp.dot(dst_ref[...], qm, preferred_element_type=f32) * scale
        dv = jnp.dot(pt_ref[...], dom, preferred_element_type=f32)
        kwin = pl.ds(pl.multiple_of(width + start, 128), WINDOW)
        vwin = pl.ds(pl.multiple_of(2 * width + start, 128), WINDOW)
        dqkv_ref[0, :, kwin] = jnp.where(mask, dk.astype(bf16), dqkv_ref[0, :, kwin])
        dqkv_ref[0, :, vwin] = jnp.where(mask, dv.astype(bf16), dqkv_ref[0, :, vwin])
        return carry

    lax.fori_loop(0, heads, one, 0)
    dqkv_ref[0, :, :width] = dqt_ref[...].T.astype(bf16)
    sum_ref[0, 0] = jnp.sum(dqkv_ref[0].astype(f32), axis=0, keepdims=True)


def attn_bwd(qkv, grad, mixed, lse, heads, blk=256):
    n, seq, wide = qkv.shape
    width = wide // 6
    spec = lambda j: pl.BlockSpec((1, seq, width), lambda b, h: (b, 0, 3 * h + j))
    out = pl.BlockSpec((1, seq, width), lambda b, h: (b, 0, h))
    return pl.pallas_call(
        partial(attn_bwd_kernel, blk=blk, heads=heads),
        grid=(n, 2),
        in_specs=[
            spec(0), spec(1), spec(2), out, out,
            pl.BlockSpec((1, 1, heads, seq), lambda b, h: (b, h, 0, 0)),
        ],
        out_specs=[
            pl.BlockSpec((1, seq, 3 * width), lambda b, h: (b, 0, h)),
            pl.BlockSpec((1, 1, 1, 3 * width), lambda b, h: (b, h, 0, 0)),
        ],
        out_shape=[
            jax.ShapeDtypeStruct(qkv.shape, bf16),
            jax.ShapeDtypeStruct((n, 2, 1, 3 * width), f32),
        ],
        scratch_shapes=[
            pltpu.VMEM((width, seq), f32),
            pltpu.VMEM((heads, seq), f32),
            pltpu.VMEM((seq, seq), bf16),
            pltpu.VMEM((seq, seq), bf16),
        ],
        compiler_params=pltpu.CompilerParams(vmem_limit_bytes=56 << 20),
        cost_estimate=pl.CostEstimate(flops=0, bytes_accessed=0, transcendentals=0),
        name="attention_backward",
    )(qkv, qkv, qkv, grad, mixed, lse)


def gelu_with_slope(u):
    k, cubic = 0.7978845608028654, 0.7978845608028654 * 0.044715
    square = u * u
    half = 0.5 + 0.5 * jnp.tanh(u * (k + cubic * square))
    value = u * half
    return value, half + value * (1.0 - half) * (2.0 * k + 6.0 * cubic * square)


def tile_steps(rows, cols, sub_rows, sub_cols):
    return [
        (slice(i, i + sub_rows), slice(j, j + sub_cols))
        for j in range(0, cols, sub_cols)
        for i in range(0, rows, sub_rows)
    ]


def up_forward_kernel(x_ref, w_ref, b_ref, act_ref, slope_ref):
    steps = tile_steps(*act_ref.shape, 256, 256)
    product = lambda r, c: jnp.dot(x_ref[r, :], w_ref[:, c], preferred_element_type=f32)
    now = product(*steps[0])
    for n, (r, c) in enumerate(steps):
        later = product(*steps[n + 1]) if n + 1 < len(steps) else None
        value, slope = gelu_with_slope(now + b_ref[:, c])
        act_ref[r, c] = value.astype(bf16)
        slope_ref[r, c] = slope.astype(bf16)
        now = later


def up_forward(x, w, bias):
    count, seq, depth = x.shape
    hidden = bias.shape[0]
    rows, cols = 1024, hidden // 3
    tile = pl.BlockSpec((rows, cols), lambda j, i: (i, j))
    act, slope = pl.pallas_call(
        up_forward_kernel,
        grid=(hidden // cols, count * seq // rows),
        in_specs=[
            pl.BlockSpec((rows, depth), lambda j, i: (i, 0)),
            pl.BlockSpec((depth, cols), lambda j, i: (0, j)),
            pl.BlockSpec((1, cols), lambda j, i: (0, j)),
        ],
        out_specs=[tile, tile],
        out_shape=[jax.ShapeDtypeStruct((count * seq, hidden), bf16)] * 2,
        compiler_params=pltpu.CompilerParams(vmem_limit_bytes=56 << 20),
        cost_estimate=pl.CostEstimate(
            flops=2 * count * seq * depth * hidden,
            bytes_accessed=4 * count * seq * hidden,
            transcendentals=count * seq * hidden,
        ),
        name="up_forward",
    )(x.reshape(count * seq, depth), w, bias.reshape(1, hidden))
    return act.reshape(count, seq, hidden), slope.reshape(count, seq, hidden)


def down_backward_kernel(g_ref, w_ref, slope_ref, out_ref, sum_ref):
    steps = tile_steps(*out_ref.shape, out_ref.shape[0], 256)
    product = lambda r, c: jnp.dot(g_ref[r, :], w_ref[:, c], preferred_element_type=f32)

    @pl.when(pl.program_id(1) == 0)
    def _():
        sum_ref[...] = jnp.zeros_like(sum_ref)

    now = product(*steps[0])
    for n, (r, c) in enumerate(steps):
        later = product(*steps[n + 1]) if n + 1 < len(steps) else None
        grad = (now * slope_ref[r, c].astype(f32)).astype(bf16)
        out_ref[r, c] = grad
        sum_ref[:, c] += jnp.sum(grad.astype(f32), axis=0, keepdims=True)
        now = later


def down_backward(g, w, slope):
    count, seq, depth = g.shape
    hidden = slope.shape[2]
    rows, cols = 1024, hidden // 3
    tile = pl.BlockSpec((rows, cols), lambda j, i: (i, j))
    grad, total = pl.pallas_call(
        down_backward_kernel,
        grid=(hidden // cols, count * seq // rows),
        in_specs=[
            pl.BlockSpec((rows, depth), lambda j, i: (i, 0)),
            pl.BlockSpec((depth, cols), lambda j, i: (0, j)),
            tile,
        ],
        out_specs=[tile, pl.BlockSpec((1, cols), lambda j, i: (0, j))],
        out_shape=[
            jax.ShapeDtypeStruct((count * seq, hidden), bf16),
            jax.ShapeDtypeStruct((1, hidden), f32),
        ],
        compiler_params=pltpu.CompilerParams(vmem_limit_bytes=56 << 20),
        cost_estimate=pl.CostEstimate(
            flops=2 * count * seq * depth * hidden,
            bytes_accessed=4 * count * seq * hidden,
            transcendentals=0,
        ),
        name="down_backward",
    )(g.reshape(count * seq, depth), w, slope.reshape(count * seq, hidden))
    return grad.reshape(count, seq, hidden), total[0]


CORES = 2
ROWS = 2


def place(rank):
    return rank // (ROWS * CORES), rank // CORES % ROWS, rank % CORES


def rank_of(z, y, core):
    return (z * ROWS + y) * CORES + core


def greet(side):
    rank = lax.axis_index("dp")
    groups = lax.axis_size("dp")
    barrier = pltpu.get_barrier_semaphore()
    for step in range(1, groups):
        pl.semaphore_signal(barrier, inc=1, device_id={"dp": lax.rem(rank + step, groups)}, device_id_type=MESH)
    pl.semaphore_signal(barrier, inc=1, device_id={"tensor": 1 - side}, device_id_type=MESH)
    pl.semaphore_wait(barrier, groups)


class Spread:
    def __init__(self, source, out, sends, arrivals, lanes=None):
        self.source, self.out, self.sends, self.arrivals = source, out, sends, arrivals
        self.lanes = lanes
        self.rank = lax.axis_index("dp")
        self.z, self.y, self.core = place(self.rank)
        self.depth = lax.axis_size("dp") // (ROWS * CORES)
        self.started = []

    def block(self, origin):
        return self.out.at[origin] if self.lanes is None else self.out.at[origin, :, self.lanes]

    def copy(self, origin, edge, target, source=None):
        return pltpu.make_async_remote_copy(
            src_ref=self.block(origin) if source is None else source,
            dst_ref=self.block(origin),
            send_sem=self.sends.at[origin, edge],
            recv_sem=self.arrivals.at[origin],
            device_id={"dp": target},
            device_id_type=MESH,
        )

    def send(self, origin, edge, target, source=None, when=None):
        sent = self.copy(origin, edge, target, source)
        if when is None:
            sent.start()
        else:
            pl.when(when)(sent.start)
        self.started.append((sent, when))

    def arrive(self, origin):
        self.copy(origin, 0, rank_of(self.z, 1 - self.y, self.core)).wait_recv()

    def up(self):
        return rank_of(self.z + 1, self.y, self.core)

    def down(self):
        return rank_of(self.z - 1, self.y, self.core)

    def across(self):
        return rank_of(self.z, 1 - self.y, self.core)

    def sibling(self):
        return rank_of(self.z, self.y, 1 - self.core)

    def begin(self):
        rank, source = self.rank, self.source
        self.send(rank, 0, self.up(), source, self.z < self.depth - 1)
        self.send(rank, 3, self.down(), source, self.z > 0)
        self.send(rank, 1, self.across(), source)
        self.send(rank, 2, self.sibling(), source)

    def relay(self, hop):
        for toward, there in ((1, self.z >= hop), (-1, self.z + hop < self.depth)):
            origin = rank_of(self.z - toward * hop, self.y, self.core)
            further = (self.z < self.depth - 1) if toward > 0 else (self.z > 0)
            pl.when(there)(lambda: self.arrive(origin))
            self.send(
                origin, 0, self.up() if toward > 0 else self.down(), when=there & further
            )
            self.send(origin, 1, self.across(), when=there)
            self.send(origin, 2, self.sibling(), when=there)

    def relay_across(self, hop):
        for toward, there in ((1, self.z >= hop), (-1, self.z + hop < self.depth)):
            if hop == 0 and toward < 0:
                continue
            origin = rank_of(self.z - toward * hop, 1 - self.y, self.core)
            pl.when(there)(lambda: self.arrive(origin))
            self.send(origin, 2, self.sibling(), when=there)

    def finish(self):
        for z in range(self.depth):
            for y in range(ROWS):
                self.arrive(rank_of(z, y, 1 - self.core))
        for sent, when in self.started:
            if when is None:
                sent.wait_send()
            else:
                pl.when(when)(sent.wait_send)


class DirectSpread:
    def __init__(self, out, sends, arrivals):
        self.out, self.sends, self.arrivals = out, sends, arrivals
        self.rank = lax.axis_index("dp")
        self.groups = lax.axis_size("dp")
        self.sibling = self.rank + 1 - 2 * lax.rem(self.rank, CORES)
        self.steps = range(CORES, self.groups, CORES)

    def copy(self, origin, send, target):
        return pltpu.make_async_remote_copy(
            src_ref=self.out.at[origin],
            dst_ref=self.out.at[origin],
            send_sem=self.sends.at[send],
            recv_sem=self.arrivals.at[origin],
            device_id={"dp": target},
            device_id_type=MESH,
        )

    def peer(self, step):
        return lax.rem(self.rank + step, self.groups)

    def begin(self):
        for step in self.steps:
            self.copy(self.rank, step, self.peer(step)).start()
        self.copy(self.rank, 0, self.sibling).start()

    def relay(self):
        for step in self.steps:
            origin = self.peer(step)
            self.copy(origin, step, origin).wait_recv()
            self.copy(origin, step + 1, self.sibling).start()

    def finish(self):
        for step in range(0, self.groups, CORES):
            origin = lax.rem(self.sibling + step, self.groups)
            self.copy(origin, 0, self.sibling).wait_recv()
        for step in self.steps:
            self.copy(self.rank, step, self.peer(step)).wait_send()
            self.copy(self.peer(step), step + 1, self.sibling).wait_send()
        self.copy(self.rank, 0, self.sibling).wait_send()


class Exchange:
    def __init__(self, source, out, sends, arrivals):
        self.source, self.out, self.sends, self.arrivals = source, out, sends, arrivals
        self.rank = lax.axis_index("dp")
        self.groups = lax.axis_size("dp")

    def copy(self, step):
        peer = lax.rem(self.rank + step, self.groups)
        return pltpu.make_async_remote_copy(
            src_ref=self.source.at[peer],
            dst_ref=self.out.at[self.rank],
            send_sem=self.sends.at[step],
            recv_sem=self.arrivals.at[self.rank],
            device_id={"dp": peer},
            device_id_type=MESH,
        )

    def begin(self):
        self.out[self.rank] = self.source[self.rank]
        for step in range(1, self.groups):
            self.copy(step).start()

    def finish(self):
        for step in range(1, self.groups):
            peer = lax.rem(self.rank + step, self.groups)
            pltpu.make_async_remote_copy(
                src_ref=self.source.at[peer],
                dst_ref=self.out.at[peer],
                send_sem=self.sends.at[step],
                recv_sem=self.arrivals.at[peer],
                device_id={"dp": peer},
                device_id_type=MESH,
            ).wait_recv()

    def drain(self):
        for step in range(1, self.groups):
            self.copy(step).wait_send()


def to_partner(source, target, side, sends, arrivals, k):
    return pltpu.make_async_remote_copy(
        src_ref=source,
        dst_ref=target,
        send_sem=sends.at[k],
        recv_sem=arrivals.at[k],
        device_id={"tensor": 1 - side},
        device_id_type=MESH,
    )


def opening_kernel(
    cond_ref, mod_w_ref, mod_bias_ref, bias_ref, head_ref, rest_ref, latent_ref,
    head_out, rest_out, latent_out, mod_out, cond_out, bias_out,
    part_ref, mod_in,
    x_send, x_recv, c_send, c_recv, m_send, m_recv, h_send, h_recv, local_sem,
):
    side = lax.axis_index("tensor")
    rank = lax.axis_index("dp")
    greet(side)
    conds = Exchange(cond_ref, cond_out, c_send, c_recv)
    conds.begin()
    lanes = head_ref.shape[1]
    mine = Spread(head_ref, head_out, h_send.at[0], h_recv.at[0], pl.ds(0, lanes))
    other = Spread(None, head_out, h_send.at[1], h_recv.at[1], pl.ds(lanes, lanes))
    head_swap = to_partner(head_ref, other.block(rank), side, x_send, x_recv, 0)
    head_swap.start()
    mine.begin()
    biases = to_partner(bias_ref, bias_out, side, x_send, x_recv, 3)
    biases.start()
    rest = to_partner(rest_ref, rest_out, side, x_send, x_recv, 1)
    rest.start()
    own = latent_out.shape[0]
    latents = to_partner(
        latent_ref.at[pl.ds((1 - side) * own, own)], latent_out, side, x_send, x_recv, 4
    )
    latents.start()
    keep = pltpu.make_async_copy(head_ref, mine.block(rank), local_sem)
    keep.start()
    conds.finish()
    groups, rows, lanes = cond_out.shape
    half = mod_bias_ref.shape[1]
    low = cond_out[...].reshape(groups * rows, lanes).astype(bf16)
    front = lax.broadcasted_iota(jnp.int32, (groups * rows, half), 0) % rows < rows // 2
    part_ref[...] = jnp.where(
        front,
        jnp.dot(low, mod_w_ref[0], preferred_element_type=f32),
        jnp.dot(low, mod_w_ref[1], preferred_element_type=f32),
    ).reshape(groups, rows, half)
    mods = Exchange(part_ref, mod_in, m_send, m_recv)
    mods.begin()
    head_swap.wait_recv()
    other.begin()
    mine.relay(1)
    mods.finish()
    mod_out[0] = jnp.sum(mod_in[...], axis=0) + mod_bias_ref[...]
    mod_swap = to_partner(mod_out.at[0], mod_out.at[1], side, x_send, x_recv, 2)
    mod_swap.start()
    other.relay(1)
    mine.relay_across(0)
    other.relay_across(0)
    depth = mine.depth
    for hop in range(2, depth):
        for s in (mine, other):
            s.relay(hop)
            s.relay_across(hop - 1)
    for s in (mine, other):
        s.relay_across(depth - 1)
    keep.wait()
    mine.finish()
    other.finish()
    mod_swap.wait()
    rest.wait()
    latents.wait()
    biases.wait()
    head_swap.wait_send()
    conds.drain()
    mods.drain()


def opening(cond_low, mod_weight, mod_bias, biases, head, rest, latent):
    groups = lax.axis_size("dp")
    count = cond_low.shape[0]
    depth = cond_low.shape[1] // groups
    half = mod_weight.shape[1] * mod_weight.shape[2] // 2
    blocks = cond_low.astype(f32).reshape(count, groups, depth).transpose(1, 0, 2)
    blocks = jnp.concatenate([blocks, blocks], axis=1)
    blocks = jnp.pad(blocks, ((0, 0), (0, 0), (0, 128 - depth)))
    weights = jnp.pad(mod_weight.reshape(depth, 2, half), ((0, 128 - depth), (0, 0), (0, 0))).transpose(1, 0, 2)
    bias = jnp.repeat(mod_bias.astype(f32).reshape(2, half), count, axis=0)
    dma = pltpu.SemaphoreType.DMA
    vmem = pl.BlockSpec(memory_space=pltpu.VMEM)
    anywhere = pl.BlockSpec(memory_space=pl.ANY)
    return pl.pallas_call(
        opening_kernel,
        in_specs=[vmem, vmem, vmem, vmem, anywhere, anywhere, anywhere],
        out_specs=[anywhere, anywhere, anywhere, vmem, vmem, vmem],
        out_shape=[
            jax.ShapeDtypeStruct((groups, depth, 2 * head.shape[1]), bf16),
            jax.ShapeDtypeStruct(rest.shape, bf16),
            jax.ShapeDtypeStruct((count // 2,) + latent.shape[1:], bf16),
            jax.ShapeDtypeStruct((2, 2 * count, half), f32),
            jax.ShapeDtypeStruct(blocks.shape, f32),
            jax.ShapeDtypeStruct(biases.shape, f32),
        ],
        scratch_shapes=[
            pltpu.VMEM((groups, 2 * count, half), f32),
            pltpu.VMEM((groups, 2 * count, half), f32),
            dma((5,)), dma((5,)),
            dma((groups,)), dma((groups,)),
            dma((groups,)), dma((groups,)),
            dma((2, groups, 4)), dma((2, groups)),
            dma,
        ],
        compiler_params=pltpu.CompilerParams(collective_id=0, has_side_effects=True, vmem_limit_bytes=32 << 20),
        cost_estimate=pl.CostEstimate(flops=0, bytes_accessed=0, transcendentals=0),
        name="opening",
    )(blocks, weights, bias, biases, head, rest, latent)


def closing_kernel(
    mod_ref, bias_ref, mod_w_ref,
    mod_out, bias_out, cond_out,
    mod_unit, bias_unit, bias_in, part_ref, cond_in,
    x_send, x_recv, m_send, m_recv, b_send, b_recv, c_send, c_recv,
):
    side = lax.axis_index("tensor")
    rank = lax.axis_index("dp")
    greet(side)
    rows = mod_ref.shape[1]
    mod_swap = to_partner(mod_ref.at[1], mod_unit.at[1], side, x_send, x_recv, 0)
    mod_swap.start()
    bias_swap = to_partner(bias_ref.at[1], bias_unit.at[1], side, x_send, x_recv, 1)
    bias_swap.start()
    mod_swap.wait()
    bias_swap.wait()
    mod_out[rank] = mod_ref[0] + mod_unit[1]
    bias_in[rank] = bias_ref[0] + bias_unit[1]
    mods = DirectSpread(mod_out, m_send, m_recv)
    biases = DirectSpread(bias_in, b_send, b_recv)
    mods.begin()
    biases.begin()
    mods.relay()
    biases.relay()
    mods.finish()
    groups, rows, half = mod_out.shape
    low = mod_out[...].reshape(groups * rows, half).astype(bf16)
    lanes = mod_w_ref.shape[1]
    front = lax.broadcasted_iota(jnp.int32, (groups * rows, lanes), 0) % rows < rows // 2
    part_ref[...] = jnp.where(
        front,
        lax.dot_general(low, mod_w_ref[0], NT, preferred_element_type=f32),
        lax.dot_general(low, mod_w_ref[1], NT, preferred_element_type=f32),
    ).reshape(groups, rows, lanes)
    conds = Exchange(part_ref, cond_in, c_send, c_recv)
    conds.begin()
    biases.finish()
    bias_out[...] = jnp.sum(bias_in[...], axis=0)
    conds.finish()
    cond_out[0] = cond_in[...]
    cond_swap = to_partner(cond_out.at[0], cond_out.at[1], side, x_send, x_recv, 2)
    cond_swap.start()
    cond_swap.wait()
    conds.drain()


def closing(mod_pair, bias_pair, mod_weight):
    groups = lax.axis_size("dp")
    rows, half = mod_pair.shape[1:]
    depth = mod_weight.shape[0]
    weights = jnp.pad(mod_weight.reshape(depth, 2, half), ((0, 128 - depth), (0, 0), (0, 0))).transpose(1, 0, 2)
    dma = pltpu.SemaphoreType.DMA
    vmem = pl.BlockSpec(memory_space=pltpu.VMEM)
    lines = bias_pair.shape[1]
    return pl.pallas_call(
        closing_kernel,
        in_specs=[vmem, vmem, vmem],
        out_specs=[vmem, vmem, vmem],
        out_shape=[
            jax.ShapeDtypeStruct((groups, rows, half), f32),
            jax.ShapeDtypeStruct((lines, 128), f32),
            jax.ShapeDtypeStruct((2, groups, rows, 128), f32),
        ],
        scratch_shapes=[
            pltpu.VMEM((2, rows, half), f32),
            pltpu.VMEM((2, lines, 128), f32),
            pltpu.VMEM((groups, lines, 128), f32),
            pltpu.VMEM((groups, rows, 128), f32),
            pltpu.VMEM((groups, rows, 128), f32),
            dma((3,)), dma((3,)),
            dma((groups,)), dma((groups,)),
            dma((groups,)), dma((groups,)),
            dma((groups,)), dma((groups,)),
        ],
        compiler_params=pltpu.CompilerParams(collective_id=1, has_side_effects=True, vmem_limit_bytes=32 << 20),
        cost_estimate=pl.CostEstimate(flops=0, bytes_accessed=0, transcendentals=0),
        name="closing",
    )(mod_pair, bias_pair, weights)


class Collect:
    def __init__(self, grads, totals, from_core, from_row, from_z, terms, row_out, z_out, *sems):
        self.grads, self.totals = grads, totals
        self.from_core, self.from_row, self.from_z = from_core, from_row, from_z
        self.terms, self.row_out, self.z_out = terms, row_out, z_out
        (self.core_send, self.core_recv, self.row_send, self.row_recv, self.z_send, self.z_recv, self.local) = sems
        self.rank = lax.axis_index("dp")
        self.z, self.y, self.core = place(self.rank)
        self.depth = lax.axis_size("dp") // (ROWS * CORES)
        self.pieces, _, _, self.width = from_core.shape
        self.outer = (self.z == 0) | (self.z == self.depth - 1)

    def lanes(self, n):
        return pl.ds(pl.multiple_of(n * self.width, 128), self.width)

    def block(self, n, rank):
        return self.grads.at[rank, :, self.lanes(n)]

    def level(self, k):
        falling = self.depth - 1 - k
        falling = falling - jnp.where(falling <= self.z, 1, 0)
        rising = k + jnp.where(k >= self.z, 1, 0)
        there = jnp.where(self.z < self.depth // 2, falling, rising)
        return jnp.where(k == self.depth - 1, self.z, there)

    def core_copy(self, n, level, y):
        k = level * ROWS + y
        return pltpu.make_async_remote_copy(
            src_ref=self.block(n, rank_of(level, y, 1 - self.core)),
            dst_ref=self.from_core.at[n, k],
            send_sem=self.core_send.at[n, k],
            recv_sem=self.core_recv.at[n, k],
            device_id={"dp": rank_of(self.z, self.y, 1 - self.core)},
            device_id_type=MESH,
        )

    def row_copy(self, n, k):
        level = self.level(k)
        return pltpu.make_async_remote_copy(
            src_ref=self.row_out.at[k],
            dst_ref=self.from_row.at[n, level],
            send_sem=self.row_send.at[n, k],
            recv_sem=self.row_recv.at[n, level],
            device_id={"dp": rank_of(self.z, 1 - self.y, self.core)},
            device_id_type=MESH,
        )

    def z_copy(self, n, k):
        level = self.level(k)
        above = jnp.where(level > self.z, 1, 0)
        return pltpu.make_async_remote_copy(
            src_ref=self.z_out.at[k],
            dst_ref=self.from_z.at[n, 1 - above, level],
            send_sem=self.z_send.at[n, k],
            recv_sem=self.z_recv.at[n, 1 - above, level],
            device_id={"dp": rank_of(self.z + 2 * above - 1, self.y, self.core)},
            device_id_type=MESH,
        )

    def z_arrival(self, n, way, level):
        return pltpu.make_async_remote_copy(
            src_ref=self.z_out.at[0],
            dst_ref=self.from_z.at[n, way, level],
            send_sem=self.z_send.at[n, 0],
            recv_sem=self.z_recv.at[n, way, level],
            device_id={"dp": rank_of(self.z, 1 - self.y, self.core)},
            device_id_type=MESH,
        )

    def each_core_copy(self, act):
        def some(i, carry):
            n, level = i // self.depth, self.level(i % self.depth)
            act(self.core_copy(n, level, 1 - self.y))
            act(self.core_copy(n, level, self.y))
            return carry

        lax.fori_loop(0, self.pieces * self.depth, some, 0)

    def begin(self):
        self.each_core_copy(lambda copy: copy.start())

    def fetches(self, kind, n, k):
        level = self.level(k)
        y = 1 - self.y if kind == "row" else self.y
        slot = k if kind == "row" else self.depth + k

        def get(j, ref):
            return pltpu.make_async_copy(ref, self.terms.at[slot, j], self.local.at[slot, j])

        found = [
            (get(0, self.block(n, rank_of(level, y, self.core))), None),
            (get(1, self.from_core.at[n, level * ROWS + y]), None),
        ]
        if kind == "z":
            below = (level >= self.z) & (self.z > 0)
            above = (level <= self.z) & (self.z < self.depth - 1)
            found.append((get(2, self.from_row.at[n, level]), None))
            found.append((get(3, self.from_z.at[n, 0, level]), below))
            found.append((get(4, self.from_z.at[n, 1, level]), above))
        return found

    def load(self, kind, n, k):
        level = self.level(k)
        y = 1 - self.y if kind == "row" else self.y
        self.core_copy(n, level, y).wait_recv()
        if kind == "z":
            self.row_copy(n, k).wait_recv()
        for j, (fetch, when) in enumerate(self.fetches(kind, n, k)):
            if when is None:
                fetch.start()
            else:

                def arrived(j=j, fetch=fetch):
                    self.z_arrival(n, j - 3, level).wait_recv()
                    fetch.start()

                pl.when(when)(arrived)

    def finish(self, kind, n, k, last=False):
        total = None
        slot = k if kind == "row" else self.depth + k
        for j, (fetch, when) in enumerate(self.fetches(kind, n, k)):
            if when is None:
                fetch.wait()
            else:
                pl.when(when)(fetch.wait)
            term = self.terms[slot, j].astype(f32)
            if when is not None:
                term = jnp.where(when, term, 0.0)
            total = term if total is None else total + term
        if last:
            self.totals[:, self.lanes(n)] = total
            return
        copy = self.row_copy if kind == "row" else self.z_copy
        out = self.row_out if kind == "row" else self.z_out
        pl.when(n > 0)(lambda: copy(n - 1, k).wait_send())
        out[k] = total.astype(bf16)
        copy(n, k).start()

    def units(self, r):
        found = []
        final = self.depth - 1
        valid = lambda n: (n >= 0) & (n < self.pieces)
        for k in range(self.depth):
            found.append((valid(r), "row", r, k, False))
        for k in range(final):
            age = jnp.where(self.outer, 2, 3 if k < final - 1 else 4)
            found.append((valid(r - age), "z", r - age, k, False))
        found.append((valid(r - 5), "z", r - 5, final, True))
        return found

    def rounds(self):
        return self.pieces + 5

    def load_round(self, r):
        for when, kind, n, k, _ in self.units(r):
            pl.when(when)(lambda kind=kind, n=n, k=k: self.load(kind, n, k))

    def finish_round(self, r):
        for when, kind, n, k, last in self.units(r):
            pl.when(when)(lambda kind=kind, n=n, k=k, last=last: self.finish(kind, n, k, last))

    def end(self):
        n = self.pieces - 1
        for k in range(self.depth):
            self.row_copy(n, k).wait_send()
        for k in range(self.depth - 1):
            self.z_copy(n, k).wait_send()
        self.each_core_copy(lambda copy: copy.wait_send())


def collect_shapes(pieces, width, groups, depth):
    levels = groups // (ROWS * CORES)
    dma = pltpu.SemaphoreType.DMA
    arrivals = [
        jax.ShapeDtypeStruct((pieces, levels * ROWS, depth, width), bf16),
        jax.ShapeDtypeStruct((pieces, levels, depth, width), bf16),
        jax.ShapeDtypeStruct((pieces, 2, levels, depth, width), bf16),
    ]
    scratch = [
        pltpu.VMEM((2 * levels, 5, depth, width), bf16),
        pltpu.VMEM((levels, depth, width), bf16),
        pltpu.VMEM((levels - 1, depth, width), bf16),
        dma((pieces, levels * ROWS)), dma((pieces, levels * ROWS)),
        dma((pieces, levels)), dma((pieces, levels)),
        dma((pieces, levels)), dma((pieces, 2, levels)),
        dma((2 * levels, 5)),
    ]
    return arrivals, scratch


TILE = 256


def latents_backward_kernel(
    dqkv_ref, w_ref, lat_ref, first_ref, scale_ref, grads_ref,
    out_ref, sums_ref, totals_ref, rows_in, from_core, from_row, from_z,
    rows_out, x_send, x_recv, *collect,
):
    side = lax.axis_index("tensor")
    r = pl.program_id(0)
    engine = Collect(grads_ref, totals_ref, from_core, from_row, from_z, *collect)
    count, half_seq, _ = rows_in.shape
    per_half = half_seq // TILE
    sent = count * per_half

    def row_copy(i):
        return to_partner(
            rows_out.at[i],
            rows_in.at[i // per_half, pl.ds(pl.multiple_of(i % per_half * TILE, TILE), TILE)],
            side, x_send, x_recv, i,
        )

    @pl.when(r == 0)
    def _():
        greet(side)
        engine.begin()
        sums_ref[...] = jnp.zeros_like(sums_ref)

    engine.load_round(r)

    @pl.when(r < 2 * sent)
    def _():
        grad = lax.dot_general(dqkv_ref[...], w_ref[...], NT, preferred_element_type=f32)
        norm, inverse = normed(lat_ref[...].astype(f32))
        latent = r % sent // per_half
        sums_ref[latent] += jnp.concatenate(
            [jnp.sum(grad, axis=0, keepdims=True), jnp.sum(grad * norm, axis=0, keepdims=True)], axis=0
        )
        back = normed_back(grad * (1.0 + scale_ref[0]), norm, inverse)
        result = (first_ref[...] + back).astype(bf16)
        out_ref[...] = result

        @pl.when(r < sent)
        def _():
            rows_out[r] = result
            row_copy(r).start()

    engine.finish_round(r)

    @pl.when(r == pl.num_programs(0) - 1)
    def _():
        engine.end()
        for i in range(sent):
            row_copy(i).wait()


def latents_backward(dqkv, w, lat, first_grad, scale, grads):
    count, seq, wide = dqkv.shape
    width = lat.shape[2]
    groups = lax.axis_size("dp")
    depth = grads.shape[0] // groups
    per_half = seq // 2 // TILE
    sent = count * per_half
    pieces, piece = 6, wide // 6
    arrivals, scratch = collect_shapes(pieces, piece, groups, depth)

    def tile(r):
        r = jnp.minimum(r, 2 * sent - 1)
        i = r % sent
        return i // per_half * 2 * per_half + i % per_half + jnp.where(r < sent, per_half, 0)

    rows = lambda cols: pl.BlockSpec((TILE, cols), lambda r: (tile(r), 0))
    anywhere = pl.BlockSpec(memory_space=pl.ANY)
    flat = lambda a: a.reshape(count * seq, a.shape[2])
    dma = pltpu.SemaphoreType.DMA
    return pl.pallas_call(
        latents_backward_kernel,
        grid=(max(pieces + 5, 2 * sent),),
        in_specs=[
            rows(wide),
            pl.BlockSpec((width, wide), lambda r: (0, 0), pipeline_mode=pl.Buffered(1)),
            rows(width),
            rows(width),
            pl.BlockSpec((1, 1, width), lambda r: (tile(r) // (2 * per_half), 0, 0)),
            anywhere,
        ],
        out_specs=[
            rows(width),
            pl.BlockSpec((count, 2, width), lambda r: (0, 0, 0)),
            pl.BlockSpec((depth, wide), lambda r: (0, 0)),
        ]
        + [anywhere] * 4,
        out_shape=[
            jax.ShapeDtypeStruct((count * seq, width), bf16),
            jax.ShapeDtypeStruct((count, 2, width), f32),
            jax.ShapeDtypeStruct((depth, wide), f32),
            jax.ShapeDtypeStruct((count, seq // 2, width), bf16),
        ]
        + arrivals,
        scratch_shapes=[pltpu.VMEM((sent, TILE, width), bf16), dma((sent,)), dma((sent,))] + scratch,
        compiler_params=pltpu.CompilerParams(
            collective_id=2, has_side_effects=True, vmem_limit_bytes=56 << 20
        ),
        cost_estimate=pl.CostEstimate(flops=0, bytes_accessed=0, transcendentals=0),
        name="latents_backward",
    )(flat(dqkv), w, flat(lat), flat(first_grad), scale, grads.reshape(groups, depth, wide))[:4]


def normed(values):
    centred = values - jnp.mean(values, axis=-1, keepdims=True)
    variance = jnp.mean(centred * centred, axis=-1, keepdims=True)
    inverse = lax.rsqrt(variance + EPSILON)
    return centred * inverse, inverse


def normed_back(grad, norm, inverse):
    return inverse * (
        grad
        - jnp.mean(grad, axis=-1, keepdims=True)
        - norm * jnp.mean(grad * norm, axis=-1, keepdims=True)
    )


def mm(spec, a, b):
    return jnp.einsum(spec, a, b, preferred_element_type=f32)


def body_by_latents(
    latent,
    condition,
    cotangent,
    mod_weight,
    mod_bias,
    head_weight,
    head_bias,
    mix_weight,
    branch_bias,
    up_weight,
    up_bias,
    down_weight,
):
    side = lax.axis_index("tensor")
    rank = lax.axis_index("dp")
    groups = lax.axis_size("dp")
    count, half_seq, width = latent.shape
    own = count // 2
    cols = width // 2
    depth = head_weight.shape[0]
    hidden = 2 * up_weight.shape[1]

    def swap(a):
        return lax.ppermute(a, "tensor", [(0, 1), (1, 0)])

    def in_order(mine, other, axis):
        return jnp.where(
            side == 0,
            jnp.concatenate([mine, other], axis=axis),
            jnp.concatenate([other, mine], axis=axis),
        )

    def own_latents(a, axis=0):
        return lax.dynamic_slice_in_dim(a, side * own, own, axis)

    def other_latents(a, axis=0):
        return lax.dynamic_slice_in_dim(a, (1 - side) * own, own, axis)

    def placed(a, arrived):
        mine = lax.broadcasted_iota(jnp.int32, (2, 1, 1, 1), 0) == side
        whole = jnp.where(mine, a[None, :, :half_seq], arrived[None])
        return whole.reshape(count, half_seq, width)

    cond_f = condition.astype(f32)
    cond_low = jax.nn.silu(cond_f).astype(bf16)
    heads = cols // HEAD_DIM
    room = -(-cols // 128) * 128

    def roomy(a):
        return jnp.pad(a, [(0, 0)] * (a.ndim - 1) + [(0, room - cols)])

    head_shard = roomy(head_weight).reshape(depth, 3 * room)
    shards = jnp.concatenate([up_weight, roomy(mix_weight.T)], axis=1)
    branch = branch_bias.astype(f32)
    flat = [a.astype(f32).reshape(-1) for a in (head_bias, branch, up_bias)]
    head_all, shards_in, latent_in, mod_parts, cond_blocks, biases_in = opening(
        cond_low,
        mod_weight,
        mod_bias,
        jnp.concatenate(flat).reshape(-1, 128),
        head_shard,
        shards,
        latent,
    )
    biases_in = biases_in.reshape(-1)
    head_bias_in = biases_in[: 2 * cols].reshape(2, cols)
    branch_in = biases_in[2 * cols : 4 * cols].reshape(2, cols)
    head_all = head_all.reshape(width, 6 * room)
    mod_parts = mod_parts.reshape(2, 2, count, 3, cols)
    mod_parts = own_latents(mod_parts, 2).transpose(0, 2, 1, 3, 4).reshape(2, own, 6, cols)
    modulation = in_order(mod_parts[0], mod_parts[1], 2)
    cond_cols = cond_blocks[:, :count, :depth].reshape(groups * count, depth).astype(bf16)
    branch_all = in_order(branch, branch_in, 1)
    row = lambda k: modulation[:, k][:, None, :]
    shift_a, scale_a, gate_a, shift_m, scale_m, gate_m = [row(k) for k in range(6)]

    cuts = (0, hidden // 2, hidden // 2 + room)
    pieces = [a[:, lo:hi] for lo, hi in zip(cuts, cuts[1:]) for a in (shards, shards_in)]
    up_mix = lax.all_gather(jnp.concatenate(pieces, axis=1), "dp", axis=0, tiled=True)
    up_all = up_mix[:, :hidden]
    mix_t = up_mix[:, hidden:]
    down_mine, _ = lax.optimization_barrier((down_weight.T, latent_in))
    down_t = lax.all_gather(
        jnp.concatenate([down_mine, swap(down_mine)], axis=1), "dp", axis=0, tiled=True
    )
    up_bias_f = jnp.concatenate([flat[2], biases_in[4 * cols :]])

    lat = jnp.concatenate([own_latents(latent), latent_in], axis=1)
    lat_f = lat.astype(f32)
    norm1, inv1 = normed(lat_f)
    attn_in = (norm1 * (1.0 + scale_a) + shift_a).astype(bf16)
    empty = jnp.zeros((room,), f32)
    qkv_bias = jnp.concatenate(
        [c for b in (roomy(head_bias.astype(f32)), roomy(head_bias_in)) for c in (b[0], empty, b[1])]
    )
    qkv = (mm("bsd,dc->bsc", attn_in, head_all) + qkv_bias).astype(bf16)
    later, qkv = lax.optimization_barrier((other_latents(cotangent), qkv))
    upstream_low = jnp.concatenate([own_latents(cotangent), swap(later)], axis=1)
    mixed, logsum = attn_fwd(qkv, heads)
    attn_out = mm("bsc,dc->bsd", mixed, mix_t) + branch_all[0]
    first = lat_f + gate_a * attn_out
    norm2, inv2 = normed(first)
    mlp_in = (norm2 * (1.0 + scale_m) + shift_m).astype(bf16)
    act, slope = up_forward(mlp_in, up_mix, up_bias_f)
    upstream = upstream_low.astype(f32)
    mlp_grad = (gate_m * upstream).astype(bf16)
    down_grad = mm("bsd,bsf->df", mlp_grad, act).astype(bf16)
    down_grad, mlp_grad, act = lax.optimization_barrier((down_grad, mlp_grad, act))
    down_sum = lax.psum_scatter(down_grad, "dp", scatter_dimension=0, tiled=True)
    mlp_out = mm("bsf,df->bsd", act, down_t) + branch_all[1]
    block = (first + gate_m * mlp_out).astype(bf16)
    block_in = swap(block[:, half_seq:])

    gate_m_grad = jnp.sum(upstream * mlp_out, axis=1)
    tail_bias_grad = jnp.sum(gate_m[:, 0] * jnp.sum(upstream, axis=1), axis=0)
    pre_grad, up_bias_term = down_backward(mlp_grad, down_t, slope)
    up_grad = mm("bsd,bsf->df", mlp_in, pre_grad).astype(bf16)
    up_grad, pre_grad = lax.optimization_barrier((up_grad, pre_grad))
    mlp_in_grad = mm("bsf,df->bsd", pre_grad, up_all)
    shift_m_grad = jnp.sum(mlp_in_grad, axis=1)
    scale_m_grad = jnp.sum(mlp_in_grad * norm2, axis=1)
    first_grad = upstream + normed_back(mlp_in_grad * (1.0 + scale_m), norm2, inv2)
    gate_a_grad = jnp.sum(first_grad * attn_out, axis=1)
    attn_bias_grad = jnp.sum(gate_a[:, 0] * jnp.sum(first_grad, axis=1), axis=0)
    attn_grad = (gate_a * first_grad).astype(bf16)
    attn_grad, down_sum = lax.optimization_barrier((attn_grad, down_sum))
    mixed_grad = mm("bsd,dc->bsc", attn_grad, mix_t).astype(bf16)
    mix_grad = mm("bsd,bsc->dc", attn_grad, mixed).astype(bf16)
    up_grad = jnp.concatenate([up_grad, mix_grad], axis=1)
    up_grad, mixed_grad = lax.optimization_barrier((up_grad, mixed_grad))
    up_sum = lax.psum_scatter(up_grad, "dp", scatter_dimension=0, tiled=True)
    qkv_grad, qkv_bias_term = attn_bwd(qkv, mixed_grad, mixed, logsum, heads)
    qkv_bias_term = jnp.sum(qkv_bias_term, axis=0)
    head_grad = mm("bsd,bsc->dc", attn_in, qkv_grad).astype(bf16)
    head_grad, up_sum, block_in = lax.optimization_barrier((head_grad, up_sum, block_in))
    block_out = placed(block, block_in)
    lat_grad, sums, head_sum, lat_grad_in = latents_backward(
        qkv_grad, head_all, lat, first_grad, scale_a, head_grad
    )
    shift_a_grad, scale_a_grad = sums[:, 0], sums[:, 1]

    mod_low = jnp.stack(
        [shift_a_grad, scale_a_grad, gate_a_grad, shift_m_grad, scale_m_grad, gate_m_grad], axis=1
    ).astype(bf16)
    branch_term = jnp.stack([attn_bias_grad, tail_bias_grad])
    head_term = qkv_bias_term.reshape(2, 3, room)[:, 0::2, :cols]
    ups = up_bias_term.reshape(2, hidden // 2)

    def mod_share(owner):
        mine = lax.dynamic_slice_in_dim(mod_low.astype(f32), owner * cols, cols, 2)
        mine = mine.reshape(own, 2, 3 * cols).transpose(1, 0, 2)
        empty = jnp.zeros((2, count, 3 * cols), f32)
        return lax.dynamic_update_slice_in_dim(empty, mine, side * own, 1).reshape(2 * count, 3 * cols)

    def bias_share(owner, k):
        branch_cols = lax.dynamic_slice_in_dim(branch_term, owner * cols, cols, 1)
        flat = jnp.concatenate([head_term[k].reshape(-1), branch_cols.reshape(-1), ups[k]])
        return flat.reshape(-1, 128)

    mod_pair = jnp.stack([mod_share(side), mod_share(1 - side)])
    mod_blocks, biases, cond_parts = closing(
        mod_pair,
        jnp.stack([bias_share(side, 0), bias_share(1 - side, 1)]),
        mod_weight,
    )
    latent_grad = placed(lat_grad.reshape(own, 2 * half_seq, width), lat_grad_in)
    biases = biases.reshape(-1)
    mod_rows = mod_blocks.astype(bf16).reshape(groups, 2, count, 3, cols)
    mod_rows = mod_rows.transpose(0, 2, 1, 3, 4).reshape(groups * count, 6, cols)
    mod_weight_grad = mm("bd,bkc->dkc", cond_cols, mod_rows)
    mod_bias_grad = jnp.sum(mod_rows, axis=0, dtype=f32)
    cond_act = jnp.sum(cond_parts[..., :depth].reshape(2, groups, 2, count, depth), axis=(0, 2))
    cond_act = cond_act.transpose(1, 0, 2).reshape(count, groups * depth)
    gate = jax.nn.sigmoid(cond_f)
    condition_grad = cond_act * (gate * (1.0 + cond_f * (1.0 - gate)))

    def joined(summed, axis):
        mine, other = jnp.split(summed, 2, axis=axis)
        return mine.astype(f32) + swap(other.astype(bf16)).astype(f32)

    head_weight_grad = joined(head_sum, 1).reshape(depth, 3, room)[..., :cols]
    mix_weight_grad = joined(up_sum[:, hidden:], 1)[:, :cols].T
    up_weight_grad = joined(up_sum[:, :hidden], 1)
    down_weight_grad = joined(down_sum, 1).T
    return (
        block_out,
        latent_grad,
        condition_grad,
        mod_weight_grad,
        mod_bias_grad,
        head_weight_grad,
        biases[: 2 * cols].reshape(2, cols),
        mix_weight_grad,
        biases[2 * cols : 4 * cols].reshape(2, cols),
        up_weight_grad,
        biases[4 * cols :],
        down_weight_grad,
    )


def solution(mesh):
    placed = (
        P("dp", "tensor", None),
        P("dp", None),
        P("dp", "tensor", None),
        P("dp", None, "tensor"),
        P(None, "tensor"),
        P("dp", None, "tensor"),
        P(None, "tensor"),
        P("tensor", "dp"),
        P(None, "tensor"),
        P("dp", "tensor"),
        P("tensor"),
        P("tensor", "dp"),
    )
    whole_latents = dict(mesh.shape) == {"dp": 16, "tensor": 2}
    return jax.shard_map(
        body_by_latents if whole_latents else body_by_heads,
        mesh=mesh,
        in_specs=placed,
        out_specs=(
            P("dp", "tensor", None),
            P("dp", "tensor", None),
            P("dp", None),
            P("dp", None, "tensor"),
            P(None, "tensor"),
            P("dp", None, "tensor"),
            P(None, "tensor"),
            P("tensor", "dp"),
            P(None, "tensor"),
            P("dp", "tensor"),
            P("tensor"),
            P("tensor", "dp"),
        ),
        check_vma=False,
    )
```

```python
from functools import partial

import jax
import jax.numpy as jnp
from jax import lax
from jax.experimental import pallas as pl
from jax.experimental.pallas import tpu as pltpu
from jax.sharding import PartitionSpec as P

SEQ = 1024
HEAD_DIM = 72
MICRO = 4
LOG2E = 1.4426950408889634
WINDOW = 256
f32 = jnp.float32
bf16 = jnp.bfloat16
NT = (((1,), (1,)), ((), ()))
TN = (((0,), (0,)), ((), ()))
MESH = pl.DeviceIdType.MESH


EPSILON = 1e-06


def layer_norm(values):
    centred = values - jnp.mean(values, axis=-1, keepdims=True)
    variance = jnp.mean(centred * centred, axis=-1, keepdims=True)
    return centred * lax.rsqrt(variance + EPSILON)


def modulate(values, shift, scale):
    return layer_norm(values) * (1.0 + scale[:, None, :]) + shift[:, None, :]


def gelu_tanh(values):
    return jax.nn.gelu(values, approximate=True)


def fetch_weights(mod_weight, head_weight, mix_weight, up_weight, down_weight):
    return (
        lax.all_gather(mod_weight, "dp", axis=0, tiled=True),
        lax.all_gather(head_weight, "dp", axis=0, tiled=True),
        lax.all_gather(mix_weight, "dp", axis=1, tiled=True),
        lax.all_gather(up_weight, "dp", axis=0, tiled=True),
        lax.all_gather(down_weight, "dp", axis=1, tiled=True),
    )


def reduce_weights(grads):
    return (
        lax.psum_scatter(
            grads[0].astype(jnp.bfloat16), "dp", scatter_dimension=0, tiled=True
        ).astype(jnp.float32),
        lax.psum_scatter(
            grads[1].astype(jnp.bfloat16), "dp", scatter_dimension=0, tiled=True
        ).astype(jnp.float32),
        lax.psum_scatter(
            grads[2].astype(jnp.bfloat16), "dp", scatter_dimension=1, tiled=True
        ).astype(jnp.float32),
        lax.psum_scatter(
            grads[3].astype(jnp.bfloat16), "dp", scatter_dimension=0, tiled=True
        ).astype(jnp.float32),
        lax.psum_scatter(
            grads[4].astype(jnp.bfloat16), "dp", scatter_dimension=1, tiled=True
        ).astype(jnp.float32),
    )


def attend_forward(queries, keys, values, block_rows, scale_factor):
    seq_len = queries.shape[0]
    blocked = queries.reshape(seq_len // block_rows, block_rows, queries.shape[1], queries.shape[2])

    def one_block(query_block):
        scores = (
            jnp.einsum("qhd,khd->hqk", query_block, keys, preferred_element_type=jnp.float32)
            * scale_factor
        )
        peak = jnp.max(scores, axis=-1, keepdims=True)
        raised = jnp.exp(scores - peak)
        total = jnp.sum(raised, axis=-1, keepdims=True)
        weights = (raised / total).astype(jnp.bfloat16)
        mixed = jnp.einsum("hqk,khd->qhd", weights, values, preferred_element_type=jnp.float32)
        return (mixed, (peak + jnp.log(total))[..., 0])

    mixed, logsum = lax.map(one_block, blocked)
    return (mixed.reshape(queries.shape), logsum)


def attend_backward(queries, keys, values, grad_mixed, logsum, block_rows, scale_factor):
    seq_len = queries.shape[0]
    block_shape = (seq_len // block_rows, block_rows, queries.shape[1], queries.shape[2])

    def one_block(carried, pieces):
        key_sum, value_sum = carried
        query_block, grad_block, logsum_block = pieces
        scores = (
            jnp.einsum("qhd,khd->hqk", query_block, keys, preferred_element_type=jnp.float32)
            * scale_factor
        )
        probs = jnp.exp(scores - logsum_block[..., None])
        prob_grad = jnp.einsum(
            "qhd,khd->hqk", grad_block, values, preferred_element_type=jnp.float32
        )
        inner = jnp.sum(probs * prob_grad, axis=-1, keepdims=True)
        score_grad = (probs * (prob_grad - inner)).astype(jnp.bfloat16)
        query_grad = (
            jnp.einsum("hqk,khd->qhd", score_grad, keys, preferred_element_type=jnp.float32)
            * scale_factor
        )
        key_sum = (
            key_sum
            + jnp.einsum(
                "hqk,qhd->khd", score_grad, query_block, preferred_element_type=jnp.float32
            )
            * scale_factor
        )
        value_sum = value_sum + jnp.einsum(
            "hqk,qhd->khd",
            probs.astype(jnp.bfloat16),
            grad_block,
            preferred_element_type=jnp.float32,
        )
        return ((key_sum, value_sum), query_grad)

    empty = jnp.zeros(keys.shape, jnp.float32)
    (key_grad, value_grad), query_grads = lax.scan(
        one_block,
        (empty, empty),
        (queries.reshape(block_shape), grad_mixed.reshape(block_shape), logsum),
    )
    return (query_grads.reshape(queries.shape), key_grad, value_grad)


def body_by_heads(
    latent,
    condition,
    cotangent,
    mod_weight,
    mod_bias,
    head_weight,
    head_bias,
    mix_weight,
    branch_bias,
    up_weight,
    up_bias,
    down_weight,
):
    per_group = latent.shape[0] // MICRO
    seq_len = SEQ
    head_cols = head_weight.shape[2]
    local_heads = head_cols // HEAD_DIM
    block_rows = min(512, seq_len)
    scale_factor = HEAD_DIM ** (-0.5)
    attend_fwd = jax.vmap(partial(attend_forward, block_rows=block_rows, scale_factor=scale_factor))
    attend_bwd = jax.vmap(
        partial(attend_backward, block_rows=block_rows, scale_factor=scale_factor)
    )
    head_bias_f = head_bias.astype(jnp.float32)
    up_bias_f = up_bias.astype(jnp.float32)
    mod_bias_f = mod_bias.astype(jnp.float32)
    branch_bias_f = branch_bias.astype(jnp.float32)
    bias_totals = (
        jnp.zeros(mod_bias.shape, jnp.float32),
        jnp.zeros(head_bias.shape, jnp.float32),
        jnp.zeros(up_bias.shape, jnp.float32),
        jnp.zeros(branch_bias.shape, jnp.float32),
    )
    grad_sums = None
    block_outs = []
    latent_grads = []
    condition_grads = []
    for micro_step in range(MICRO):
        row_start = micro_step * per_group
        row_stop = row_start + per_group
        mod_full, head_full, mix_full, up_full, down_full = fetch_weights(
            mod_weight, head_weight, mix_weight, up_weight, down_weight
        )
        lat_part = latent[row_start:row_stop].astype(jnp.float32)
        cond_part = condition[row_start:row_stop].astype(jnp.float32)
        cond_act, silu_back = jax.vjp(jax.nn.silu, cond_part)
        cond_low = cond_act.astype(jnp.bfloat16)
        mod_cols = (
            jnp.einsum("bd,dkc->bkc", cond_low, mod_full, preferred_element_type=jnp.float32)
            + mod_bias_f
        )
        mod_all, bias_all = (
            lax.all_gather(mod_cols, "tensor", axis=2, tiled=True),
            lax.all_gather(branch_bias_f, "tensor", axis=1, tiled=True),
        )
        norm_first, first_back = jax.vjp(modulate, lat_part, mod_all[:, 0], mod_all[:, 1])
        attn_rows = lax.all_gather(norm_first.astype(jnp.bfloat16), "tensor", axis=1, tiled=True)
        projected = jnp.einsum(
            "bsd,dkc->bskc", attn_rows, head_full, preferred_element_type=jnp.float32
        )
        head_shape = (per_group, seq_len, local_heads, HEAD_DIM)
        query_heads = (projected[:, :, 0] + head_bias_f[0]).astype(jnp.bfloat16).reshape(head_shape)
        key_heads = projected[:, :, 1].astype(jnp.bfloat16).reshape(head_shape)
        value_heads = (projected[:, :, 2] + head_bias_f[1]).astype(jnp.bfloat16).reshape(head_shape)
        mixed, logsum = attend_fwd(query_heads, key_heads, value_heads)
        mixed_low = mixed.reshape(per_group, seq_len, head_cols).astype(jnp.bfloat16)
        attn_part = jnp.einsum(
            "bsc,cd->bsd", mixed_low, mix_full, preferred_element_type=jnp.float32
        )
        attn_local = lax.psum_scatter(
            attn_part.astype(jnp.bfloat16), "tensor", scatter_dimension=1, tiled=True
        ).astype(jnp.float32)
        gate_attn = mod_all[:, 2][:, None, :]
        gate_mlp = mod_all[:, 5][:, None, :]
        first = lat_part + gate_attn * (attn_local + bias_all[0])
        norm_second, second_back = jax.vjp(modulate, first, mod_all[:, 3], mod_all[:, 4])
        mlp_rows = lax.all_gather(norm_second.astype(jnp.bfloat16), "tensor", axis=1, tiled=True)
        pre_act = (
            jnp.einsum("bsd,df->bsf", mlp_rows, up_full, preferred_element_type=jnp.float32)
            + up_bias_f
        )
        act_value, gelu_back = jax.vjp(gelu_tanh, pre_act)
        act_low = act_value.astype(jnp.bfloat16)
        mlp_part = jnp.einsum("bsf,fd->bsd", act_low, down_full, preferred_element_type=jnp.float32)
        mlp_local = lax.psum_scatter(
            mlp_part.astype(jnp.bfloat16), "tensor", scatter_dimension=1, tiled=True
        ).astype(jnp.float32)
        block_outs.append((first + gate_mlp * (mlp_local + bias_all[1])).astype(jnp.bfloat16))
        mod_full, head_full, mix_full, up_full, down_full = fetch_weights(
            mod_weight, head_weight, mix_weight, up_weight, down_weight
        )
        upstream = cotangent[row_start:row_stop].astype(jnp.float32)
        gate_m_grad = jnp.sum(upstream * (mlp_local + bias_all[1]), axis=1)
        tail_bias_grad = jnp.sum(gate_mlp * upstream, axis=(0, 1))
        mlp_grad = lax.all_gather(
            (gate_mlp * upstream).astype(jnp.bfloat16), "tensor", axis=1, tiled=True
        )
        down_grad = jnp.einsum("bsf,bsd->fd", act_low, mlp_grad, preferred_element_type=jnp.float32)
        act_grad = jnp.einsum(
            "bsd,fd->bsf", mlp_grad, down_full, preferred_element_type=jnp.float32
        )
        pre_grad = gelu_back(act_grad)[0].astype(jnp.bfloat16)
        up_bias_term = jnp.sum(pre_grad, axis=(0, 1), dtype=jnp.float32)
        up_grad = jnp.einsum("bsd,bsf->df", mlp_rows, pre_grad, preferred_element_type=jnp.float32)
        mlp_in_part = jnp.einsum(
            "bsf,df->bsd", pre_grad, up_full, preferred_element_type=jnp.float32
        )
        mlp_in_grad = lax.psum_scatter(
            mlp_in_part.astype(jnp.bfloat16), "tensor", scatter_dimension=1, tiled=True
        ).astype(jnp.float32)
        first_grad, shift_m_grad, scale_m_grad = second_back(mlp_in_grad)
        first_grad = first_grad + upstream
        gate_a_grad = jnp.sum(first_grad * (attn_local + bias_all[0]), axis=1)
        attn_bias_grad = jnp.sum(gate_attn * first_grad, axis=(0, 1))
        attn_branch_grad = (gate_attn * first_grad).astype(jnp.bfloat16)
        attn_grad = lax.all_gather(attn_branch_grad, "tensor", axis=1, tiled=True)
        mix_grad = jnp.einsum(
            "bsc,bsd->cd", mixed_low, attn_grad, preferred_element_type=jnp.float32
        )
        mixed_grad = jnp.einsum(
            "bsd,cd->bsc", attn_grad, mix_full, preferred_element_type=jnp.float32
        ).astype(jnp.bfloat16)
        query_grad, key_grad, value_grad = attend_bwd(
            query_heads, key_heads, value_heads, mixed_grad.reshape(head_shape), logsum
        )
        head_grads = (
            jnp.stack([query_grad, key_grad, value_grad], axis=2)
            .reshape(per_group, seq_len, 3, head_cols)
            .astype(jnp.bfloat16)
        )
        head_bias_term = jnp.sum(head_grads[:, :, 0::2], axis=(0, 1), dtype=jnp.float32)
        head_grad = jnp.einsum(
            "bsd,bskc->dkc", attn_rows, head_grads, preferred_element_type=jnp.float32
        )
        attn_in_part = jnp.einsum(
            "bskc,dkc->bsd", head_grads, head_full, preferred_element_type=jnp.float32
        )
        attn_in_grad = lax.psum_scatter(
            attn_in_part.astype(jnp.bfloat16), "tensor", scatter_dimension=1, tiled=True
        ).astype(jnp.float32)
        lat_grad, shift_a_grad, scale_a_grad = first_back(attn_in_grad)
        latent_grads.append((lat_grad + first_grad).astype(jnp.bfloat16))
        mod_terms = jnp.stack(
            [shift_a_grad, scale_a_grad, gate_a_grad, shift_m_grad, scale_m_grad, gate_m_grad],
            axis=1,
        )
        branch_terms = jnp.stack([attn_bias_grad, tail_bias_grad], axis=0)
        mod_grad_cols, branch_grad_cols = (
            lax.psum_scatter(
                mod_terms.astype(jnp.bfloat16), "tensor", scatter_dimension=2, tiled=True
            ).astype(jnp.float32),
            lax.psum_scatter(
                branch_terms.astype(jnp.bfloat16), "tensor", scatter_dimension=1, tiled=True
            ).astype(jnp.float32),
        )
        mod_grad_low = mod_grad_cols.astype(jnp.bfloat16)
        mod_grad = jnp.einsum(
            "bd,bkc->dkc", cond_low, mod_grad_low, preferred_element_type=jnp.float32
        )
        mod_bias_term = jnp.sum(mod_grad_low, axis=0, dtype=jnp.float32)
        cond_part_grad = jnp.einsum(
            "bkc,dkc->bd", mod_grad_low, mod_full, preferred_element_type=jnp.float32
        )
        cond_act_grad = lax.psum(cond_part_grad, "tensor")
        condition_grads.append(silu_back(cond_act_grad)[0])
        bias_totals = (
            bias_totals[0] + mod_bias_term,
            bias_totals[1] + head_bias_term,
            bias_totals[2] + up_bias_term,
            bias_totals[3] + branch_grad_cols,
        )
        weight_terms = (mod_grad, head_grad, mix_grad, up_grad, down_grad)
        grad_sums = (
            weight_terms if grad_sums is None else jax.tree.map(jnp.add, grad_sums, weight_terms)
        )
    grad_sums = reduce_weights(grad_sums)
    bias_sums = lax.psum((bias_totals[0], bias_totals[1], bias_totals[2], bias_totals[3]), "dp")
    return (
        jnp.concatenate(block_outs, axis=0),
        jnp.concatenate(latent_grads, axis=0),
        jnp.concatenate(condition_grads, axis=0),
        grad_sums[0],
        bias_sums[0],
        grad_sums[1],
        bias_sums[1],
        grad_sums[2],
        bias_sums[3],
        grad_sums[3],
        bias_sums[2],
        grad_sums[4],
    )


def head_window(col, width):
    start = jnp.minimum(col // 128 * 128, width - WINDOW)
    return pl.multiple_of(start, 128), col - start


def head_members(heads, width):
    col = lax.broadcasted_iota(jnp.int32, (heads, width), 1)
    first = lax.broadcasted_iota(jnp.int32, (heads, width), 0) * HEAD_DIM
    return jnp.where((col >= first) & (col < first + HEAD_DIM), 1.0, 0.0).astype(bf16)


def attn_fwd_kernel(q_ref, k_ref, v_ref, o_ref, lse_ref, ot_ref, *, blk, heads):
    seq, width = q_ref.shape[1:]
    c = HEAD_DIM ** -0.5 * LOG2E
    ot_ref[...] = v_ref[0].astype(f32).T
    lanes = lax.broadcasted_iota(jnp.int32, (blk, WINDOW), 1)
    ones = jnp.ones((8, seq), f32)
    member = head_members(heads, width)
    longest = [
        jnp.max(
            lax.dot_general(member, ref[0] * ref[0], NT, preferred_element_type=f32),
            axis=1,
            keepdims=True,
        )
        for ref in (q_ref, k_ref)
    ]
    bound = longest[0] * longest[1] * (1.1 * c * c)
    which = lax.broadcasted_iota(jnp.int32, bound.shape, 0) // 2

    def pair(i, carry):
        def run(shifted):
            steps = [(2 * i + odd, b) for odd in range(2) for b in range(seq // blk)]

            def scores(head, b):
                start, off = head_window(head * HEAD_DIM, width)
                mask = (lanes >= off) & (lanes < off + HEAD_DIM)
                qb = q_ref[0, b * blk : (b + 1) * blk, pl.ds(start, WINDOW)]
                qb = jnp.where(mask, qb, jnp.zeros_like(qb))
                return lax.dot_general(
                    k_ref[0, :, pl.ds(start, WINDOW)], qb, NT, preferred_element_type=f32
                )

            st = scores(*steps[0])
            vt = None
            for n, (head, b) in enumerate(steps):
                after = scores(*steps[n + 1]) if n + 1 < len(steps) else None
                mine = pl.ds(pl.multiple_of(head * HEAD_DIM, 8), HEAD_DIM)
                if b == 0:
                    vt = jnp.concatenate([ot_ref[mine, :], ones], axis=0).astype(bf16)
                rows = slice(b * blk, (b + 1) * blk)
                if shifted:
                    m = jnp.max(st, axis=0, keepdims=True)
                    p = jnp.exp2((st - m) * c).astype(bf16)
                else:
                    p = jnp.exp2(st * c).astype(bf16)
                ot = jnp.dot(vt, p, preferred_element_type=f32)
                l = ot[HEAD_DIM : HEAD_DIM + 1]
                ot_ref[mine, rows] = ot[:HEAD_DIM] * (1.0 / l)
                lse_ref[0, 0, pl.ds(head, 1), rows] = jnp.log2(l) + m * c if shifted else jnp.log2(l)
                st = after

        small = jnp.max(jnp.where(which == i, bound, 0.0)) < 85.0 * 85.0
        pl.when(small)(lambda: run(False))
        pl.when(jnp.logical_not(small))(lambda: run(True))
        return carry

    lax.fori_loop(0, heads // 2, pair, 0)
    o_ref[0] = ot_ref[...].T.astype(bf16)


def attn_fwd(qkv, heads, blk=256):
    n, seq, wide = qkv.shape
    width = wide // 6
    spec = lambda j: pl.BlockSpec((1, seq, width), lambda b, h: (b, 0, 3 * h + j))
    return pl.pallas_call(
        partial(attn_fwd_kernel, blk=blk, heads=heads),
        grid=(n, 2),
        in_specs=[spec(0), spec(1), spec(2)],
        out_specs=[
            pl.BlockSpec((1, seq, width), lambda b, h: (b, 0, h)),
            pl.BlockSpec((1, 1, heads, seq), lambda b, h: (b, h, 0, 0)),
        ],
        out_shape=[
            jax.ShapeDtypeStruct((n, seq, 2 * width), bf16),
            jax.ShapeDtypeStruct((n, 2, heads, seq), f32),
        ],
        scratch_shapes=[pltpu.VMEM((width, seq), f32)],
        compiler_params=pltpu.CompilerParams(vmem_limit_bytes=56 << 20),
        cost_estimate=pl.CostEstimate(
            flops=8 * n * seq * seq * width,
            bytes_accessed=16 * n * seq * width,
            transcendentals=2 * n * heads * seq * seq,
        ),
        name="attention_forward",
    )(qkv, qkv, qkv)


def attn_bwd_kernel(
    q_ref, k_ref, v_ref, do_ref, o_ref, lse_ref, dqkv_ref, sum_ref,
    dqt_ref, delta_ref, pt_ref, dst_ref, *, blk, heads
):
    seq, width = q_ref.shape[1:]
    scale = HEAD_DIM ** -0.5
    c = scale * LOG2E
    dqt_ref[...] = k_ref[0].astype(f32).T
    prod = do_ref[0].astype(f32) * o_ref[0].astype(f32)
    high = prod.astype(bf16)
    low = (prod - high.astype(f32)).astype(bf16)
    member = head_members(heads, width)
    delta_ref[...] = lax.dot_general(member, high, NT, preferred_element_type=f32) + lax.dot_general(
        member, low, NT, preferred_element_type=f32
    )
    lanes = lax.broadcasted_iota(jnp.int32, (seq, WINDOW), 1)
    edge = heads * HEAD_DIM // 128 * 128
    for part in (1, 2):
        dqkv_ref[0, :, part * width + edge : (part + 1) * width] = jnp.zeros((seq, width - edge), bf16)

    def one(head, carry):
        start, off = head_window(head * HEAD_DIM, width)
        window = pl.ds(start, WINDOW)
        mask = (lanes >= off) & (lanes < off + HEAD_DIM)
        keys = k_ref[0, :, window]
        values = v_ref[0, :, window]
        qm = q_ref[0, :, window]
        qm = jnp.where(mask, qm, jnp.zeros_like(qm))
        dom = do_ref[0, :, window]
        dom = jnp.where(mask, dom, jnp.zeros_like(dom))
        mine = pl.ds(pl.multiple_of(head * HEAD_DIM, 8), HEAD_DIM)
        kt = dqt_ref[mine, :].astype(bf16)
        def products(b):
            rows = slice(b * blk, (b + 1) * blk)
            st = lax.dot_general(keys, qm[rows], NT, preferred_element_type=f32)
            return st, lax.dot_general(values, dom[rows], NT, preferred_element_type=f32)

        now = products(0)
        for b in range(seq // blk):
            rows = slice(b * blk, (b + 1) * blk)
            later = products(b + 1) if b + 1 < seq // blk else None
            st, dpt = now
            p = jnp.exp2(st * c - lse_ref[0, 0, pl.ds(head, 1), rows])
            dst = (p * (dpt - delta_ref[pl.ds(head, 1), rows])).astype(bf16)
            pt_ref[:, rows] = p.astype(bf16)
            dst_ref[:, rows] = dst
            dqt_ref[mine, rows] = jnp.dot(kt, dst, preferred_element_type=f32) * scale
            now = later
        dk = jnp.dot(dst_ref[...], qm, preferred_element_type=f32) * scale
        dv = jnp.dot(pt_ref[...], dom, preferred_element_type=f32)
        kwin = pl.ds(pl.multiple_of(width + start, 128), WINDOW)
        vwin = pl.ds(pl.multiple_of(2 * width + start, 128), WINDOW)
        dqkv_ref[0, :, kwin] = jnp.where(mask, dk.astype(bf16), dqkv_ref[0, :, kwin])
        dqkv_ref[0, :, vwin] = jnp.where(mask, dv.astype(bf16), dqkv_ref[0, :, vwin])
        return carry

    lax.fori_loop(0, heads, one, 0)
    dqkv_ref[0, :, :width] = dqt_ref[...].T.astype(bf16)
    sum_ref[0, 0] = jnp.sum(dqkv_ref[0].astype(f32), axis=0, keepdims=True)


def attn_bwd(qkv, grad, mixed, lse, heads, blk=256):
    n, seq, wide = qkv.shape
    width = wide // 6
    spec = lambda j: pl.BlockSpec((1, seq, width), lambda b, h: (b, 0, 3 * h + j))
    out = pl.BlockSpec((1, seq, width), lambda b, h: (b, 0, h))
    return pl.pallas_call(
        partial(attn_bwd_kernel, blk=blk, heads=heads),
        grid=(n, 2),
        in_specs=[
            spec(0), spec(1), spec(2), out, out,
            pl.BlockSpec((1, 1, heads, seq), lambda b, h: (b, h, 0, 0)),
        ],
        out_specs=[
            pl.BlockSpec((1, seq, 3 * width), lambda b, h: (b, 0, h)),
            pl.BlockSpec((1, 1, 1, 3 * width), lambda b, h: (b, h, 0, 0)),
        ],
        out_shape=[
            jax.ShapeDtypeStruct(qkv.shape, bf16),
            jax.ShapeDtypeStruct((n, 2, 1, 3 * width), f32),
        ],
        scratch_shapes=[
            pltpu.VMEM((width, seq), f32),
            pltpu.VMEM((heads, seq), f32),
            pltpu.VMEM((seq, seq), bf16),
            pltpu.VMEM((seq, seq), bf16),
        ],
        compiler_params=pltpu.CompilerParams(vmem_limit_bytes=56 << 20),
        cost_estimate=pl.CostEstimate(flops=0, bytes_accessed=0, transcendentals=0),
        name="attention_backward",
    )(qkv, qkv, qkv, grad, mixed, lse)


def gelu_with_slope(u):
    k, cubic = 0.7978845608028654, 0.7978845608028654 * 0.044715
    square = u * u
    half = 0.5 + 0.5 * jnp.tanh(u * (k + cubic * square))
    value = u * half
    return value, half + value * (1.0 - half) * (2.0 * k + 6.0 * cubic * square)


def tile_steps(rows, cols, sub_rows, sub_cols):
    return [
        (slice(i, i + sub_rows), slice(j, j + sub_cols))
        for j in range(0, cols, sub_cols)
        for i in range(0, rows, sub_rows)
    ]


def up_forward_kernel(x_ref, w_ref, b_ref, act_ref, slope_ref):
    steps = tile_steps(*act_ref.shape, 256, 256)
    product = lambda r, c: jnp.dot(x_ref[r, :], w_ref[:, c], preferred_element_type=f32)
    now = product(*steps[0])
    for n, (r, c) in enumerate(steps):
        later = product(*steps[n + 1]) if n + 1 < len(steps) else None
        value, slope = gelu_with_slope(now + b_ref[:, c])
        act_ref[r, c] = value.astype(bf16)
        slope_ref[r, c] = slope.astype(bf16)
        now = later


def up_forward(x, w, bias):
    count, seq, depth = x.shape
    hidden = bias.shape[0]
    rows, cols = 1024, hidden // 3
    tile = pl.BlockSpec((rows, cols), lambda j, i: (i, j))
    act, slope = pl.pallas_call(
        up_forward_kernel,
        grid=(hidden // cols, count * seq // rows),
        in_specs=[
            pl.BlockSpec((rows, depth), lambda j, i: (i, 0)),
            pl.BlockSpec((depth, cols), lambda j, i: (0, j)),
            pl.BlockSpec((1, cols), lambda j, i: (0, j)),
        ],
        out_specs=[tile, tile],
        out_shape=[jax.ShapeDtypeStruct((count * seq, hidden), bf16)] * 2,
        compiler_params=pltpu.CompilerParams(vmem_limit_bytes=56 << 20),
        cost_estimate=pl.CostEstimate(
            flops=2 * count * seq * depth * hidden,
            bytes_accessed=4 * count * seq * hidden,
            transcendentals=count * seq * hidden,
        ),
        name="up_forward",
    )(x.reshape(count * seq, depth), w, bias.reshape(1, hidden))
    return act.reshape(count, seq, hidden), slope.reshape(count, seq, hidden)


def down_backward_kernel(g_ref, w_ref, slope_ref, out_ref, sum_ref):
    steps = tile_steps(*out_ref.shape, out_ref.shape[0], 256)
    product = lambda r, c: jnp.dot(g_ref[r, :], w_ref[:, c], preferred_element_type=f32)

    @pl.when(pl.program_id(1) == 0)
    def _():
        sum_ref[...] = jnp.zeros_like(sum_ref)

    now = product(*steps[0])
    for n, (r, c) in enumerate(steps):
        later = product(*steps[n + 1]) if n + 1 < len(steps) else None
        grad = (now * slope_ref[r, c].astype(f32)).astype(bf16)
        out_ref[r, c] = grad
        sum_ref[:, c] += jnp.sum(grad.astype(f32), axis=0, keepdims=True)
        now = later


def down_backward(g, w, slope):
    count, seq, depth = g.shape
    hidden = slope.shape[2]
    rows, cols = 1024, hidden // 3
    tile = pl.BlockSpec((rows, cols), lambda j, i: (i, j))
    grad, total = pl.pallas_call(
        down_backward_kernel,
        grid=(hidden // cols, count * seq // rows),
        in_specs=[
            pl.BlockSpec((rows, depth), lambda j, i: (i, 0)),
            pl.BlockSpec((depth, cols), lambda j, i: (0, j)),
            tile,
        ],
        out_specs=[tile, pl.BlockSpec((1, cols), lambda j, i: (0, j))],
        out_shape=[
            jax.ShapeDtypeStruct((count * seq, hidden), bf16),
            jax.ShapeDtypeStruct((1, hidden), f32),
        ],
        compiler_params=pltpu.CompilerParams(vmem_limit_bytes=56 << 20),
        cost_estimate=pl.CostEstimate(
            flops=2 * count * seq * depth * hidden,
            bytes_accessed=4 * count * seq * hidden,
            transcendentals=0,
        ),
        name="down_backward",
    )(g.reshape(count * seq, depth), w, slope.reshape(count * seq, hidden))
    return grad.reshape(count, seq, hidden), total[0]


CORES = 2
ROWS = 2


def place(rank):
    return rank // (ROWS * CORES), rank // CORES % ROWS, rank % CORES


def rank_of(z, y, core):
    return (z * ROWS + y) * CORES + core


def greet(side):
    rank = lax.axis_index("dp")
    groups = lax.axis_size("dp")
    barrier = pltpu.get_barrier_semaphore()
    for step in range(1, groups):
        pl.semaphore_signal(barrier, inc=1, device_id={"dp": lax.rem(rank + step, groups)}, device_id_type=MESH)
    pl.semaphore_signal(barrier, inc=1, device_id={"tensor": 1 - side}, device_id_type=MESH)
    pl.semaphore_wait(barrier, groups)


class Spread:
    def __init__(self, source, out, sends, arrivals, lanes=None):
        self.source, self.out, self.sends, self.arrivals = source, out, sends, arrivals
        self.lanes = lanes
        self.rank = lax.axis_index("dp")
        self.z, self.y, self.core = place(self.rank)
        self.depth = lax.axis_size("dp") // (ROWS * CORES)
        self.started = []

    def block(self, origin):
        return self.out.at[origin] if self.lanes is None else self.out.at[origin, :, self.lanes]

    def copy(self, origin, edge, target, source=None):
        return pltpu.make_async_remote_copy(
            src_ref=self.block(origin) if source is None else source,
            dst_ref=self.block(origin),
            send_sem=self.sends.at[origin, edge],
            recv_sem=self.arrivals.at[origin],
            device_id={"dp": target},
            device_id_type=MESH,
        )

    def send(self, origin, edge, target, source=None, when=None):
        sent = self.copy(origin, edge, target, source)
        if when is None:
            sent.start()
        else:
            pl.when(when)(sent.start)
        self.started.append((sent, when))

    def arrive(self, origin):
        self.copy(origin, 0, rank_of(self.z, 1 - self.y, self.core)).wait_recv()

    def up(self):
        return rank_of(self.z + 1, self.y, self.core)

    def down(self):
        return rank_of(self.z - 1, self.y, self.core)

    def across(self):
        return rank_of(self.z, 1 - self.y, self.core)

    def sibling(self):
        return rank_of(self.z, self.y, 1 - self.core)

    def begin(self):
        rank, source = self.rank, self.source
        self.send(rank, 0, self.up(), source, self.z < self.depth - 1)
        self.send(rank, 3, self.down(), source, self.z > 0)
        self.send(rank, 1, self.across(), source)
        self.send(rank, 2, self.sibling(), source)

    def relay(self, hop):
        for toward, there in ((1, self.z >= hop), (-1, self.z + hop < self.depth)):
            origin = rank_of(self.z - toward * hop, self.y, self.core)
            further = (self.z < self.depth - 1) if toward > 0 else (self.z > 0)
            pl.when(there)(lambda: self.arrive(origin))
            self.send(
                origin, 0, self.up() if toward > 0 else self.down(), when=there & further
            )
            self.send(origin, 1, self.across(), when=there)
            self.send(origin, 2, self.sibling(), when=there)

    def relay_across(self, hop):
        for toward, there in ((1, self.z >= hop), (-1, self.z + hop < self.depth)):
            if hop == 0 and toward < 0:
                continue
            origin = rank_of(self.z - toward * hop, 1 - self.y, self.core)
            pl.when(there)(lambda: self.arrive(origin))
            self.send(origin, 2, self.sibling(), when=there)

    def finish(self):
        for z in range(self.depth):
            for y in range(ROWS):
                self.arrive(rank_of(z, y, 1 - self.core))
        for sent, when in self.started:
            if when is None:
                sent.wait_send()
            else:
                pl.when(when)(sent.wait_send)


class DirectSpread:
    def __init__(self, out, sends, arrivals):
        self.out, self.sends, self.arrivals = out, sends, arrivals
        self.rank = lax.axis_index("dp")
        self.groups = lax.axis_size("dp")
        self.sibling = self.rank + 1 - 2 * lax.rem(self.rank, CORES)
        self.steps = range(CORES, self.groups, CORES)

    def copy(self, origin, send, target):
        return pltpu.make_async_remote_copy(
            src_ref=self.out.at[origin],
            dst_ref=self.out.at[origin],
            send_sem=self.sends.at[send],
            recv_sem=self.arrivals.at[origin],
            device_id={"dp": target},
            device_id_type=MESH,
        )

    def peer(self, step):
        return lax.rem(self.rank + step, self.groups)

    def begin(self):
        for step in self.steps:
            self.copy(self.rank, step, self.peer(step)).start()
        self.copy(self.rank, 0, self.sibling).start()

    def relay(self):
        for step in self.steps:
            origin = self.peer(step)
            self.copy(origin, step, origin).wait_recv()
            self.copy(origin, step + 1, self.sibling).start()

    def finish(self):
        for step in range(0, self.groups, CORES):
            origin = lax.rem(self.sibling + step, self.groups)
            self.copy(origin, 0, self.sibling).wait_recv()
        for step in self.steps:
            self.copy(self.rank, step, self.peer(step)).wait_send()
            self.copy(self.peer(step), step + 1, self.sibling).wait_send()
        self.copy(self.rank, 0, self.sibling).wait_send()


class Exchange:
    def __init__(self, source, out, sends, arrivals):
        self.source, self.out, self.sends, self.arrivals = source, out, sends, arrivals
        self.rank = lax.axis_index("dp")
        self.groups = lax.axis_size("dp")

    def copy(self, step):
        peer = lax.rem(self.rank + step, self.groups)
        return pltpu.make_async_remote_copy(
            src_ref=self.source.at[peer],
            dst_ref=self.out.at[self.rank],
            send_sem=self.sends.at[step],
            recv_sem=self.arrivals.at[self.rank],
            device_id={"dp": peer},
            device_id_type=MESH,
        )

    def begin(self):
        self.out[self.rank] = self.source[self.rank]
        for step in range(1, self.groups):
            self.copy(step).start()

    def finish(self):
        for step in range(1, self.groups):
            peer = lax.rem(self.rank + step, self.groups)
            pltpu.make_async_remote_copy(
                src_ref=self.source.at[peer],
                dst_ref=self.out.at[peer],
                send_sem=self.sends.at[step],
                recv_sem=self.arrivals.at[peer],
                device_id={"dp": peer},
                device_id_type=MESH,
            ).wait_recv()

    def drain(self):
        for step in range(1, self.groups):
            self.copy(step).wait_send()


def to_partner(source, target, side, sends, arrivals, k):
    return pltpu.make_async_remote_copy(
        src_ref=source,
        dst_ref=target,
        send_sem=sends.at[k],
        recv_sem=arrivals.at[k],
        device_id={"tensor": 1 - side},
        device_id_type=MESH,
    )


def opening_kernel(
    cond_ref, mod_w_ref, mod_bias_ref, bias_ref, head_ref, rest_ref, latent_ref,
    head_out, rest_out, latent_out, mod_out, cond_out, bias_out,
    part_ref, mod_in,
    x_send, x_recv, c_send, c_recv, m_send, m_recv, h_send, h_recv, local_sem,
):
    side = lax.axis_index("tensor")
    rank = lax.axis_index("dp")
    greet(side)
    conds = Exchange(cond_ref, cond_out, c_send, c_recv)
    conds.begin()
    lanes = head_ref.shape[1]
    mine = Spread(head_ref, head_out, h_send.at[0], h_recv.at[0], pl.ds(0, lanes))
    other = Spread(None, head_out, h_send.at[1], h_recv.at[1], pl.ds(lanes, lanes))
    head_swap = to_partner(head_ref, other.block(rank), side, x_send, x_recv, 0)
    head_swap.start()
    mine.begin()
    biases = to_partner(bias_ref, bias_out, side, x_send, x_recv, 3)
    biases.start()
    rest = to_partner(rest_ref, rest_out, side, x_send, x_recv, 1)
    rest.start()
    own = latent_out.shape[0]
    latents = to_partner(
        latent_ref.at[pl.ds((1 - side) * own, own)], latent_out, side, x_send, x_recv, 4
    )
    latents.start()
    keep = pltpu.make_async_copy(head_ref, mine.block(rank), local_sem)
    keep.start()
    conds.finish()
    groups, rows, lanes = cond_out.shape
    half = mod_bias_ref.shape[1]
    low = cond_out[...].reshape(groups * rows, lanes).astype(bf16)
    front = lax.broadcasted_iota(jnp.int32, (groups * rows, half), 0) % rows < rows // 2
    part_ref[...] = jnp.where(
        front,
        jnp.dot(low, mod_w_ref[0], preferred_element_type=f32),
        jnp.dot(low, mod_w_ref[1], preferred_element_type=f32),
    ).reshape(groups, rows, half)
    mods = Exchange(part_ref, mod_in, m_send, m_recv)
    mods.begin()
    head_swap.wait_recv()
    other.begin()
    mine.relay(1)
    mods.finish()
    mod_out[0] = jnp.sum(mod_in[...], axis=0) + mod_bias_ref[...]
    mod_swap = to_partner(mod_out.at[0], mod_out.at[1], side, x_send, x_recv, 2)
    mod_swap.start()
    other.relay(1)
    mine.relay_across(0)
    other.relay_across(0)
    depth = mine.depth
    for hop in range(2, depth):
        for s in (mine, other):
            s.relay(hop)
            s.relay_across(hop - 1)
    for s in (mine, other):
        s.relay_across(depth - 1)
    keep.wait()
    mine.finish()
    other.finish()
    mod_swap.wait()
    rest.wait()
    latents.wait()
    biases.wait()
    head_swap.wait_send()
    conds.drain()
    mods.drain()


def opening(cond_low, mod_weight, mod_bias, biases, head, rest, latent):
    groups = lax.axis_size("dp")
    count = cond_low.shape[0]
    depth = cond_low.shape[1] // groups
    half = mod_weight.shape[1] * mod_weight.shape[2] // 2
    blocks = cond_low.astype(f32).reshape(count, groups, depth).transpose(1, 0, 2)
    blocks = jnp.concatenate([blocks, blocks], axis=1)
    blocks = jnp.pad(blocks, ((0, 0), (0, 0), (0, 128 - depth)))
    weights = jnp.pad(mod_weight.reshape(depth, 2, half), ((0, 128 - depth), (0, 0), (0, 0))).transpose(1, 0, 2)
    bias = jnp.repeat(mod_bias.astype(f32).reshape(2, half), count, axis=0)
    dma = pltpu.SemaphoreType.DMA
    vmem = pl.BlockSpec(memory_space=pltpu.VMEM)
    anywhere = pl.BlockSpec(memory_space=pl.ANY)
    return pl.pallas_call(
        opening_kernel,
        in_specs=[vmem, vmem, vmem, vmem, anywhere, anywhere, anywhere],
        out_specs=[anywhere, anywhere, anywhere, vmem, vmem, vmem],
        out_shape=[
            jax.ShapeDtypeStruct((groups, depth, 2 * head.shape[1]), bf16),
            jax.ShapeDtypeStruct(rest.shape, bf16),
            jax.ShapeDtypeStruct((count // 2,) + latent.shape[1:], bf16),
            jax.ShapeDtypeStruct((2, 2 * count, half), f32),
            jax.ShapeDtypeStruct(blocks.shape, f32),
            jax.ShapeDtypeStruct(biases.shape, f32),
        ],
        scratch_shapes=[
            pltpu.VMEM((groups, 2 * count, half), f32),
            pltpu.VMEM((groups, 2 * count, half), f32),
            dma((5,)), dma((5,)),
            dma((groups,)), dma((groups,)),
            dma((groups,)), dma((groups,)),
            dma((2, groups, 4)), dma((2, groups)),
            dma,
        ],
        compiler_params=pltpu.CompilerParams(collective_id=0, has_side_effects=True, vmem_limit_bytes=32 << 20),
        cost_estimate=pl.CostEstimate(flops=0, bytes_accessed=0, transcendentals=0),
        name="opening",
    )(blocks, weights, bias, biases, head, rest, latent)


def closing_kernel(
    mod_ref, bias_ref, mod_w_ref, conds_ref,
    bias_out, cond_out, weight_out, sum_out,
    mod_out, mod_unit, bias_unit, bias_in, part_ref, cond_in,
    x_send, x_recv, m_send, m_recv, b_send, b_recv, c_send, c_recv,
):
    side = lax.axis_index("tensor")
    rank = lax.axis_index("dp")
    greet(side)
    rows = mod_ref.shape[1]
    mod_swap = to_partner(mod_ref.at[1], mod_unit.at[1], side, x_send, x_recv, 0)
    mod_swap.start()
    bias_swap = to_partner(bias_ref.at[1], bias_unit.at[1], side, x_send, x_recv, 1)
    bias_swap.start()
    mod_swap.wait()
    bias_swap.wait()
    mod_out[rank] = mod_ref[0] + mod_unit[1]
    bias_in[rank] = bias_ref[0] + bias_unit[1]
    mods = DirectSpread(mod_out, m_send, m_recv)
    biases = DirectSpread(bias_in, b_send, b_recv)
    mods.begin()
    biases.begin()
    mods.relay()
    biases.relay()
    mods.finish()
    groups, rows, half = mod_out.shape
    low = mod_out[...].reshape(groups * rows, half).astype(bf16)
    lanes = mod_w_ref.shape[1]
    front = lax.broadcasted_iota(jnp.int32, (groups * rows, lanes), 0) % rows < rows // 2
    part_ref[...] = jnp.where(
        front,
        lax.dot_general(low, mod_w_ref[0], NT, preferred_element_type=f32),
        lax.dot_general(low, mod_w_ref[1], NT, preferred_element_type=f32),
    ).reshape(groups, rows, lanes)
    conds = Exchange(part_ref, cond_in, c_send, c_recv)
    conds.begin()
    values = conds_ref[...].reshape(groups * rows, conds_ref.shape[2]).astype(bf16)
    ahead = lax.broadcasted_iota(jnp.int32, values.shape, 0) % rows < rows // 2
    depth, cols = weight_out.shape[1:]
    whole = jnp.sum(mod_out[...], axis=0)
    for k in range(2):
        picked = jnp.where(ahead == (k == 0), values, jnp.zeros_like(values))
        grad = lax.dot_general(picked, low, TN, preferred_element_type=f32)[:depth]
        total = jnp.sum(whole[k * (rows // 2) : (k + 1) * (rows // 2)], axis=0, keepdims=True)
        for j in range(3):
            weight_out[3 * k + j] = grad[:, j * cols : (j + 1) * cols]
            sum_out[3 * k + j] = total[:, j * cols : (j + 1) * cols]
    biases.finish()
    bias_out[...] = jnp.sum(bias_in[...], axis=0)
    conds.finish()
    cond_out[0] = cond_in[...]
    cond_swap = to_partner(cond_out.at[0], cond_out.at[1], side, x_send, x_recv, 2)
    cond_swap.start()
    cond_swap.wait()
    conds.drain()


def closing(mod_pair, bias_pair, mod_weight, conds):
    groups = lax.axis_size("dp")
    rows, half = mod_pair.shape[1:]
    depth = mod_weight.shape[0]
    weights = jnp.pad(mod_weight.reshape(depth, 2, half), ((0, 128 - depth), (0, 0), (0, 0))).transpose(1, 0, 2)
    dma = pltpu.SemaphoreType.DMA
    vmem = pl.BlockSpec(memory_space=pltpu.VMEM)
    lines = bias_pair.shape[1]
    return pl.pallas_call(
        closing_kernel,
        in_specs=[vmem] * 4,
        out_specs=[vmem] * 4,
        out_shape=[
            jax.ShapeDtypeStruct((lines, 128), f32),
            jax.ShapeDtypeStruct((2, groups, rows, 128), f32),
            jax.ShapeDtypeStruct((6, depth, half // 3), f32),
            jax.ShapeDtypeStruct((6, 1, half // 3), f32),
        ],
        scratch_shapes=[
            pltpu.VMEM((groups, rows, half), f32),
            pltpu.VMEM((2, rows, half), f32),
            pltpu.VMEM((2, lines, 128), f32),
            pltpu.VMEM((groups, lines, 128), f32),
            pltpu.VMEM((groups, rows, 128), f32),
            pltpu.VMEM((groups, rows, 128), f32),
            dma((3,)), dma((3,)),
            dma((groups,)), dma((groups,)),
            dma((groups,)), dma((groups,)),
            dma((groups,)), dma((groups,)),
        ],
        compiler_params=pltpu.CompilerParams(collective_id=1, has_side_effects=True, vmem_limit_bytes=32 << 20),
        cost_estimate=pl.CostEstimate(flops=0, bytes_accessed=0, transcendentals=0),
        name="closing",
    )(mod_pair, bias_pair, weights, conds)


class Collect:
    def __init__(self, grads, totals, from_core, from_row, from_z, terms, row_out, z_out, *sems):
        self.grads, self.totals = grads, totals
        self.from_core, self.from_row, self.from_z = from_core, from_row, from_z
        self.terms, self.row_out, self.z_out = terms, row_out, z_out
        (self.core_send, self.core_recv, self.row_send, self.row_recv, self.z_send, self.z_recv, self.local) = sems
        self.rank = lax.axis_index("dp")
        self.z, self.y, self.core = place(self.rank)
        self.depth = lax.axis_size("dp") // (ROWS * CORES)
        self.pieces, _, _, self.width = from_core.shape
        self.outer = (self.z == 0) | (self.z == self.depth - 1)

    def lanes(self, n):
        return pl.ds(pl.multiple_of(n * self.width, 128), self.width)

    def block(self, n, rank):
        return self.grads.at[rank, :, self.lanes(n)]

    def level(self, k):
        falling = self.depth - 1 - k
        falling = falling - jnp.where(falling <= self.z, 1, 0)
        rising = k + jnp.where(k >= self.z, 1, 0)
        there = jnp.where(self.z < self.depth // 2, falling, rising)
        return jnp.where(k == self.depth - 1, self.z, there)

    def core_copy(self, n, level, y):
        k = level * ROWS + y
        return pltpu.make_async_remote_copy(
            src_ref=self.block(n, rank_of(level, y, 1 - self.core)),
            dst_ref=self.from_core.at[n, k],
            send_sem=self.core_send.at[n, k],
            recv_sem=self.core_recv.at[n, k],
            device_id={"dp": rank_of(self.z, self.y, 1 - self.core)},
            device_id_type=MESH,
        )

    def row_copy(self, n, k):
        level = self.level(k)
        return pltpu.make_async_remote_copy(
            src_ref=self.row_out.at[k],
            dst_ref=self.from_row.at[n, level],
            send_sem=self.row_send.at[n, k],
            recv_sem=self.row_recv.at[n, level],
            device_id={"dp": rank_of(self.z, 1 - self.y, self.core)},
            device_id_type=MESH,
        )

    def z_copy(self, n, k):
        level = self.level(k)
        above = jnp.where(level > self.z, 1, 0)
        return pltpu.make_async_remote_copy(
            src_ref=self.z_out.at[k],
            dst_ref=self.from_z.at[n, 1 - above, level],
            send_sem=self.z_send.at[n, k],
            recv_sem=self.z_recv.at[n, 1 - above, level],
            device_id={"dp": rank_of(self.z + 2 * above - 1, self.y, self.core)},
            device_id_type=MESH,
        )

    def z_arrival(self, n, way, level):
        return pltpu.make_async_remote_copy(
            src_ref=self.z_out.at[0],
            dst_ref=self.from_z.at[n, way, level],
            send_sem=self.z_send.at[n, 0],
            recv_sem=self.z_recv.at[n, way, level],
            device_id={"dp": rank_of(self.z, 1 - self.y, self.core)},
            device_id_type=MESH,
        )

    def each_core_copy(self, act):
        def some(i, carry):
            n, level = i // self.depth, self.level(i % self.depth)
            act(self.core_copy(n, level, 1 - self.y))
            act(self.core_copy(n, level, self.y))
            return carry

        lax.fori_loop(0, self.pieces * self.depth, some, 0)

    def begin(self):
        self.each_core_copy(lambda copy: copy.start())

    def fetches(self, kind, n, k):
        level = self.level(k)
        y = 1 - self.y if kind == "row" else self.y
        slot = k if kind == "row" else self.depth + k

        def get(j, ref):
            return pltpu.make_async_copy(ref, self.terms.at[slot, j], self.local.at[slot, j])

        found = [
            (get(0, self.block(n, rank_of(level, y, self.core))), None),
            (get(1, self.from_core.at[n, level * ROWS + y]), None),
        ]
        if kind == "z":
            below = (level >= self.z) & (self.z > 0)
            above = (level <= self.z) & (self.z < self.depth - 1)
            found.append((get(2, self.from_row.at[n, level]), None))
            found.append((get(3, self.from_z.at[n, 0, level]), below))
            found.append((get(4, self.from_z.at[n, 1, level]), above))
        return found

    def load(self, kind, n, k):
        level = self.level(k)
        y = 1 - self.y if kind == "row" else self.y
        self.core_copy(n, level, y).wait_recv()
        if kind == "z":
            self.row_copy(n, k).wait_recv()
        for j, (fetch, when) in enumerate(self.fetches(kind, n, k)):
            if when is None:
                fetch.start()
            else:

                def arrived(j=j, fetch=fetch):
                    self.z_arrival(n, j - 3, level).wait_recv()
                    fetch.start()

                pl.when(when)(arrived)

    def finish(self, kind, n, k, last=False):
        total = None
        slot = k if kind == "row" else self.depth + k
        for j, (fetch, when) in enumerate(self.fetches(kind, n, k)):
            if when is None:
                fetch.wait()
            else:
                pl.when(when)(fetch.wait)
            term = self.terms[slot, j].astype(f32)
            if when is not None:
                term = jnp.where(when, term, 0.0)
            total = term if total is None else total + term
        if last:
            self.totals[:, self.lanes(n)] = total
            return
        copy = self.row_copy if kind == "row" else self.z_copy
        out = self.row_out if kind == "row" else self.z_out
        pl.when(n > 0)(lambda: copy(n - 1, k).wait_send())
        out[k] = total.astype(bf16)
        copy(n, k).start()

    def units(self, r):
        found = []
        final = self.depth - 1
        valid = lambda n: (n >= 0) & (n < self.pieces)
        for k in range(self.depth):
            found.append((valid(r), "row", r, k, False))
        for k in range(final):
            age = jnp.where(self.outer, 2, 3 if k < final - 1 else 4)
            found.append((valid(r - age), "z", r - age, k, False))
        found.append((valid(r - 5), "z", r - 5, final, True))
        return found

    def rounds(self):
        return self.pieces + 5

    def load_round(self, r):
        for when, kind, n, k, _ in self.units(r):
            pl.when(when)(lambda kind=kind, n=n, k=k: self.load(kind, n, k))

    def finish_round(self, r):
        for when, kind, n, k, last in self.units(r):
            pl.when(when)(lambda kind=kind, n=n, k=k, last=last: self.finish(kind, n, k, last))

    def end(self):
        n = self.pieces - 1
        for k in range(self.depth):
            self.row_copy(n, k).wait_send()
        for k in range(self.depth - 1):
            self.z_copy(n, k).wait_send()
        self.each_core_copy(lambda copy: copy.wait_send())


def collect_shapes(pieces, width, groups, depth):
    levels = groups // (ROWS * CORES)
    dma = pltpu.SemaphoreType.DMA
    arrivals = [
        jax.ShapeDtypeStruct((pieces, levels * ROWS, depth, width), bf16),
        jax.ShapeDtypeStruct((pieces, levels, depth, width), bf16),
        jax.ShapeDtypeStruct((pieces, 2, levels, depth, width), bf16),
    ]
    scratch = [
        pltpu.VMEM((2 * levels, 5, depth, width), bf16),
        pltpu.VMEM((levels, depth, width), bf16),
        pltpu.VMEM((levels - 1, depth, width), bf16),
        dma((pieces, levels * ROWS)), dma((pieces, levels * ROWS)),
        dma((pieces, levels)), dma((pieces, levels)),
        dma((pieces, levels)), dma((pieces, 2, levels)),
        dma((2 * levels, 5)),
    ]
    return arrivals, scratch


TILE = 256


def latents_backward_kernel(
    dqkv_ref, w_ref, lat_ref, first_ref, scale_ref, grads_ref,
    out_ref, sums_ref, totals_ref, from_core, from_row, from_z,
    tiles, x_send, x_recv, kept, *collect,
):
    side = lax.axis_index("tensor")
    r = pl.program_id(0)
    engine = Collect(grads_ref, totals_ref, from_core, from_row, from_z, *collect)
    both, half_seq, _ = out_ref.shape
    count = both // 2
    per_half = half_seq // TILE
    sent = count * per_half

    def place_of(i):
        rows = pl.ds(pl.multiple_of(i % per_half * TILE, TILE), TILE)
        return out_ref.at[side * count + i // per_half, rows]

    def row_copy(i):
        return to_partner(tiles.at[i], place_of(i), side, x_send, x_recv, i)

    def keep_copy(i):
        return pltpu.make_async_copy(tiles.at[sent + i], place_of(i), kept.at[i])

    @pl.when(r == 0)
    def _():
        greet(side)
        engine.begin()
        sums_ref[...] = jnp.zeros_like(sums_ref)

    engine.load_round(r)

    @pl.when(r < 2 * sent)
    def _():
        grad = lax.dot_general(dqkv_ref[...], w_ref[...], NT, preferred_element_type=f32)
        norm, inverse = normed(lat_ref[...].astype(f32))
        latent = r % sent // per_half
        sums_ref[latent] += jnp.concatenate(
            [jnp.sum(grad, axis=0, keepdims=True), jnp.sum(grad * norm, axis=0, keepdims=True)], axis=0
        )
        back = normed_back(grad * (1.0 + scale_ref[0]), norm, inverse)
        tiles[r] = (first_ref[...] + back).astype(bf16)
        pl.when(r < sent)(lambda: row_copy(r).start())
        pl.when(r >= sent)(lambda: keep_copy(r - sent).start())

    engine.finish_round(r)

    @pl.when(r == pl.num_programs(0) - 1)
    def _():
        engine.end()
        for i in range(sent):
            row_copy(i).wait()
            keep_copy(i).wait()


def latents_backward(dqkv, w, lat, first_grad, scale, grads):
    count, seq, wide = dqkv.shape
    width = lat.shape[2]
    groups = lax.axis_size("dp")
    depth = grads.shape[0] // groups
    per_half = seq // 2 // TILE
    sent = count * per_half
    pieces, piece = 6, wide // 6
    arrivals, scratch = collect_shapes(pieces, piece, groups, depth)

    def tile(r):
        r = jnp.minimum(r, 2 * sent - 1)
        i = r % sent
        return i // per_half * 2 * per_half + i % per_half + jnp.where(r < sent, per_half, 0)

    rows = lambda cols: pl.BlockSpec((TILE, cols), lambda r: (tile(r), 0))
    anywhere = pl.BlockSpec(memory_space=pl.ANY)
    flat = lambda a: a.reshape(count * seq, a.shape[2])
    dma = pltpu.SemaphoreType.DMA
    return pl.pallas_call(
        latents_backward_kernel,
        grid=(max(pieces + 5, 2 * sent),),
        in_specs=[
            rows(wide),
            pl.BlockSpec((width, wide), lambda r: (0, 0), pipeline_mode=pl.Buffered(1)),
            rows(width),
            rows(width),
            pl.BlockSpec((1, 1, width), lambda r: (tile(r) // (2 * per_half), 0, 0)),
            anywhere,
        ],
        out_specs=[
            anywhere,
            pl.BlockSpec((count, 2, width), lambda r: (0, 0, 0)),
            pl.BlockSpec((depth, wide), lambda r: (0, 0)),
        ]
        + [anywhere] * 3,
        out_shape=[
            jax.ShapeDtypeStruct((2 * count, seq // 2, width), bf16),
            jax.ShapeDtypeStruct((count, 2, width), f32),
            jax.ShapeDtypeStruct((depth, wide), f32),
        ]
        + arrivals,
        scratch_shapes=[pltpu.VMEM((2 * sent, TILE, width), bf16), dma((sent,)), dma((sent,)), dma((sent,))]
        + scratch,
        compiler_params=pltpu.CompilerParams(
            collective_id=2, has_side_effects=True, vmem_limit_bytes=56 << 20
        ),
        cost_estimate=pl.CostEstimate(flops=0, bytes_accessed=0, transcendentals=0),
        name="latents_backward",
    )(flat(dqkv), w, flat(lat), flat(first_grad), scale, grads.reshape(groups, depth, wide))[:3]


def normed(values):
    centred = values - jnp.mean(values, axis=-1, keepdims=True)
    variance = jnp.mean(centred * centred, axis=-1, keepdims=True)
    inverse = lax.rsqrt(variance + EPSILON)
    return centred * inverse, inverse


def normed_back(grad, norm, inverse):
    return inverse * (
        grad
        - jnp.mean(grad, axis=-1, keepdims=True)
        - norm * jnp.mean(grad * norm, axis=-1, keepdims=True)
    )


def mm(spec, a, b):
    return jnp.einsum(spec, a, b, preferred_element_type=f32)


def body_by_latents(
    latent,
    condition,
    cotangent,
    mod_weight,
    mod_bias,
    head_weight,
    head_bias,
    mix_weight,
    branch_bias,
    up_weight,
    up_bias,
    down_weight,
):
    side = lax.axis_index("tensor")
    rank = lax.axis_index("dp")
    groups = lax.axis_size("dp")
    count, half_seq, width = latent.shape
    own = count // 2
    cols = width // 2
    depth = head_weight.shape[0]
    hidden = 2 * up_weight.shape[1]

    def swap(a):
        return lax.ppermute(a, "tensor", [(0, 1), (1, 0)])

    def in_order(mine, other, axis):
        return jnp.where(
            side == 0,
            jnp.concatenate([mine, other], axis=axis),
            jnp.concatenate([other, mine], axis=axis),
        )

    def own_latents(a, axis=0):
        return lax.dynamic_slice_in_dim(a, side * own, own, axis)

    def other_latents(a, axis=0):
        return lax.dynamic_slice_in_dim(a, (1 - side) * own, own, axis)

    def placed(a, arrived):
        mine = lax.broadcasted_iota(jnp.int32, (2, 1, 1, 1), 0) == side
        whole = jnp.where(mine, a[None, :, :half_seq], arrived[None])
        return whole.reshape(count, half_seq, width)

    cond_f = condition.astype(f32)
    cond_low = jax.nn.silu(cond_f).astype(bf16)
    heads = cols // HEAD_DIM
    room = -(-cols // 128) * 128

    def roomy(a):
        return jnp.pad(a, [(0, 0)] * (a.ndim - 1) + [(0, room - cols)])

    head_shard = roomy(head_weight).reshape(depth, 3 * room)
    shards = jnp.concatenate([up_weight, roomy(mix_weight.T)], axis=1)
    branch = branch_bias.astype(f32)
    flat = [a.astype(f32).reshape(-1) for a in (head_bias, branch, up_bias)]
    head_all, shards_in, latent_in, mod_parts, cond_blocks, biases_in = opening(
        cond_low,
        mod_weight,
        mod_bias,
        jnp.concatenate(flat).reshape(-1, 128),
        head_shard,
        shards,
        latent,
    )
    biases_in = biases_in.reshape(-1)
    head_bias_in = biases_in[: 2 * cols].reshape(2, cols)
    branch_in = biases_in[2 * cols : 4 * cols].reshape(2, cols)
    head_all = head_all.reshape(width, 6 * room)
    mod_parts = mod_parts.reshape(2, 2, count, 3, cols)
    mod_parts = own_latents(mod_parts, 2).transpose(0, 2, 1, 3, 4).reshape(2, own, 6, cols)
    modulation = in_order(mod_parts[0], mod_parts[1], 2)
    branch_all = in_order(branch, branch_in, 1)
    row = lambda k: modulation[:, k][:, None, :]
    shift_a, scale_a, gate_a, shift_m, scale_m, gate_m = [row(k) for k in range(6)]

    cuts = (0, hidden // 2, hidden // 2 + room)
    pieces = [a[:, lo:hi] for lo, hi in zip(cuts, cuts[1:]) for a in (shards, shards_in)]
    up_mix = lax.all_gather(jnp.concatenate(pieces, axis=1), "dp", axis=0, tiled=True)
    up_all = up_mix[:, :hidden]
    mix_t = up_mix[:, hidden:]
    up_bias_f = jnp.concatenate([flat[2], biases_in[4 * cols :]])

    lat = jnp.concatenate([own_latents(latent), latent_in], axis=1)
    lat_f = lat.astype(f32)
    norm1, inv1 = normed(lat_f)
    attn_in = (norm1 * (1.0 + scale_a) + shift_a).astype(bf16)
    empty = jnp.zeros((room,), f32)
    qkv_bias = jnp.concatenate(
        [c for b in (roomy(head_bias.astype(f32)), roomy(head_bias_in)) for c in (b[0], empty, b[1])]
    )
    qkv = (mm("bsd,dc->bsc", attn_in, head_all) + qkv_bias).astype(bf16)
    later, down_mine, qkv = lax.optimization_barrier((other_latents(cotangent), down_weight.T, qkv))
    down_t = lax.all_gather(
        jnp.concatenate([down_mine, swap(down_mine)], axis=1), "dp", axis=0, tiled=True
    )
    upstream_low = jnp.concatenate([own_latents(cotangent), swap(later)], axis=1)
    mixed, logsum = attn_fwd(qkv, heads)
    attn_out = mm("bsc,dc->bsd", mixed, mix_t) + branch_all[0]
    first = lat_f + gate_a * attn_out
    norm2, inv2 = normed(first)
    mlp_in = (norm2 * (1.0 + scale_m) + shift_m).astype(bf16)
    act, slope = up_forward(mlp_in, up_mix, up_bias_f)
    upstream = upstream_low.astype(f32)
    mlp_grad = (gate_m * upstream).astype(bf16)
    down_grad = mm("bsd,bsf->df", mlp_grad, act).astype(bf16)
    down_grad, mlp_grad, act = lax.optimization_barrier((down_grad, mlp_grad, act))
    down_sum = lax.psum_scatter(down_grad, "dp", scatter_dimension=0, tiled=True)
    mlp_out = mm("bsf,df->bsd", act, down_t) + branch_all[1]
    block = (first + gate_m * mlp_out).astype(bf16)
    block_in = swap(block[:, half_seq:])

    gate_m_grad = jnp.sum(upstream * mlp_out, axis=1)
    tail_bias_grad = jnp.sum(gate_m[:, 0] * jnp.sum(upstream, axis=1), axis=0)
    pre_grad, up_bias_term = down_backward(mlp_grad, down_t, slope)
    up_grad = mm("bsd,bsf->df", mlp_in, pre_grad).astype(bf16)
    up_grad, pre_grad = lax.optimization_barrier((up_grad, pre_grad))
    mlp_in_grad = mm("bsf,df->bsd", pre_grad, up_all)
    shift_m_grad = jnp.sum(mlp_in_grad, axis=1)
    scale_m_grad = jnp.sum(mlp_in_grad * norm2, axis=1)
    first_grad = upstream + normed_back(mlp_in_grad * (1.0 + scale_m), norm2, inv2)
    gate_a_grad = jnp.sum(first_grad * attn_out, axis=1)
    attn_bias_grad = jnp.sum(gate_a[:, 0] * jnp.sum(first_grad, axis=1), axis=0)
    attn_grad = (gate_a * first_grad).astype(bf16)
    attn_grad, down_sum = lax.optimization_barrier((attn_grad, down_sum))
    mixed_grad = mm("bsd,dc->bsc", attn_grad, mix_t).astype(bf16)
    mix_grad = mm("bsd,bsc->dc", attn_grad, mixed).astype(bf16)
    up_grad = jnp.concatenate([up_grad, mix_grad], axis=1)
    up_grad, mixed_grad = lax.optimization_barrier((up_grad, mixed_grad))
    up_sum = lax.psum_scatter(up_grad, "dp", scatter_dimension=0, tiled=True)
    qkv_grad, qkv_bias_term = attn_bwd(qkv, mixed_grad, mixed, logsum, heads)
    qkv_bias_term = jnp.sum(qkv_bias_term, axis=0)
    head_grad = mm("bsd,bsc->dc", attn_in, qkv_grad).astype(bf16)
    head_grad, up_sum, block_in = lax.optimization_barrier((head_grad, up_sum, block_in))
    block_out = placed(block, block_in)
    latent_grad, sums, head_sum = latents_backward(
        qkv_grad, head_all, lat, first_grad, scale_a, head_grad
    )
    shift_a_grad, scale_a_grad = sums[:, 0], sums[:, 1]

    mod_low = jnp.stack(
        [shift_a_grad, scale_a_grad, gate_a_grad, shift_m_grad, scale_m_grad, gate_m_grad], axis=1
    ).astype(bf16)
    branch_term = jnp.stack([attn_bias_grad, tail_bias_grad])
    head_term = qkv_bias_term.reshape(2, 3, room)[:, 0::2, :cols]
    ups = up_bias_term.reshape(2, hidden // 2)

    def mod_share(owner):
        mine = lax.dynamic_slice_in_dim(mod_low.astype(f32), owner * cols, cols, 2)
        mine = mine.reshape(own, 2, 3 * cols).transpose(1, 0, 2)
        empty = jnp.zeros((2, count, 3 * cols), f32)
        return lax.dynamic_update_slice_in_dim(empty, mine, side * own, 1).reshape(2 * count, 3 * cols)

    def bias_share(owner, k):
        branch_cols = lax.dynamic_slice_in_dim(branch_term, owner * cols, cols, 1)
        flat = jnp.concatenate([head_term[k].reshape(-1), branch_cols.reshape(-1), ups[k]])
        return flat.reshape(-1, 128)

    mod_pair = jnp.stack([mod_share(side), mod_share(1 - side)])
    biases, cond_parts, mod_weight_grad, mod_bias_grad = closing(
        mod_pair,
        jnp.stack([bias_share(side, 0), bias_share(1 - side, 1)]),
        mod_weight,
        cond_blocks,
    )
    biases = biases.reshape(-1)
    mod_weight_grad = mod_weight_grad.transpose(1, 0, 2)
    mod_bias_grad = mod_bias_grad[:, 0]
    cond_act = jnp.sum(cond_parts[..., :depth].reshape(2, groups, 2, count, depth), axis=(0, 2))
    cond_act = cond_act.transpose(1, 0, 2).reshape(count, groups * depth)
    gate = jax.nn.sigmoid(cond_f)
    condition_grad = cond_act * (gate * (1.0 + cond_f * (1.0 - gate)))

    def joined(summed, axis):
        mine, other = jnp.split(summed, 2, axis=axis)
        return mine.astype(f32) + swap(other.astype(bf16)).astype(f32)

    head_weight_grad = joined(head_sum, 1).reshape(depth, 3, room)[..., :cols]
    mix_weight_grad = joined(up_sum[:, hidden:], 1)[:, :cols].T
    up_weight_grad = joined(up_sum[:, :hidden], 1)
    down_weight_grad = joined(down_sum, 1).T
    return (
        block_out,
        latent_grad,
        condition_grad,
        mod_weight_grad,
        mod_bias_grad,
        head_weight_grad,
        biases[: 2 * cols].reshape(2, cols),
        mix_weight_grad,
        biases[2 * cols : 4 * cols].reshape(2, cols),
        up_weight_grad,
        biases[4 * cols :],
        down_weight_grad,
    )


def solution(mesh):
    placed = (
        P("dp", "tensor", None),
        P("dp", None),
        P("dp", "tensor", None),
        P("dp", None, "tensor"),
        P(None, "tensor"),
        P("dp", None, "tensor"),
        P(None, "tensor"),
        P("tensor", "dp"),
        P(None, "tensor"),
        P("dp", "tensor"),
        P("tensor"),
        P("tensor", "dp"),
    )
    whole_latents = dict(mesh.shape) == {"dp": 16, "tensor": 2}
    return jax.shard_map(
        body_by_latents if whole_latents else body_by_heads,
        mesh=mesh,
        in_specs=placed,
        out_specs=(
            P("dp", "tensor", None),
            P("dp", "tensor", None),
            P("dp", None),
            P("dp", None, "tensor"),
            P(None, "tensor"),
            P("dp", None, "tensor"),
            P(None, "tensor"),
            P("tensor", "dp"),
            P(None, "tensor"),
            P("dp", "tensor"),
            P("tensor"),
            P("tensor", "dp"),
        ),
        check_vma=False,
    )
```

```python
from functools import partial

import jax
import jax.numpy as jnp
from jax import lax
from jax.experimental import pallas as pl
from jax.experimental.pallas import tpu as pltpu
from jax.sharding import PartitionSpec as P

SEQ = 1024
HEAD_DIM = 72
MICRO = 4
LOG2E = 1.4426950408889634
WINDOW = 256
f32 = jnp.float32
bf16 = jnp.bfloat16
NT = (((1,), (1,)), ((), ()))
TN = (((0,), (0,)), ((), ()))
MESH = pl.DeviceIdType.MESH


EPSILON = 1e-06


def layer_norm(values):
    centred = values - jnp.mean(values, axis=-1, keepdims=True)
    variance = jnp.mean(centred * centred, axis=-1, keepdims=True)
    return centred * lax.rsqrt(variance + EPSILON)


def modulate(values, shift, scale):
    return layer_norm(values) * (1.0 + scale[:, None, :]) + shift[:, None, :]


def gelu_tanh(values):
    return jax.nn.gelu(values, approximate=True)


def fetch_weights(mod_weight, head_weight, mix_weight, up_weight, down_weight):
    return (
        lax.all_gather(mod_weight, "dp", axis=0, tiled=True),
        lax.all_gather(head_weight, "dp", axis=0, tiled=True),
        lax.all_gather(mix_weight, "dp", axis=1, tiled=True),
        lax.all_gather(up_weight, "dp", axis=0, tiled=True),
        lax.all_gather(down_weight, "dp", axis=1, tiled=True),
    )


def reduce_weights(grads):
    return (
        lax.psum_scatter(
            grads[0].astype(jnp.bfloat16), "dp", scatter_dimension=0, tiled=True
        ).astype(jnp.float32),
        lax.psum_scatter(
            grads[1].astype(jnp.bfloat16), "dp", scatter_dimension=0, tiled=True
        ).astype(jnp.float32),
        lax.psum_scatter(
            grads[2].astype(jnp.bfloat16), "dp", scatter_dimension=1, tiled=True
        ).astype(jnp.float32),
        lax.psum_scatter(
            grads[3].astype(jnp.bfloat16), "dp", scatter_dimension=0, tiled=True
        ).astype(jnp.float32),
        lax.psum_scatter(
            grads[4].astype(jnp.bfloat16), "dp", scatter_dimension=1, tiled=True
        ).astype(jnp.float32),
    )


def attend_forward(queries, keys, values, block_rows, scale_factor):
    seq_len = queries.shape[0]
    blocked = queries.reshape(seq_len // block_rows, block_rows, queries.shape[1], queries.shape[2])

    def one_block(query_block):
        scores = (
            jnp.einsum("qhd,khd->hqk", query_block, keys, preferred_element_type=jnp.float32)
            * scale_factor
        )
        peak = jnp.max(scores, axis=-1, keepdims=True)
        raised = jnp.exp(scores - peak)
        total = jnp.sum(raised, axis=-1, keepdims=True)
        weights = (raised / total).astype(jnp.bfloat16)
        mixed = jnp.einsum("hqk,khd->qhd", weights, values, preferred_element_type=jnp.float32)
        return (mixed, (peak + jnp.log(total))[..., 0])

    mixed, logsum = lax.map(one_block, blocked)
    return (mixed.reshape(queries.shape), logsum)


def attend_backward(queries, keys, values, grad_mixed, logsum, block_rows, scale_factor):
    seq_len = queries.shape[0]
    block_shape = (seq_len // block_rows, block_rows, queries.shape[1], queries.shape[2])

    def one_block(carried, pieces):
        key_sum, value_sum = carried
        query_block, grad_block, logsum_block = pieces
        scores = (
            jnp.einsum("qhd,khd->hqk", query_block, keys, preferred_element_type=jnp.float32)
            * scale_factor
        )
        probs = jnp.exp(scores - logsum_block[..., None])
        prob_grad = jnp.einsum(
            "qhd,khd->hqk", grad_block, values, preferred_element_type=jnp.float32
        )
        inner = jnp.sum(probs * prob_grad, axis=-1, keepdims=True)
        score_grad = (probs * (prob_grad - inner)).astype(jnp.bfloat16)
        query_grad = (
            jnp.einsum("hqk,khd->qhd", score_grad, keys, preferred_element_type=jnp.float32)
            * scale_factor
        )
        key_sum = (
            key_sum
            + jnp.einsum(
                "hqk,qhd->khd", score_grad, query_block, preferred_element_type=jnp.float32
            )
            * scale_factor
        )
        value_sum = value_sum + jnp.einsum(
            "hqk,qhd->khd",
            probs.astype(jnp.bfloat16),
            grad_block,
            preferred_element_type=jnp.float32,
        )
        return ((key_sum, value_sum), query_grad)

    empty = jnp.zeros(keys.shape, jnp.float32)
    (key_grad, value_grad), query_grads = lax.scan(
        one_block,
        (empty, empty),
        (queries.reshape(block_shape), grad_mixed.reshape(block_shape), logsum),
    )
    return (query_grads.reshape(queries.shape), key_grad, value_grad)


def body_by_heads(
    latent,
    condition,
    cotangent,
    mod_weight,
    mod_bias,
    head_weight,
    head_bias,
    mix_weight,
    branch_bias,
    up_weight,
    up_bias,
    down_weight,
):
    per_group = latent.shape[0] // MICRO
    seq_len = SEQ
    head_cols = head_weight.shape[2]
    local_heads = head_cols // HEAD_DIM
    block_rows = min(512, seq_len)
    scale_factor = HEAD_DIM ** (-0.5)
    attend_fwd = jax.vmap(partial(attend_forward, block_rows=block_rows, scale_factor=scale_factor))
    attend_bwd = jax.vmap(
        partial(attend_backward, block_rows=block_rows, scale_factor=scale_factor)
    )
    head_bias_f = head_bias.astype(jnp.float32)
    up_bias_f = up_bias.astype(jnp.float32)
    mod_bias_f = mod_bias.astype(jnp.float32)
    branch_bias_f = branch_bias.astype(jnp.float32)
    bias_totals = (
        jnp.zeros(mod_bias.shape, jnp.float32),
        jnp.zeros(head_bias.shape, jnp.float32),
        jnp.zeros(up_bias.shape, jnp.float32),
        jnp.zeros(branch_bias.shape, jnp.float32),
    )
    grad_sums = None
    block_outs = []
    latent_grads = []
    condition_grads = []
    for micro_step in range(MICRO):
        row_start = micro_step * per_group
        row_stop = row_start + per_group
        mod_full, head_full, mix_full, up_full, down_full = fetch_weights(
            mod_weight, head_weight, mix_weight, up_weight, down_weight
        )
        lat_part = latent[row_start:row_stop].astype(jnp.float32)
        cond_part = condition[row_start:row_stop].astype(jnp.float32)
        cond_act, silu_back = jax.vjp(jax.nn.silu, cond_part)
        cond_low = cond_act.astype(jnp.bfloat16)
        mod_cols = (
            jnp.einsum("bd,dkc->bkc", cond_low, mod_full, preferred_element_type=jnp.float32)
            + mod_bias_f
        )
        mod_all, bias_all = (
            lax.all_gather(mod_cols, "tensor", axis=2, tiled=True),
            lax.all_gather(branch_bias_f, "tensor", axis=1, tiled=True),
        )
        norm_first, first_back = jax.vjp(modulate, lat_part, mod_all[:, 0], mod_all[:, 1])
        attn_rows = lax.all_gather(norm_first.astype(jnp.bfloat16), "tensor", axis=1, tiled=True)
        projected = jnp.einsum(
            "bsd,dkc->bskc", attn_rows, head_full, preferred_element_type=jnp.float32
        )
        head_shape = (per_group, seq_len, local_heads, HEAD_DIM)
        query_heads = (projected[:, :, 0] + head_bias_f[0]).astype(jnp.bfloat16).reshape(head_shape)
        key_heads = projected[:, :, 1].astype(jnp.bfloat16).reshape(head_shape)
        value_heads = (projected[:, :, 2] + head_bias_f[1]).astype(jnp.bfloat16).reshape(head_shape)
        mixed, logsum = attend_fwd(query_heads, key_heads, value_heads)
        mixed_low = mixed.reshape(per_group, seq_len, head_cols).astype(jnp.bfloat16)
        attn_part = jnp.einsum(
            "bsc,cd->bsd", mixed_low, mix_full, preferred_element_type=jnp.float32
        )
        attn_local = lax.psum_scatter(
            attn_part.astype(jnp.bfloat16), "tensor", scatter_dimension=1, tiled=True
        ).astype(jnp.float32)
        gate_attn = mod_all[:, 2][:, None, :]
        gate_mlp = mod_all[:, 5][:, None, :]
        first = lat_part + gate_attn * (attn_local + bias_all[0])
        norm_second, second_back = jax.vjp(modulate, first, mod_all[:, 3], mod_all[:, 4])
        mlp_rows = lax.all_gather(norm_second.astype(jnp.bfloat16), "tensor", axis=1, tiled=True)
        pre_act = (
            jnp.einsum("bsd,df->bsf", mlp_rows, up_full, preferred_element_type=jnp.float32)
            + up_bias_f
        )
        act_value, gelu_back = jax.vjp(gelu_tanh, pre_act)
        act_low = act_value.astype(jnp.bfloat16)
        mlp_part = jnp.einsum("bsf,fd->bsd", act_low, down_full, preferred_element_type=jnp.float32)
        mlp_local = lax.psum_scatter(
            mlp_part.astype(jnp.bfloat16), "tensor", scatter_dimension=1, tiled=True
        ).astype(jnp.float32)
        block_outs.append((first + gate_mlp * (mlp_local + bias_all[1])).astype(jnp.bfloat16))
        mod_full, head_full, mix_full, up_full, down_full = fetch_weights(
            mod_weight, head_weight, mix_weight, up_weight, down_weight
        )
        upstream = cotangent[row_start:row_stop].astype(jnp.float32)
        gate_m_grad = jnp.sum(upstream * (mlp_local + bias_all[1]), axis=1)
        tail_bias_grad = jnp.sum(gate_mlp * upstream, axis=(0, 1))
        mlp_grad = lax.all_gather(
            (gate_mlp * upstream).astype(jnp.bfloat16), "tensor", axis=1, tiled=True
        )
        down_grad = jnp.einsum("bsf,bsd->fd", act_low, mlp_grad, preferred_element_type=jnp.float32)
        act_grad = jnp.einsum(
            "bsd,fd->bsf", mlp_grad, down_full, preferred_element_type=jnp.float32
        )
        pre_grad = gelu_back(act_grad)[0].astype(jnp.bfloat16)
        up_bias_term = jnp.sum(pre_grad, axis=(0, 1), dtype=jnp.float32)
        up_grad = jnp.einsum("bsd,bsf->df", mlp_rows, pre_grad, preferred_element_type=jnp.float32)
        mlp_in_part = jnp.einsum(
            "bsf,df->bsd", pre_grad, up_full, preferred_element_type=jnp.float32
        )
        mlp_in_grad = lax.psum_scatter(
            mlp_in_part.astype(jnp.bfloat16), "tensor", scatter_dimension=1, tiled=True
        ).astype(jnp.float32)
        first_grad, shift_m_grad, scale_m_grad = second_back(mlp_in_grad)
        first_grad = first_grad + upstream
        gate_a_grad = jnp.sum(first_grad * (attn_local + bias_all[0]), axis=1)
        attn_bias_grad = jnp.sum(gate_attn * first_grad, axis=(0, 1))
        attn_branch_grad = (gate_attn * first_grad).astype(jnp.bfloat16)
        attn_grad = lax.all_gather(attn_branch_grad, "tensor", axis=1, tiled=True)
        mix_grad = jnp.einsum(
            "bsc,bsd->cd", mixed_low, attn_grad, preferred_element_type=jnp.float32
        )
        mixed_grad = jnp.einsum(
            "bsd,cd->bsc", attn_grad, mix_full, preferred_element_type=jnp.float32
        ).astype(jnp.bfloat16)
        query_grad, key_grad, value_grad = attend_bwd(
            query_heads, key_heads, value_heads, mixed_grad.reshape(head_shape), logsum
        )
        head_grads = (
            jnp.stack([query_grad, key_grad, value_grad], axis=2)
            .reshape(per_group, seq_len, 3, head_cols)
            .astype(jnp.bfloat16)
        )
        head_bias_term = jnp.sum(head_grads[:, :, 0::2], axis=(0, 1), dtype=jnp.float32)
        head_grad = jnp.einsum(
            "bsd,bskc->dkc", attn_rows, head_grads, preferred_element_type=jnp.float32
        )
        attn_in_part = jnp.einsum(
            "bskc,dkc->bsd", head_grads, head_full, preferred_element_type=jnp.float32
        )
        attn_in_grad = lax.psum_scatter(
            attn_in_part.astype(jnp.bfloat16), "tensor", scatter_dimension=1, tiled=True
        ).astype(jnp.float32)
        lat_grad, shift_a_grad, scale_a_grad = first_back(attn_in_grad)
        latent_grads.append((lat_grad + first_grad).astype(jnp.bfloat16))
        mod_terms = jnp.stack(
            [shift_a_grad, scale_a_grad, gate_a_grad, shift_m_grad, scale_m_grad, gate_m_grad],
            axis=1,
        )
        branch_terms = jnp.stack([attn_bias_grad, tail_bias_grad], axis=0)
        mod_grad_cols, branch_grad_cols = (
            lax.psum_scatter(
                mod_terms.astype(jnp.bfloat16), "tensor", scatter_dimension=2, tiled=True
            ).astype(jnp.float32),
            lax.psum_scatter(
                branch_terms.astype(jnp.bfloat16), "tensor", scatter_dimension=1, tiled=True
            ).astype(jnp.float32),
        )
        mod_grad_low = mod_grad_cols.astype(jnp.bfloat16)
        mod_grad = jnp.einsum(
            "bd,bkc->dkc", cond_low, mod_grad_low, preferred_element_type=jnp.float32
        )
        mod_bias_term = jnp.sum(mod_grad_low, axis=0, dtype=jnp.float32)
        cond_part_grad = jnp.einsum(
            "bkc,dkc->bd", mod_grad_low, mod_full, preferred_element_type=jnp.float32
        )
        cond_act_grad = lax.psum(cond_part_grad, "tensor")
        condition_grads.append(silu_back(cond_act_grad)[0])
        bias_totals = (
            bias_totals[0] + mod_bias_term,
            bias_totals[1] + head_bias_term,
            bias_totals[2] + up_bias_term,
            bias_totals[3] + branch_grad_cols,
        )
        weight_terms = (mod_grad, head_grad, mix_grad, up_grad, down_grad)
        grad_sums = (
            weight_terms if grad_sums is None else jax.tree.map(jnp.add, grad_sums, weight_terms)
        )
    grad_sums = reduce_weights(grad_sums)
    bias_sums = lax.psum((bias_totals[0], bias_totals[1], bias_totals[2], bias_totals[3]), "dp")
    return (
        jnp.concatenate(block_outs, axis=0),
        jnp.concatenate(latent_grads, axis=0),
        jnp.concatenate(condition_grads, axis=0),
        grad_sums[0],
        bias_sums[0],
        grad_sums[1],
        bias_sums[1],
        grad_sums[2],
        bias_sums[3],
        grad_sums[3],
        bias_sums[2],
        grad_sums[4],
    )


def head_window(col, width):
    start = jnp.minimum(col // 128 * 128, width - WINDOW)
    return pl.multiple_of(start, 128), col - start


def head_members(heads, width):
    col = lax.broadcasted_iota(jnp.int32, (heads, width), 1)
    first = lax.broadcasted_iota(jnp.int32, (heads, width), 0) * HEAD_DIM
    return jnp.where((col >= first) & (col < first + HEAD_DIM), 1.0, 0.0).astype(bf16)


def attn_fwd_kernel(q_ref, k_ref, v_ref, o_ref, lse_ref, ot_ref, *, blk, heads):
    seq, width = q_ref.shape[1:]
    c = HEAD_DIM ** -0.5 * LOG2E
    ot_ref[...] = v_ref[0].astype(f32).T
    lanes = lax.broadcasted_iota(jnp.int32, (blk, WINDOW), 1)
    ones = jnp.ones((8, seq), f32)
    member = head_members(heads, width)
    longest = [
        jnp.max(
            lax.dot_general(member, ref[0] * ref[0], NT, preferred_element_type=f32),
            axis=1,
            keepdims=True,
        )
        for ref in (q_ref, k_ref)
    ]
    bound = longest[0] * longest[1] * (1.1 * c * c)
    which = lax.broadcasted_iota(jnp.int32, bound.shape, 0) // 2

    def pair(i, carry):
        def run(shifted):
            steps = [(2 * i + odd, b) for odd in range(2) for b in range(seq // blk)]

            def scores(head, b):
                start, off = head_window(head * HEAD_DIM, width)
                mask = (lanes >= off) & (lanes < off + HEAD_DIM)
                qb = q_ref[0, b * blk : (b + 1) * blk, pl.ds(start, WINDOW)]
                qb = jnp.where(mask, qb, jnp.zeros_like(qb))
                return lax.dot_general(
                    k_ref[0, :, pl.ds(start, WINDOW)], qb, NT, preferred_element_type=f32
                )

            st = scores(*steps[0])
            vt = None
            for n, (head, b) in enumerate(steps):
                after = scores(*steps[n + 1]) if n + 1 < len(steps) else None
                mine = pl.ds(pl.multiple_of(head * HEAD_DIM, 8), HEAD_DIM)
                if b == 0:
                    vt = jnp.concatenate([ot_ref[mine, :], ones], axis=0).astype(bf16)
                rows = slice(b * blk, (b + 1) * blk)
                if shifted:
                    m = jnp.max(st, axis=0, keepdims=True)
                    p = jnp.exp2((st - m) * c).astype(bf16)
                else:
                    p = jnp.exp2(st * c).astype(bf16)
                ot = jnp.dot(vt, p, preferred_element_type=f32)
                l = ot[HEAD_DIM : HEAD_DIM + 1]
                ot_ref[mine, rows] = ot[:HEAD_DIM] * (1.0 / l)
                lse_ref[0, 0, pl.ds(head, 1), rows] = jnp.log2(l) + m * c if shifted else jnp.log2(l)
                st = after

        small = jnp.max(jnp.where(which == i, bound, 0.0)) < 85.0 * 85.0
        pl.when(small)(lambda: run(False))
        pl.when(jnp.logical_not(small))(lambda: run(True))
        return carry

    lax.fori_loop(0, heads // 2, pair, 0)
    o_ref[0] = ot_ref[...].T.astype(bf16)


def attn_fwd(qkv, heads, blk=256):
    n, seq, wide = qkv.shape
    width = wide // 6
    spec = lambda j: pl.BlockSpec((1, seq, width), lambda b, h: (b, 0, 3 * h + j))
    return pl.pallas_call(
        partial(attn_fwd_kernel, blk=blk, heads=heads),
        grid=(n, 2),
        in_specs=[spec(0), spec(1), spec(2)],
        out_specs=[
            pl.BlockSpec((1, seq, width), lambda b, h: (b, 0, h)),
            pl.BlockSpec((1, 1, heads, seq), lambda b, h: (b, h, 0, 0)),
        ],
        out_shape=[
            jax.ShapeDtypeStruct((n, seq, 2 * width), bf16),
            jax.ShapeDtypeStruct((n, 2, heads, seq), f32),
        ],
        scratch_shapes=[pltpu.VMEM((width, seq), f32)],
        compiler_params=pltpu.CompilerParams(vmem_limit_bytes=56 << 20),
        cost_estimate=pl.CostEstimate(
            flops=8 * n * seq * seq * width,
            bytes_accessed=16 * n * seq * width,
            transcendentals=2 * n * heads * seq * seq,
        ),
        name="attention_forward",
    )(qkv, qkv, qkv)


def attn_bwd_kernel(
    q_ref, k_ref, v_ref, do_ref, o_ref, lse_ref, dqkv_ref, sum_ref,
    dqt_ref, delta_ref, pt_ref, dst_ref, *, blk, heads
):
    seq, width = q_ref.shape[1:]
    scale = HEAD_DIM ** -0.5
    c = scale * LOG2E
    dqt_ref[...] = k_ref[0].astype(f32).T
    prod = do_ref[0].astype(f32) * o_ref[0].astype(f32)
    high = prod.astype(bf16)
    low = (prod - high.astype(f32)).astype(bf16)
    member = head_members(heads, width)
    delta_ref[...] = lax.dot_general(member, high, NT, preferred_element_type=f32) + lax.dot_general(
        member, low, NT, preferred_element_type=f32
    )
    lanes = lax.broadcasted_iota(jnp.int32, (seq, WINDOW), 1)
    edge = heads * HEAD_DIM // 128 * 128
    for part in (1, 2):
        dqkv_ref[0, :, part * width + edge : (part + 1) * width] = jnp.zeros((seq, width - edge), bf16)

    def one(head, carry):
        start, off = head_window(head * HEAD_DIM, width)
        window = pl.ds(start, WINDOW)
        mask = (lanes >= off) & (lanes < off + HEAD_DIM)
        keys = k_ref[0, :, window]
        values = v_ref[0, :, window]
        qm = q_ref[0, :, window]
        qm = jnp.where(mask, qm, jnp.zeros_like(qm))
        dom = do_ref[0, :, window]
        dom = jnp.where(mask, dom, jnp.zeros_like(dom))
        mine = pl.ds(pl.multiple_of(head * HEAD_DIM, 8), HEAD_DIM)
        kt = dqt_ref[mine, :].astype(bf16)
        def products(b):
            rows = slice(b * blk, (b + 1) * blk)
            st = lax.dot_general(keys, qm[rows], NT, preferred_element_type=f32)
            return st, lax.dot_general(values, dom[rows], NT, preferred_element_type=f32)

        now = products(0)
        for b in range(seq // blk):
            rows = slice(b * blk, (b + 1) * blk)
            later = products(b + 1) if b + 1 < seq // blk else None
            st, dpt = now
            p = jnp.exp2(st * c - lse_ref[0, 0, pl.ds(head, 1), rows])
            dst = (p * (dpt - delta_ref[pl.ds(head, 1), rows])).astype(bf16)
            pt_ref[:, rows] = p.astype(bf16)
            dst_ref[:, rows] = dst
            dqt_ref[mine, rows] = jnp.dot(kt, dst, preferred_element_type=f32) * scale
            now = later
        dk = jnp.dot(dst_ref[...], qm, preferred_element_type=f32) * scale
        dv = jnp.dot(pt_ref[...], dom, preferred_element_type=f32)
        kwin = pl.ds(pl.multiple_of(width + start, 128), WINDOW)
        vwin = pl.ds(pl.multiple_of(2 * width + start, 128), WINDOW)
        dqkv_ref[0, :, kwin] = jnp.where(mask, dk.astype(bf16), dqkv_ref[0, :, kwin])
        dqkv_ref[0, :, vwin] = jnp.where(mask, dv.astype(bf16), dqkv_ref[0, :, vwin])
        return carry

    lax.fori_loop(0, heads, one, 0)
    dqkv_ref[0, :, :width] = dqt_ref[...].T.astype(bf16)
    sum_ref[0, 0] = jnp.sum(dqkv_ref[0].astype(f32), axis=0, keepdims=True)


def attn_bwd(qkv, grad, mixed, lse, heads, blk=256):
    n, seq, wide = qkv.shape
    width = wide // 6
    spec = lambda j: pl.BlockSpec((1, seq, width), lambda b, h: (b, 0, 3 * h + j))
    out = pl.BlockSpec((1, seq, width), lambda b, h: (b, 0, h))
    return pl.pallas_call(
        partial(attn_bwd_kernel, blk=blk, heads=heads),
        grid=(n, 2),
        in_specs=[
            spec(0), spec(1), spec(2), out, out,
            pl.BlockSpec((1, 1, heads, seq), lambda b, h: (b, h, 0, 0)),
        ],
        out_specs=[
            pl.BlockSpec((1, seq, 3 * width), lambda b, h: (b, 0, h)),
            pl.BlockSpec((1, 1, 1, 3 * width), lambda b, h: (b, h, 0, 0)),
        ],
        out_shape=[
            jax.ShapeDtypeStruct(qkv.shape, bf16),
            jax.ShapeDtypeStruct((n, 2, 1, 3 * width), f32),
        ],
        scratch_shapes=[
            pltpu.VMEM((width, seq), f32),
            pltpu.VMEM((heads, seq), f32),
            pltpu.VMEM((seq, seq), bf16),
            pltpu.VMEM((seq, seq), bf16),
        ],
        compiler_params=pltpu.CompilerParams(vmem_limit_bytes=56 << 20),
        cost_estimate=pl.CostEstimate(flops=0, bytes_accessed=0, transcendentals=0),
        name="attention_backward",
    )(qkv, qkv, qkv, grad, mixed, lse)


def gelu_with_slope(u):
    k, cubic = 0.7978845608028654, 0.7978845608028654 * 0.044715
    square = u * u
    half = 0.5 + 0.5 * jnp.tanh(u * (k + cubic * square))
    value = u * half
    return value, half + value * (1.0 - half) * (2.0 * k + 6.0 * cubic * square)


def tile_steps(rows, cols, sub_rows, sub_cols):
    return [
        (slice(i, i + sub_rows), slice(j, j + sub_cols))
        for j in range(0, cols, sub_cols)
        for i in range(0, rows, sub_rows)
    ]


def up_forward_kernel(x_ref, w_ref, b_ref, act_ref, slope_ref):
    steps = tile_steps(*act_ref.shape, 256, 256)
    product = lambda r, c: jnp.dot(x_ref[r, :], w_ref[:, c], preferred_element_type=f32)
    now = product(*steps[0])
    for n, (r, c) in enumerate(steps):
        later = product(*steps[n + 1]) if n + 1 < len(steps) else None
        value, slope = gelu_with_slope(now + b_ref[:, c])
        act_ref[r, c] = value.astype(bf16)
        slope_ref[r, c] = slope.astype(bf16)
        now = later


def up_forward(x, w, bias):
    count, seq, depth = x.shape
    hidden = bias.shape[0]
    rows, cols = 1024, hidden // 3
    tile = pl.BlockSpec((rows, cols), lambda j, i: (i, j))
    act, slope = pl.pallas_call(
        up_forward_kernel,
        grid=(hidden // cols, count * seq // rows),
        in_specs=[
            pl.BlockSpec((rows, depth), lambda j, i: (i, 0)),
            pl.BlockSpec((depth, cols), lambda j, i: (0, j)),
            pl.BlockSpec((1, cols), lambda j, i: (0, j)),
        ],
        out_specs=[tile, tile],
        out_shape=[jax.ShapeDtypeStruct((count * seq, hidden), bf16)] * 2,
        compiler_params=pltpu.CompilerParams(vmem_limit_bytes=56 << 20),
        cost_estimate=pl.CostEstimate(
            flops=2 * count * seq * depth * hidden,
            bytes_accessed=4 * count * seq * hidden,
            transcendentals=count * seq * hidden,
        ),
        name="up_forward",
    )(x.reshape(count * seq, depth), w, bias.reshape(1, hidden))
    return act.reshape(count, seq, hidden), slope.reshape(count, seq, hidden)


def down_backward_kernel(g_ref, w_ref, slope_ref, out_ref, sum_ref):
    steps = tile_steps(*out_ref.shape, out_ref.shape[0], 256)
    product = lambda r, c: jnp.dot(g_ref[r, :], w_ref[:, c], preferred_element_type=f32)

    @pl.when(pl.program_id(1) == 0)
    def _():
        sum_ref[...] = jnp.zeros_like(sum_ref)

    now = product(*steps[0])
    for n, (r, c) in enumerate(steps):
        later = product(*steps[n + 1]) if n + 1 < len(steps) else None
        grad = (now * slope_ref[r, c].astype(f32)).astype(bf16)
        out_ref[r, c] = grad
        sum_ref[:, c] += jnp.sum(grad.astype(f32), axis=0, keepdims=True)
        now = later


def down_backward(g, w, slope):
    count, seq, depth = g.shape
    hidden = slope.shape[2]
    rows, cols = 1024, hidden // 3
    tile = pl.BlockSpec((rows, cols), lambda j, i: (i, j))
    grad, total = pl.pallas_call(
        down_backward_kernel,
        grid=(hidden // cols, count * seq // rows),
        in_specs=[
            pl.BlockSpec((rows, depth), lambda j, i: (i, 0)),
            pl.BlockSpec((depth, cols), lambda j, i: (0, j)),
            tile,
        ],
        out_specs=[tile, pl.BlockSpec((1, cols), lambda j, i: (0, j))],
        out_shape=[
            jax.ShapeDtypeStruct((count * seq, hidden), bf16),
            jax.ShapeDtypeStruct((1, hidden), f32),
        ],
        compiler_params=pltpu.CompilerParams(vmem_limit_bytes=56 << 20),
        cost_estimate=pl.CostEstimate(
            flops=2 * count * seq * depth * hidden,
            bytes_accessed=4 * count * seq * hidden,
            transcendentals=0,
        ),
        name="down_backward",
    )(g.reshape(count * seq, depth), w, slope.reshape(count * seq, hidden))
    return grad.reshape(count, seq, hidden), total[0]


CORES = 2
ROWS = 2


def place(rank):
    return rank // (ROWS * CORES), rank // CORES % ROWS, rank % CORES


def rank_of(z, y, core):
    return (z * ROWS + y) * CORES + core


def greet(side):
    rank = lax.axis_index("dp")
    groups = lax.axis_size("dp")
    barrier = pltpu.get_barrier_semaphore()
    for step in range(1, groups):
        pl.semaphore_signal(barrier, inc=1, device_id={"dp": lax.rem(rank + step, groups)}, device_id_type=MESH)
    pl.semaphore_signal(barrier, inc=1, device_id={"tensor": 1 - side}, device_id_type=MESH)
    pl.semaphore_wait(barrier, groups)


class Spread:
    def __init__(self, source, out, sends, arrivals, lanes=None):
        self.source, self.out, self.sends, self.arrivals = source, out, sends, arrivals
        self.lanes = lanes
        self.rank = lax.axis_index("dp")
        self.z, self.y, self.core = place(self.rank)
        self.depth = lax.axis_size("dp") // (ROWS * CORES)
        self.started = []

    def block(self, origin):
        return self.out.at[origin] if self.lanes is None else self.out.at[origin, :, self.lanes]

    def copy(self, origin, edge, target, source=None):
        return pltpu.make_async_remote_copy(
            src_ref=self.block(origin) if source is None else source,
            dst_ref=self.block(origin),
            send_sem=self.sends.at[origin, edge],
            recv_sem=self.arrivals.at[origin],
            device_id={"dp": target},
            device_id_type=MESH,
        )

    def send(self, origin, edge, target, source=None, when=None):
        sent = self.copy(origin, edge, target, source)
        if when is None:
            sent.start()
        else:
            pl.when(when)(sent.start)
        self.started.append((sent, when))

    def arrive(self, origin):
        self.copy(origin, 0, rank_of(self.z, 1 - self.y, self.core)).wait_recv()

    def up(self):
        return rank_of(self.z + 1, self.y, self.core)

    def down(self):
        return rank_of(self.z - 1, self.y, self.core)

    def across(self):
        return rank_of(self.z, 1 - self.y, self.core)

    def sibling(self):
        return rank_of(self.z, self.y, 1 - self.core)

    def begin(self):
        rank, source = self.rank, self.source
        self.send(rank, 0, self.up(), source, self.z < self.depth - 1)
        self.send(rank, 3, self.down(), source, self.z > 0)
        self.send(rank, 1, self.across(), source)
        self.send(rank, 2, self.sibling(), source)

    def relay(self, hop):
        for toward, there in ((1, self.z >= hop), (-1, self.z + hop < self.depth)):
            origin = rank_of(self.z - toward * hop, self.y, self.core)
            further = (self.z < self.depth - 1) if toward > 0 else (self.z > 0)
            pl.when(there)(lambda: self.arrive(origin))
            self.send(
                origin, 0, self.up() if toward > 0 else self.down(), when=there & further
            )
            self.send(origin, 1, self.across(), when=there)
            self.send(origin, 2, self.sibling(), when=there)

    def relay_across(self, hop):
        for toward, there in ((1, self.z >= hop), (-1, self.z + hop < self.depth)):
            if hop == 0 and toward < 0:
                continue
            origin = rank_of(self.z - toward * hop, 1 - self.y, self.core)
            pl.when(there)(lambda: self.arrive(origin))
            self.send(origin, 2, self.sibling(), when=there)

    def finish(self):
        for z in range(self.depth):
            for y in range(ROWS):
                self.arrive(rank_of(z, y, 1 - self.core))
        for sent, when in self.started:
            if when is None:
                sent.wait_send()
            else:
                pl.when(when)(sent.wait_send)


class DirectSpread:
    def __init__(self, out, sends, arrivals):
        self.out, self.sends, self.arrivals = out, sends, arrivals
        self.rank = lax.axis_index("dp")
        self.groups = lax.axis_size("dp")
        self.sibling = self.rank + 1 - 2 * lax.rem(self.rank, CORES)
        self.steps = range(CORES, self.groups, CORES)

    def copy(self, origin, send, target):
        return pltpu.make_async_remote_copy(
            src_ref=self.out.at[origin],
            dst_ref=self.out.at[origin],
            send_sem=self.sends.at[send],
            recv_sem=self.arrivals.at[origin],
            device_id={"dp": target},
            device_id_type=MESH,
        )

    def peer(self, step):
        return lax.rem(self.rank + step, self.groups)

    def begin(self):
        for step in self.steps:
            self.copy(self.rank, step, self.peer(step)).start()
        self.copy(self.rank, 0, self.sibling).start()

    def relay(self):
        for step in self.steps:
            origin = self.peer(step)
            self.copy(origin, step, origin).wait_recv()
            self.copy(origin, step + 1, self.sibling).start()

    def finish(self):
        for step in range(0, self.groups, CORES):
            origin = lax.rem(self.sibling + step, self.groups)
            self.copy(origin, 0, self.sibling).wait_recv()
        for step in self.steps:
            self.copy(self.rank, step, self.peer(step)).wait_send()
            self.copy(self.peer(step), step + 1, self.sibling).wait_send()
        self.copy(self.rank, 0, self.sibling).wait_send()


class Exchange:
    def __init__(self, source, out, sends, arrivals):
        self.source, self.out, self.sends, self.arrivals = source, out, sends, arrivals
        self.rank = lax.axis_index("dp")
        self.groups = lax.axis_size("dp")

    def copy(self, step):
        peer = lax.rem(self.rank + step, self.groups)
        return pltpu.make_async_remote_copy(
            src_ref=self.source.at[peer],
            dst_ref=self.out.at[self.rank],
            send_sem=self.sends.at[step],
            recv_sem=self.arrivals.at[self.rank],
            device_id={"dp": peer},
            device_id_type=MESH,
        )

    def begin(self):
        self.out[self.rank] = self.source[self.rank]
        for step in range(1, self.groups):
            self.copy(step).start()

    def finish(self):
        for step in range(1, self.groups):
            peer = lax.rem(self.rank + step, self.groups)
            pltpu.make_async_remote_copy(
                src_ref=self.source.at[peer],
                dst_ref=self.out.at[peer],
                send_sem=self.sends.at[step],
                recv_sem=self.arrivals.at[peer],
                device_id={"dp": peer},
                device_id_type=MESH,
            ).wait_recv()

    def drain(self):
        for step in range(1, self.groups):
            self.copy(step).wait_send()


def to_partner(source, target, side, sends, arrivals, k):
    return pltpu.make_async_remote_copy(
        src_ref=source,
        dst_ref=target,
        send_sem=sends.at[k],
        recv_sem=arrivals.at[k],
        device_id={"tensor": 1 - side},
        device_id_type=MESH,
    )


def opening_kernel(
    cond_ref, mod_w_ref, mod_bias_ref, bias_ref, head_ref, rest_ref, latent_ref,
    head_out, rest_out, latent_out, mod_out, cond_out, bias_out,
    part_ref, mod_in,
    x_send, x_recv, c_send, c_recv, m_send, m_recv, h_send, h_recv, local_sem,
):
    side = lax.axis_index("tensor")
    rank = lax.axis_index("dp")
    greet(side)
    conds = Exchange(cond_ref, cond_out, c_send, c_recv)
    conds.begin()
    lanes = head_ref.shape[1]
    mine = Spread(head_ref, head_out, h_send.at[0], h_recv.at[0], pl.ds(0, lanes))
    other = Spread(None, head_out, h_send.at[1], h_recv.at[1], pl.ds(lanes, lanes))
    head_swap = to_partner(head_ref, other.block(rank), side, x_send, x_recv, 0)
    head_swap.start()
    mine.begin()
    biases = to_partner(bias_ref, bias_out, side, x_send, x_recv, 3)
    biases.start()
    rest = to_partner(rest_ref, rest_out, side, x_send, x_recv, 1)
    rest.start()
    own = latent_out.shape[0]
    latents = to_partner(
        latent_ref.at[pl.ds((1 - side) * own, own)], latent_out, side, x_send, x_recv, 4
    )
    latents.start()
    keep = pltpu.make_async_copy(head_ref, mine.block(rank), local_sem)
    keep.start()
    conds.finish()
    groups, rows, lanes = cond_out.shape
    half = mod_bias_ref.shape[1]
    low = cond_out[...].reshape(groups * rows, lanes).astype(bf16)
    front = lax.broadcasted_iota(jnp.int32, (groups * rows, half), 0) % rows < rows // 2
    part_ref[...] = jnp.where(
        front,
        jnp.dot(low, mod_w_ref[0], preferred_element_type=f32),
        jnp.dot(low, mod_w_ref[1], preferred_element_type=f32),
    ).reshape(groups, rows, half)
    mods = Exchange(part_ref, mod_in, m_send, m_recv)
    mods.begin()
    head_swap.wait_recv()
    other.begin()
    mine.relay(1)
    mods.finish()
    mod_out[0] = jnp.sum(mod_in[...], axis=0) + mod_bias_ref[...]
    mod_swap = to_partner(mod_out.at[0], mod_out.at[1], side, x_send, x_recv, 2)
    mod_swap.start()
    other.relay(1)
    mine.relay_across(0)
    other.relay_across(0)
    depth = mine.depth
    for hop in range(2, depth):
        for s in (mine, other):
            s.relay(hop)
            s.relay_across(hop - 1)
    for s in (mine, other):
        s.relay_across(depth - 1)
    keep.wait()
    mine.finish()
    other.finish()
    mod_swap.wait()
    rest.wait()
    latents.wait()
    biases.wait()
    head_swap.wait_send()
    conds.drain()
    mods.drain()


def opening(cond_low, mod_weight, mod_bias, biases, head, rest, latent):
    groups = lax.axis_size("dp")
    count = cond_low.shape[0]
    depth = cond_low.shape[1] // groups
    half = mod_weight.shape[1] * mod_weight.shape[2] // 2
    blocks = cond_low.astype(f32).reshape(count, groups, depth).transpose(1, 0, 2)
    blocks = jnp.concatenate([blocks, blocks], axis=1)
    blocks = jnp.pad(blocks, ((0, 0), (0, 0), (0, 128 - depth)))
    weights = jnp.pad(mod_weight.reshape(depth, 2, half), ((0, 128 - depth), (0, 0), (0, 0))).transpose(1, 0, 2)
    bias = jnp.repeat(mod_bias.astype(f32).reshape(2, half), count, axis=0)
    dma = pltpu.SemaphoreType.DMA
    vmem = pl.BlockSpec(memory_space=pltpu.VMEM)
    anywhere = pl.BlockSpec(memory_space=pl.ANY)
    return pl.pallas_call(
        opening_kernel,
        in_specs=[vmem, vmem, vmem, vmem, anywhere, anywhere, anywhere],
        out_specs=[anywhere, anywhere, anywhere, vmem, vmem, vmem],
        out_shape=[
            jax.ShapeDtypeStruct((groups, depth, 2 * head.shape[1]), bf16),
            jax.ShapeDtypeStruct(rest.shape, bf16),
            jax.ShapeDtypeStruct((count // 2,) + latent.shape[1:], bf16),
            jax.ShapeDtypeStruct((2, 2 * count, half), f32),
            jax.ShapeDtypeStruct(blocks.shape, f32),
            jax.ShapeDtypeStruct(biases.shape, f32),
        ],
        scratch_shapes=[
            pltpu.VMEM((groups, 2 * count, half), f32),
            pltpu.VMEM((groups, 2 * count, half), f32),
            dma((5,)), dma((5,)),
            dma((groups,)), dma((groups,)),
            dma((groups,)), dma((groups,)),
            dma((2, groups, 4)), dma((2, groups)),
            dma,
        ],
        compiler_params=pltpu.CompilerParams(collective_id=0, has_side_effects=True, vmem_limit_bytes=32 << 20),
        cost_estimate=pl.CostEstimate(flops=0, bytes_accessed=0, transcendentals=0),
        name="opening",
    )(blocks, weights, bias, biases, head, rest, latent)


def closing_kernel(
    mod_ref, bias_ref, mod_w_ref, conds_ref,
    bias_out, cond_out, weight_out, sum_out,
    mod_out, mod_unit, bias_unit, bias_in, part_ref, cond_in,
    x_send, x_recv, m_send, m_recv, b_send, b_recv, c_send, c_recv,
):
    side = lax.axis_index("tensor")
    rank = lax.axis_index("dp")
    greet(side)
    rows = mod_ref.shape[1]
    mod_swap = to_partner(mod_ref.at[1], mod_unit.at[1], side, x_send, x_recv, 0)
    mod_swap.start()
    bias_swap = to_partner(bias_ref.at[1], bias_unit.at[1], side, x_send, x_recv, 1)
    bias_swap.start()
    mod_swap.wait()
    bias_swap.wait()
    mod_out[rank] = mod_ref[0] + mod_unit[1]
    bias_in[rank] = bias_ref[0] + bias_unit[1]
    mods = DirectSpread(mod_out, m_send, m_recv)
    biases = DirectSpread(bias_in, b_send, b_recv)
    mods.begin()
    biases.begin()
    mods.relay()
    biases.relay()
    mods.finish()
    groups, rows, half = mod_out.shape
    low = mod_out[...].reshape(groups * rows, half).astype(bf16)
    lanes = mod_w_ref.shape[1]
    front = lax.broadcasted_iota(jnp.int32, (groups * rows, lanes), 0) % rows < rows // 2
    part_ref[...] = jnp.where(
        front,
        lax.dot_general(low, mod_w_ref[0], NT, preferred_element_type=f32),
        lax.dot_general(low, mod_w_ref[1], NT, preferred_element_type=f32),
    ).reshape(groups, rows, lanes)
    conds = Exchange(part_ref, cond_in, c_send, c_recv)
    conds.begin()
    values = conds_ref[...].reshape(groups * rows, conds_ref.shape[2]).astype(bf16)
    ahead = lax.broadcasted_iota(jnp.int32, values.shape, 0) % rows < rows // 2
    depth, cols = weight_out.shape[1:]
    whole = jnp.sum(mod_out[...], axis=0)
    for k in range(2):
        picked = jnp.where(ahead == (k == 0), values, jnp.zeros_like(values))
        grad = lax.dot_general(picked, low, TN, preferred_element_type=f32)[:depth]
        total = jnp.sum(whole[k * (rows // 2) : (k + 1) * (rows // 2)], axis=0, keepdims=True)
        for j in range(3):
            weight_out[3 * k + j] = grad[:, j * cols : (j + 1) * cols]
            sum_out[3 * k + j] = total[:, j * cols : (j + 1) * cols]
    biases.finish()
    bias_out[...] = jnp.sum(bias_in[...], axis=0)
    conds.finish()
    cond_out[0] = cond_in[...]
    cond_swap = to_partner(cond_out.at[0], cond_out.at[1], side, x_send, x_recv, 2)
    cond_swap.start()
    cond_swap.wait()
    conds.drain()


def closing(mod_pair, bias_pair, mod_weight, conds):
    groups = lax.axis_size("dp")
    rows, half = mod_pair.shape[1:]
    depth = mod_weight.shape[0]
    weights = jnp.pad(mod_weight.reshape(depth, 2, half), ((0, 128 - depth), (0, 0), (0, 0))).transpose(1, 0, 2)
    dma = pltpu.SemaphoreType.DMA
    vmem = pl.BlockSpec(memory_space=pltpu.VMEM)
    lines = bias_pair.shape[1]
    return pl.pallas_call(
        closing_kernel,
        in_specs=[vmem] * 4,
        out_specs=[vmem] * 4,
        out_shape=[
            jax.ShapeDtypeStruct((lines, 128), f32),
            jax.ShapeDtypeStruct((2, groups, rows, 128), f32),
            jax.ShapeDtypeStruct((6, depth, half // 3), f32),
            jax.ShapeDtypeStruct((6, 1, half // 3), f32),
        ],
        scratch_shapes=[
            pltpu.VMEM((groups, rows, half), f32),
            pltpu.VMEM((2, rows, half), f32),
            pltpu.VMEM((2, lines, 128), f32),
            pltpu.VMEM((groups, lines, 128), f32),
            pltpu.VMEM((groups, rows, 128), f32),
            pltpu.VMEM((groups, rows, 128), f32),
            dma((3,)), dma((3,)),
            dma((groups,)), dma((groups,)),
            dma((groups,)), dma((groups,)),
            dma((groups,)), dma((groups,)),
        ],
        compiler_params=pltpu.CompilerParams(collective_id=1, has_side_effects=True, vmem_limit_bytes=32 << 20),
        cost_estimate=pl.CostEstimate(flops=0, bytes_accessed=0, transcendentals=0),
        name="closing",
    )(mod_pair, bias_pair, weights, conds)


class Collect:
    def __init__(self, grads, totals, from_core, from_row, from_z, terms, row_out, z_out, *sems):
        self.grads, self.totals = grads, totals
        self.from_core, self.from_row, self.from_z = from_core, from_row, from_z
        self.terms, self.row_out, self.z_out = terms, row_out, z_out
        (self.core_send, self.core_recv, self.row_send, self.row_recv, self.z_send, self.z_recv, self.local) = sems
        self.rank = lax.axis_index("dp")
        self.z, self.y, self.core = place(self.rank)
        self.depth = lax.axis_size("dp") // (ROWS * CORES)
        self.pieces, _, _, self.width = from_core.shape
        self.outer = (self.z == 0) | (self.z == self.depth - 1)

    def lanes(self, n):
        return pl.ds(pl.multiple_of(n * self.width, 128), self.width)

    def block(self, n, rank):
        return self.grads.at[rank, :, self.lanes(n)]

    def level(self, k):
        falling = self.depth - 1 - k
        falling = falling - jnp.where(falling <= self.z, 1, 0)
        rising = k + jnp.where(k >= self.z, 1, 0)
        there = jnp.where(self.z < self.depth // 2, falling, rising)
        return jnp.where(k == self.depth - 1, self.z, there)

    def core_copy(self, n, level, y):
        k = level * ROWS + y
        return pltpu.make_async_remote_copy(
            src_ref=self.block(n, rank_of(level, y, 1 - self.core)),
            dst_ref=self.from_core.at[n, k],
            send_sem=self.core_send.at[n, k],
            recv_sem=self.core_recv.at[n, k],
            device_id={"dp": rank_of(self.z, self.y, 1 - self.core)},
            device_id_type=MESH,
        )

    def row_copy(self, n, k):
        level = self.level(k)
        return pltpu.make_async_remote_copy(
            src_ref=self.row_out.at[k],
            dst_ref=self.from_row.at[n, level],
            send_sem=self.row_send.at[n, k],
            recv_sem=self.row_recv.at[n, level],
            device_id={"dp": rank_of(self.z, 1 - self.y, self.core)},
            device_id_type=MESH,
        )

    def z_copy(self, n, k):
        level = self.level(k)
        above = jnp.where(level > self.z, 1, 0)
        return pltpu.make_async_remote_copy(
            src_ref=self.z_out.at[k],
            dst_ref=self.from_z.at[n, 1 - above, level],
            send_sem=self.z_send.at[n, k],
            recv_sem=self.z_recv.at[n, 1 - above, level],
            device_id={"dp": rank_of(self.z + 2 * above - 1, self.y, self.core)},
            device_id_type=MESH,
        )

    def z_arrival(self, n, way, level):
        return pltpu.make_async_remote_copy(
            src_ref=self.z_out.at[0],
            dst_ref=self.from_z.at[n, way, level],
            send_sem=self.z_send.at[n, 0],
            recv_sem=self.z_recv.at[n, way, level],
            device_id={"dp": rank_of(self.z, 1 - self.y, self.core)},
            device_id_type=MESH,
        )

    def each_core_copy(self, act):
        def some(i, carry):
            n, level = i // self.depth, self.level(i % self.depth)
            act(self.core_copy(n, level, 1 - self.y))
            act(self.core_copy(n, level, self.y))
            return carry

        lax.fori_loop(0, self.pieces * self.depth, some, 0)

    def begin(self):
        self.each_core_copy(lambda copy: copy.start())

    def fetches(self, kind, n, k):
        level = self.level(k)
        y = 1 - self.y if kind == "row" else self.y
        slot = k if kind == "row" else self.depth + k

        def get(j, ref):
            return pltpu.make_async_copy(ref, self.terms.at[slot, j], self.local.at[slot, j])

        found = [
            (get(0, self.block(n, rank_of(level, y, self.core))), None),
            (get(1, self.from_core.at[n, level * ROWS + y]), None),
        ]
        if kind == "z":
            below = (level >= self.z) & (self.z > 0)
            above = (level <= self.z) & (self.z < self.depth - 1)
            found.append((get(2, self.from_row.at[n, level]), None))
            found.append((get(3, self.from_z.at[n, 0, level]), below))
            found.append((get(4, self.from_z.at[n, 1, level]), above))
        return found

    def load(self, kind, n, k):
        level = self.level(k)
        y = 1 - self.y if kind == "row" else self.y
        self.core_copy(n, level, y).wait_recv()
        if kind == "z":
            self.row_copy(n, k).wait_recv()
        for j, (fetch, when) in enumerate(self.fetches(kind, n, k)):
            if when is None:
                fetch.start()
            else:

                def arrived(j=j, fetch=fetch):
                    self.z_arrival(n, j - 3, level).wait_recv()
                    fetch.start()

                pl.when(when)(arrived)

    def finish(self, kind, n, k, last=False):
        total = None
        slot = k if kind == "row" else self.depth + k
        for j, (fetch, when) in enumerate(self.fetches(kind, n, k)):
            if when is None:
                fetch.wait()
            else:
                pl.when(when)(fetch.wait)
            term = self.terms[slot, j].astype(f32)
            if when is not None:
                term = jnp.where(when, term, 0.0)
            total = term if total is None else total + term
        if last:
            self.totals[:, self.lanes(n)] = total
            return
        copy = self.row_copy if kind == "row" else self.z_copy
        out = self.row_out if kind == "row" else self.z_out
        pl.when(n > 0)(lambda: copy(n - 1, k).wait_send())
        out[k] = total.astype(bf16)
        copy(n, k).start()

    def units(self, r):
        found = []
        final = self.depth - 1
        valid = lambda n: (n >= 0) & (n < self.pieces)
        for k in range(self.depth):
            found.append((valid(r), "row", r, k, False))
        for k in range(final):
            age = jnp.where(self.outer, 2, 3 if k < final - 1 else 4)
            found.append((valid(r - age), "z", r - age, k, False))
        found.append((valid(r - 5), "z", r - 5, final, True))
        return found

    def rounds(self):
        return self.pieces + 5

    def load_round(self, r):
        for when, kind, n, k, _ in self.units(r):
            pl.when(when)(lambda kind=kind, n=n, k=k: self.load(kind, n, k))

    def finish_round(self, r):
        for when, kind, n, k, last in self.units(r):
            pl.when(when)(lambda kind=kind, n=n, k=k, last=last: self.finish(kind, n, k, last))

    def end(self):
        n = self.pieces - 1
        for k in range(self.depth):
            self.row_copy(n, k).wait_send()
        for k in range(self.depth - 1):
            self.z_copy(n, k).wait_send()
        self.each_core_copy(lambda copy: copy.wait_send())


def collect_shapes(pieces, width, groups, depth):
    levels = groups // (ROWS * CORES)
    dma = pltpu.SemaphoreType.DMA
    arrivals = [
        jax.ShapeDtypeStruct((pieces, levels * ROWS, depth, width), bf16),
        jax.ShapeDtypeStruct((pieces, levels, depth, width), bf16),
        jax.ShapeDtypeStruct((pieces, 2, levels, depth, width), bf16),
    ]
    scratch = [
        pltpu.VMEM((2 * levels, 5, depth, width), bf16),
        pltpu.VMEM((levels, depth, width), bf16),
        pltpu.VMEM((levels - 1, depth, width), bf16),
        dma((pieces, levels * ROWS)), dma((pieces, levels * ROWS)),
        dma((pieces, levels)), dma((pieces, levels)),
        dma((pieces, levels)), dma((pieces, 2, levels)),
        dma((2 * levels, 5)),
    ]
    return arrivals, scratch


TILE = 256


def latents_backward_kernel(
    dqkv_ref, w_ref, lat_ref, first_ref, scale_ref, grads_ref,
    out_ref, sums_ref, totals_ref, from_core, from_row, from_z,
    tiles, x_send, x_recv, kept, *collect,
):
    side = lax.axis_index("tensor")
    r = pl.program_id(0)
    engine = Collect(grads_ref, totals_ref, from_core, from_row, from_z, *collect)
    both, half_seq, _ = out_ref.shape
    count = both // 2
    per_half = half_seq // TILE
    sent = count * per_half

    def place_of(i):
        rows = pl.ds(pl.multiple_of(i % per_half * TILE, TILE), TILE)
        return out_ref.at[side * count + i // per_half, rows]

    def row_copy(i):
        return to_partner(tiles.at[i], place_of(i), side, x_send, x_recv, i)

    def keep_copy(i):
        return pltpu.make_async_copy(tiles.at[sent + i], place_of(i), kept.at[i])

    @pl.when(r == 0)
    def _():
        greet(side)
        engine.begin()
        sums_ref[...] = jnp.zeros_like(sums_ref)

    engine.load_round(r)

    @pl.when(r < 2 * sent)
    def _():
        grad = lax.dot_general(dqkv_ref[...], w_ref[...], NT, preferred_element_type=f32)
        norm, inverse = normed(lat_ref[...].astype(f32))
        latent = r % sent // per_half
        sums_ref[latent] += jnp.concatenate(
            [jnp.sum(grad, axis=0, keepdims=True), jnp.sum(grad * norm, axis=0, keepdims=True)], axis=0
        )
        back = normed_back(grad * (1.0 + scale_ref[0]), norm, inverse)
        tiles[r] = (first_ref[...] + back).astype(bf16)
        pl.when(r < sent)(lambda: row_copy(r).start())
        pl.when(r >= sent)(lambda: keep_copy(r - sent).start())

    engine.finish_round(r)

    @pl.when(r == pl.num_programs(0) - 1)
    def _():
        engine.end()
        for i in range(sent):
            row_copy(i).wait()
            keep_copy(i).wait()


def latents_backward(dqkv, w, lat, first_grad, scale, grads):
    count, seq, wide = dqkv.shape
    width = lat.shape[2]
    groups = lax.axis_size("dp")
    depth = grads.shape[0] // groups
    per_half = seq // 2 // TILE
    sent = count * per_half
    pieces, piece = 6, wide // 6
    arrivals, scratch = collect_shapes(pieces, piece, groups, depth)

    def tile(r):
        r = jnp.minimum(r, 2 * sent - 1)
        i = r % sent
        return i // per_half * 2 * per_half + i % per_half + jnp.where(r < sent, per_half, 0)

    rows = lambda cols: pl.BlockSpec((TILE, cols), lambda r: (tile(r), 0))
    anywhere = pl.BlockSpec(memory_space=pl.ANY)
    flat = lambda a: a.reshape(count * seq, a.shape[2])
    dma = pltpu.SemaphoreType.DMA
    return pl.pallas_call(
        latents_backward_kernel,
        grid=(max(pieces + 5, 2 * sent),),
        in_specs=[
            rows(wide),
            pl.BlockSpec((width, wide), lambda r: (0, 0), pipeline_mode=pl.Buffered(1)),
            rows(width),
            rows(width),
            pl.BlockSpec((1, 1, width), lambda r: (tile(r) // (2 * per_half), 0, 0)),
            anywhere,
        ],
        out_specs=[
            anywhere,
            pl.BlockSpec((count, 2, width), lambda r: (0, 0, 0)),
            pl.BlockSpec((depth, wide), lambda r: (0, 0)),
        ]
        + [anywhere] * 3,
        out_shape=[
            jax.ShapeDtypeStruct((2 * count, seq // 2, width), bf16),
            jax.ShapeDtypeStruct((count, 2, width), f32),
            jax.ShapeDtypeStruct((depth, wide), f32),
        ]
        + arrivals,
        scratch_shapes=[pltpu.VMEM((2 * sent, TILE, width), bf16), dma((sent,)), dma((sent,)), dma((sent,))]
        + scratch,
        compiler_params=pltpu.CompilerParams(
            collective_id=2, has_side_effects=True, vmem_limit_bytes=56 << 20
        ),
        cost_estimate=pl.CostEstimate(flops=0, bytes_accessed=0, transcendentals=0),
        name="latents_backward",
    )(flat(dqkv), w, flat(lat), flat(first_grad), scale, grads.reshape(groups, depth, wide))[:3]


def normed(values):
    centred = values - jnp.mean(values, axis=-1, keepdims=True)
    variance = jnp.mean(centred * centred, axis=-1, keepdims=True)
    inverse = lax.rsqrt(variance + EPSILON)
    return centred * inverse, inverse


def normed_back(grad, norm, inverse):
    return inverse * (
        grad
        - jnp.mean(grad, axis=-1, keepdims=True)
        - norm * jnp.mean(grad * norm, axis=-1, keepdims=True)
    )


def mm(spec, a, b):
    return jnp.einsum(spec, a, b, preferred_element_type=f32)


def body_by_latents(
    latent,
    condition,
    cotangent,
    mod_weight,
    mod_bias,
    head_weight,
    head_bias,
    mix_weight,
    branch_bias,
    up_weight,
    up_bias,
    down_weight,
):
    side = lax.axis_index("tensor")
    rank = lax.axis_index("dp")
    groups = lax.axis_size("dp")
    count, half_seq, width = latent.shape
    own = count // 2
    cols = width // 2
    depth = head_weight.shape[0]
    hidden = 2 * up_weight.shape[1]

    def swap(a):
        return lax.ppermute(a, "tensor", [(0, 1), (1, 0)])

    def in_order(mine, other, axis):
        return jnp.where(
            side == 0,
            jnp.concatenate([mine, other], axis=axis),
            jnp.concatenate([other, mine], axis=axis),
        )

    def own_latents(a, axis=0):
        return lax.dynamic_slice_in_dim(a, side * own, own, axis)

    def other_latents(a, axis=0):
        return lax.dynamic_slice_in_dim(a, (1 - side) * own, own, axis)

    def placed(a, arrived):
        mine = lax.broadcasted_iota(jnp.int32, (2, 1, 1, 1), 0) == side
        whole = jnp.where(mine, a[None, :, :half_seq], arrived[None])
        return whole.reshape(count, half_seq, width)

    cond_f = condition.astype(f32)
    cond_low = jax.nn.silu(cond_f).astype(bf16)
    heads = cols // HEAD_DIM
    room = -(-cols // 128) * 128

    def roomy(a):
        return jnp.pad(a, [(0, 0)] * (a.ndim - 1) + [(0, room - cols)])

    head_shard = roomy(head_weight).reshape(depth, 3 * room)
    shards = jnp.concatenate([up_weight, roomy(mix_weight.T)], axis=1)
    branch = branch_bias.astype(f32)
    flat = [a.astype(f32).reshape(-1) for a in (head_bias, branch, up_bias)]
    head_all, shards_in, latent_in, mod_parts, cond_blocks, biases_in = opening(
        cond_low,
        mod_weight,
        mod_bias,
        jnp.concatenate(flat).reshape(-1, 128),
        head_shard,
        shards,
        latent,
    )
    biases_in = biases_in.reshape(-1)
    head_bias_in = biases_in[: 2 * cols].reshape(2, cols)
    branch_in = biases_in[2 * cols : 4 * cols].reshape(2, cols)
    head_all = head_all.reshape(width, 6 * room)
    mod_parts = mod_parts.reshape(2, 2, count, 3, cols)
    mod_parts = own_latents(mod_parts, 2).transpose(0, 2, 1, 3, 4).reshape(2, own, 6, cols)
    modulation = in_order(mod_parts[0], mod_parts[1], 2)
    branch_all = in_order(branch, branch_in, 1)
    row = lambda k: modulation[:, k][:, None, :]
    shift_a, scale_a, gate_a, shift_m, scale_m, gate_m = [row(k) for k in range(6)]

    cuts = (0, hidden // 2, hidden // 2 + room)
    pieces = [a[:, lo:hi] for lo, hi in zip(cuts, cuts[1:]) for a in (shards, shards_in)]
    up_mix = lax.all_gather(jnp.concatenate(pieces, axis=1), "dp", axis=0, tiled=True)
    up_all = up_mix[:, :hidden]
    mix_t = up_mix[:, hidden:]
    up_bias_f = jnp.concatenate([flat[2], biases_in[4 * cols :]])

    lat = jnp.concatenate([own_latents(latent), latent_in], axis=1)
    lat_f = lat.astype(f32)
    norm1, inv1 = normed(lat_f)
    attn_in = (norm1 * (1.0 + scale_a) + shift_a).astype(bf16)
    empty = jnp.zeros((room,), f32)
    qkv_bias = jnp.concatenate(
        [c for b in (roomy(head_bias.astype(f32)), roomy(head_bias_in)) for c in (b[0], empty, b[1])]
    )
    qkv = (mm("bsd,dc->bsc", attn_in, head_all) + qkv_bias).astype(bf16)
    later, down_mine, qkv = lax.optimization_barrier((other_latents(cotangent), down_weight.T, qkv))
    down_t = lax.all_gather(
        jnp.concatenate([down_mine, swap(down_mine)], axis=1), "dp", axis=0, tiled=True
    )
    upstream_low = jnp.concatenate([own_latents(cotangent), swap(later)], axis=1)
    mixed, logsum = attn_fwd(qkv, heads)
    attn_out = mm("bsc,dc->bsd", mixed, mix_t) + branch_all[0]
    first = lat_f + gate_a * attn_out
    norm2, inv2 = normed(first)
    mlp_in = (norm2 * (1.0 + scale_m) + shift_m).astype(bf16)
    act, slope = up_forward(mlp_in, up_mix, up_bias_f)
    upstream = upstream_low.astype(f32)
    mlp_grad = (gate_m * upstream).astype(bf16)
    down_grad = mm("bsd,bsf->df", mlp_grad, act).astype(bf16)
    down_grad, mlp_grad, act = lax.optimization_barrier((down_grad, mlp_grad, act))
    down_sum = lax.psum_scatter(down_grad, "dp", scatter_dimension=0, tiled=True)
    mlp_out = mm("bsf,df->bsd", act, down_t) + branch_all[1]
    block = (first + gate_m * mlp_out).astype(bf16)
    block_in = swap(block[:, half_seq:])

    gate_m_grad = jnp.sum(upstream * mlp_out, axis=1)
    tail_bias_grad = jnp.sum(gate_m[:, 0] * jnp.sum(upstream, axis=1), axis=0)
    pre_grad, up_bias_term = down_backward(mlp_grad, down_t, slope)
    up_grad = mm("bsd,bsf->df", mlp_in, pre_grad).astype(bf16)
    up_grad, pre_grad = lax.optimization_barrier((up_grad, pre_grad))
    mlp_in_grad = mm("bsf,df->bsd", pre_grad, up_all)
    shift_m_grad = jnp.sum(mlp_in_grad, axis=1)
    scale_m_grad = jnp.sum(mlp_in_grad * norm2, axis=1)
    first_grad = upstream + normed_back(mlp_in_grad * (1.0 + scale_m), norm2, inv2)
    gate_a_grad = jnp.sum(first_grad * attn_out, axis=1)
    attn_bias_grad = jnp.sum(gate_a[:, 0] * jnp.sum(first_grad, axis=1), axis=0)
    attn_grad = (gate_a * first_grad).astype(bf16)
    mixed_grad = mm("bsd,dc->bsc", attn_grad, mix_t).astype(bf16)
    mix_grad = mm("bsd,bsc->dc", attn_grad, mixed).astype(bf16)
    mix_grad, down_sum = lax.optimization_barrier((mix_grad, down_sum))
    up_grad = jnp.concatenate([up_grad, mix_grad], axis=1)
    up_grad, mixed_grad = lax.optimization_barrier((up_grad, mixed_grad))
    up_sum = lax.psum_scatter(up_grad, "dp", scatter_dimension=0, tiled=True)
    qkv_grad, qkv_bias_term = attn_bwd(qkv, mixed_grad, mixed, logsum, heads)
    qkv_bias_term = jnp.sum(qkv_bias_term, axis=0)
    head_grad = mm("bsd,bsc->dc", attn_in, qkv_grad).astype(bf16)
    head_grad, up_sum, block_in = lax.optimization_barrier((head_grad, up_sum, block_in))
    block_out = placed(block, block_in)
    latent_grad, sums, head_sum = latents_backward(
        qkv_grad, head_all, lat, first_grad, scale_a, head_grad
    )
    shift_a_grad, scale_a_grad = sums[:, 0], sums[:, 1]

    mod_low = jnp.stack(
        [shift_a_grad, scale_a_grad, gate_a_grad, shift_m_grad, scale_m_grad, gate_m_grad], axis=1
    ).astype(bf16)
    branch_term = jnp.stack([attn_bias_grad, tail_bias_grad])
    head_term = qkv_bias_term.reshape(2, 3, room)[:, 0::2, :cols]
    ups = up_bias_term.reshape(2, hidden // 2)

    def mod_share(owner):
        mine = lax.dynamic_slice_in_dim(mod_low.astype(f32), owner * cols, cols, 2)
        mine = mine.reshape(own, 2, 3 * cols).transpose(1, 0, 2)
        empty = jnp.zeros((2, count, 3 * cols), f32)
        return lax.dynamic_update_slice_in_dim(empty, mine, side * own, 1).reshape(2 * count, 3 * cols)

    def bias_share(owner, k):
        branch_cols = lax.dynamic_slice_in_dim(branch_term, owner * cols, cols, 1)
        flat = jnp.concatenate([head_term[k].reshape(-1), branch_cols.reshape(-1), ups[k]])
        return flat.reshape(-1, 128)

    mod_pair = jnp.stack([mod_share(side), mod_share(1 - side)])
    biases, cond_parts, mod_weight_grad, mod_bias_grad = closing(
        mod_pair,
        jnp.stack([bias_share(side, 0), bias_share(1 - side, 1)]),
        mod_weight,
        cond_blocks,
    )
    biases = biases.reshape(-1)
    mod_weight_grad = mod_weight_grad.transpose(1, 0, 2)
    mod_bias_grad = mod_bias_grad[:, 0]
    cond_act = jnp.sum(cond_parts[..., :depth].reshape(2, groups, 2, count, depth), axis=(0, 2))
    cond_act = cond_act.transpose(1, 0, 2).reshape(count, groups * depth)
    gate = jax.nn.sigmoid(cond_f)
    condition_grad = cond_act * (gate * (1.0 + cond_f * (1.0 - gate)))

    def joined(summed, axis):
        mine, other = jnp.split(summed, 2, axis=axis)
        return mine.astype(f32) + swap(other.astype(bf16)).astype(f32)

    head_weight_grad = joined(head_sum, 1).reshape(depth, 3, room)[..., :cols]
    mix_weight_grad = joined(up_sum[:, hidden:], 1)[:, :cols].T
    up_weight_grad = joined(up_sum[:, :hidden], 1)
    down_weight_grad = joined(down_sum, 1).T
    return (
        block_out,
        latent_grad,
        condition_grad,
        mod_weight_grad,
        mod_bias_grad,
        head_weight_grad,
        biases[: 2 * cols].reshape(2, cols),
        mix_weight_grad,
        biases[2 * cols : 4 * cols].reshape(2, cols),
        up_weight_grad,
        biases[4 * cols :],
        down_weight_grad,
    )


def solution(mesh):
    placed = (
        P("dp", "tensor", None),
        P("dp", None),
        P("dp", "tensor", None),
        P("dp", None, "tensor"),
        P(None, "tensor"),
        P("dp", None, "tensor"),
        P(None, "tensor"),
        P("tensor", "dp"),
        P(None, "tensor"),
        P("dp", "tensor"),
        P("tensor"),
        P("tensor", "dp"),
    )
    whole_latents = dict(mesh.shape) == {"dp": 16, "tensor": 2}
    return jax.shard_map(
        body_by_latents if whole_latents else body_by_heads,
        mesh=mesh,
        in_specs=placed,
        out_specs=(
            P("dp", "tensor", None),
            P("dp", "tensor", None),
            P("dp", None),
            P("dp", None, "tensor"),
            P(None, "tensor"),
            P("dp", None, "tensor"),
            P(None, "tensor"),
            P("tensor", "dp"),
            P(None, "tensor"),
            P("dp", "tensor"),
            P("tensor"),
            P("tensor", "dp"),
        ),
        check_vma=False,
    )
```
